128 devices in a mesh: tm: 32 (over x, z, y_hi), head: 4 (over y_lo, core).
Axes of the slice: x: 4, y: 4 (y_hi: 2, y_lo: 2; y = y_hi * 2 + y_lo), z: 4, core: 2. Of those that a mesh axis runs over, the one named last changes fastest.
Arguments:
- queries: bfloat16 [12288, 1536], P(('tm', 'head')), may hold values from -60 to 60
- keys: bfloat16 [12288, 1536], P(('tm', 'head')), may hold values from -60 to 60
- values: bfloat16 [12288, 1536], P(('tm', 'head')), may hold values from -6 to 6
- out_grad: bfloat16 [12288, 1536], P(('tm', 'head')), may hold values from -6 to 6
- window: int32 [32, 27], replicated, may hold values from 0 to 1, as said below
Outputs:
- attended: bfloat16 [12288, 1536], P(('tm', 'head'))
- query_grad: bfloat16 [12288, 1536], P(('tm', 'head'))
- key_grad: bfloat16 [12288, 1536], P(('tm', 'head'))
- value_grad: bfloat16 [12288, 1536], P(('tm', 'head'))
The draws below stay inside these ranges and needn't reach their ends.
Inputs may be any that keep to these rules, and one draw needn't show every extreme that they name: `window`: entry 9 (a + 1) + 3 (b + 1) + (c + 1) of row s refers to the key tile at offset a in time, b in height and c in width from tile s; it is 1 for a = b = c = 0, and 0 where that tile lies outside the grid of 4 x 2 x 4 tiles.
All inputs are finite; a program needn't handle non-finite values.
Results may differ from the reference program's by a relative error of at most 0.009.
Values may be sent and summed in bfloat16 or wider, within the bound.
A program may use at most 192 MiB of HBM per device.

```python
import math
import jax
import jax.numpy as jnp
import numpy as np
from jax import lax

TILE = 384
GH = 2
GW = 4
HEADS = 12
HD = 128
NTILES = 32
TOKENS = 12288


def spread_scales(key, base):
    column_key, row_key = jax.random.split(key)
    low = math.log(0.3)
    high = math.log(3.0)
    column_scale = jnp.exp(jax.random.uniform(column_key, (1, base.shape[1]), jnp.float32, low, high))
    row_scale = jnp.exp(jax.random.uniform(row_key, (base.shape[0], 1), jnp.float32, low, high))
    return base * column_scale * row_scale


def draw_queries(key, part):
    key = jax.random.fold_in(key, 1)
    base_key, scale_key = jax.random.split(key)
    base = jnp.clip(jax.random.normal(base_key, (TOKENS, HEADS * HD), jnp.float32), -6.0, 6.0)
    return spread_scales(scale_key, base).astype(jnp.bfloat16)


def draw_keys(key, part):
    key = jax.random.fold_in(key, 2)
    base_key, scale_key = jax.random.split(key)
    base = jnp.clip(jax.random.normal(base_key, (TOKENS, HEADS * HD), jnp.float32), -6.0, 6.0)
    return spread_scales(scale_key, base).astype(jnp.bfloat16)


def draw_window(key, part):
    key = jax.random.fold_in(key, 3)
    level_key, pick_key = jax.random.split(key)
    grid_rows = NTILES // (GH * GW)
    tile_ids = jnp.arange(NTILES, dtype=jnp.int32)
    row_pos = tile_ids // (GH * GW)
    high_pos = tile_ids // GW % GH
    wide_pos = tile_ids % GW
    offsets = jnp.arange(27, dtype=jnp.int32)
    step_time = offsets // 9 - 1
    step_high = offsets // 3 % 3 - 1
    step_wide = offsets % 3 - 1
    target_row = row_pos[:, None] + step_time[None, :]
    target_high = high_pos[:, None] + step_high[None, :]
    target_wide = wide_pos[:, None] + step_wide[None, :]
    inside = (target_row >= 0) & (target_row < grid_rows) & (target_high >= 0) & (target_high < GH) & (target_wide >= 0) & (target_wide < GW)
    levels = jax.random.randint(level_key, (NTILES,), 0, 9, jnp.int32)
    picks = jax.random.randint(pick_key, (NTILES, 27), 0, 8, jnp.int32) < levels[:, None]
    centre = offsets[None, :] == 13
    return jnp.where(inside & (picks | centre), 1, 0).astype(jnp.int32)


def steps_of(own_key, shape, shards, low, largest):
    factor_of, own = 1.0, jax.random.fold_in(own_key, 6)
    for axis_at, blocks in shards:
        heights = jnp.exp(jax.random.uniform(jax.random.fold_in(own, axis_at), (blocks,), jnp.float32, low / len(shards), largest / len(shards)))
        factor_of = factor_of * jnp.repeat(heights, shape[axis_at] // blocks).reshape([-1 if axis == axis_at else 1 for axis in range(len(shape))])
    return factor_of


def normal_values(stream_key, shape, deviation, reach, pieces=(), kind=jnp.bfloat16):
    entries = jax.random.normal(stream_key, shape, jnp.float32) * deviation
    if len(pieces) > 0:
        entries = steps_of(stream_key, shape, pieces, -0.22, 0.18) * entries
    return jnp.clip(entries, min=-reach, max=reach).astype(kind)


def setup_inputs(seed: int = 0) -> dict:
    streams_of = jax.random.split(jax.random.key(seed), 6)
    queries = draw_queries(jax.random.fold_in(streams_of[5], 71), 0)
    keys = draw_keys(jax.random.fold_in(streams_of[5], 71), 0)
    values = normal_values(streams_of[2], (TOKENS, HEADS * HD), 1.0, 6.0, ((0, 128),))
    out_grad = normal_values(streams_of[3], (TOKENS, HEADS * HD), 1.0, 6.0, ((0, 128),))
    window = draw_window(jax.random.fold_in(streams_of[5], 71), 0)
    return {"queries": queries, "keys": keys, "values": values, "out_grad": out_grad, "window": window}


EPSILON = 1e-06
OFFSETS = [(step_time, step_high, step_wide) for step_time in (-1, 0, 1) for step_high in (-1, 0, 1) for step_wide in (-1, 0, 1)]

def widened(value):
    return lax.optimization_barrier(value).astype(jnp.float32)

def normed(raw_rows):
    widen_rows = raw_rows.astype(jnp.float32)
    inverse = lax.rsqrt(lax.optimization_barrier(jnp.mean(widen_rows * widen_rows, axis=-1, keepdims=True)) + EPSILON)
    return (widen_rows * inverse).astype(jnp.bfloat16)

def norm_back(raw_rows, grad_in):
    widen_rows = raw_rows.astype(jnp.float32)
    inverse = lax.rsqrt(lax.optimization_barrier(jnp.mean(widen_rows * widen_rows, axis=-1, keepdims=True)) + EPSILON)
    unit_rows = widen_rows * inverse
    return inverse * (grad_in - unit_rows * lax.optimization_barrier(jnp.mean(grad_in * unit_rows, axis=-1, keepdims=True)))

def reference(queries, keys, values, out_grad, window):
    grid_rows = NTILES // (GH * GW)
    tile_shape = (NTILES, TILE, HEADS, HD)
    grid_shape = (grid_rows, GH, GW, TILE, HEADS, HD)
    query_raw = queries.reshape(tile_shape)
    key_raw = keys.reshape(tile_shape)
    value_tiles = values.reshape(tile_shape)
    grad_tiles = out_grad.reshape(tile_shape)
    query_unit = normed(query_raw)
    key_unit = normed(key_raw)
    pad_spec = [(1, 1), (1, 1), (1, 1), (0, 0), (0, 0), (0, 0)]
    key_padded = jnp.pad(key_unit.reshape(grid_shape), pad_spec)
    value_padded = jnp.pad(value_tiles.reshape(grid_shape), pad_spec)
    step_table = np.array(OFFSETS, np.int32)
    centre = jnp.asarray((np.arange(27) == 13)[:, None, None, None])
    score_scale = HD ** (-0.5)
    block_shape = (3, 3, 3, TILE, HEADS, HD)

    def one_tile(carry, tile_index):
        key_acc, value_acc = carry
        row_pos = tile_index // (GH * GW)
        high_pos = tile_index // GW % GH
        wide_pos = tile_index % GW
        zero = jnp.zeros((), jnp.int32)
        starts = (row_pos, high_pos, wide_pos, zero, zero, zero)
        key_near = lax.dynamic_slice(key_padded, starts, block_shape).reshape(27, TILE, HEADS, HD)
        value_near = lax.dynamic_slice(value_padded, starts, block_shape).reshape(27, TILE, HEADS, HD)
        inside = ((row_pos + step_table[:, 0] >= 0) & (row_pos + step_table[:, 0] < grid_rows) & (high_pos + step_table[:, 1] >= 0) & (high_pos + step_table[:, 1] < GH) & (wide_pos + step_table[:, 2] >= 0) & (wide_pos + step_table[:, 2] < GW)).astype(jnp.float32)
        window_row = lax.dynamic_index_in_dim(window, tile_index, 0, keepdims=False).astype(jnp.float32)
        mask = window_row * inside
        query_tile = lax.dynamic_index_in_dim(query_unit, tile_index, 0, keepdims=False)
        grad_in = lax.dynamic_index_in_dim(grad_tiles, tile_index, 0, keepdims=False)
        scores = jnp.einsum('qhd,ckhd->qhck', widened(query_tile), widened(key_near)) * score_scale
        weights = jnp.exp(scores) * mask[None, None, :, None]
        totals = lax.optimization_barrier(jnp.sum(weights, axis=(2, 3)))
        mixed = jnp.einsum('qhck,ckhd->qhd', widened(weights.astype(jnp.bfloat16)), widened(value_near))
        output = (mixed / totals[..., None]).astype(jnp.bfloat16)
        row_dot = lax.optimization_barrier(jnp.sum(widened(grad_in) * widened(output), axis=-1))
        attn_probs = weights / totals[..., None, None]
        prob_low = attn_probs.astype(jnp.bfloat16)
        prob_grad = jnp.einsum('qhd,ckhd->qhck', widened(grad_in), widened(value_near))
        score_grad = (attn_probs * (prob_grad - row_dot[..., None, None]) * score_scale).astype(jnp.bfloat16)
        dquery = jnp.einsum('qhck,ckhd->qhd', widened(score_grad), widened(key_near))
        key_piece = jnp.einsum('qhck,qhd->ckhd', widened(score_grad), widened(query_tile))
        value_piece = jnp.einsum('qhck,qhd->ckhd', widened(prob_low), widened(grad_in))
        key_piece = jnp.where(centre, key_piece, widened(key_piece.astype(jnp.bfloat16)))
        value_piece = jnp.where(centre, value_piece, widened(value_piece.astype(jnp.bfloat16)))
        key_block = lax.dynamic_slice(key_acc, starts, block_shape) + key_piece.reshape(block_shape)
        value_block = lax.dynamic_slice(value_acc, starts, block_shape) + value_piece.reshape(block_shape)
        key_acc = lax.dynamic_update_slice(key_acc, key_block, starts)
        value_acc = lax.dynamic_update_slice(value_acc, value_block, starts)
        return ((key_acc, value_acc), (output, dquery))
    padded_shape = (grid_rows + 2, GH + 2, GW + 2, TILE, HEADS, HD)
    start_carry = (jnp.zeros(padded_shape, jnp.float32), jnp.zeros(padded_shape, jnp.float32))
    (key_acc, value_acc), (outputs, dquery) = lax.scan(one_tile, start_carry, jnp.arange(NTILES, dtype=jnp.int32))
    key_total = key_acc[1:-1, 1:-1, 1:-1].reshape(tile_shape)
    value_total = value_acc[1:-1, 1:-1, 1:-1].reshape(tile_shape)
    flat_shape = (TOKENS, HEADS * HD)
    attended = outputs.reshape(flat_shape)
    query_grad = norm_back(query_raw, dquery).astype(jnp.bfloat16).reshape(flat_shape)
    key_grad = norm_back(key_raw, key_total).astype(jnp.bfloat16).reshape(flat_shape)
    value_grad = value_total.astype(jnp.bfloat16).reshape(flat_shape)
    return (attended, query_grad, key_grad, value_grad)
```

```python
import jax
import jax.numpy as jnp
from jax import lax
from jax.experimental import pallas as pl
from jax.experimental.pallas import tpu as pltpu
from jax.sharding import PartitionSpec as P

TILE = 384
HEADS = 12
HD = 128
QUARTER = 96
SLOTS = 18
EPSILON = 1e-06
SCALE = HD**-0.5
LOG2E = 1.4426950408889634
MESH = pl.DeviceIdType.MESH
VMEM_LIMIT = 50 * 1024 * 1024


def place():
    tm = lax.axis_index("tm")
    part = lax.axis_index("head")
    return tm, part


def worker_of(n, T, W, core):
    y = n % 4
    cc = n // 4
    x = 2 * T + cc // 2
    z = 2 * (cc % 2) + W
    return x * 8 + z * 2 + y // 2, (y % 2) * 2 + core


def work_here(tm, part):
    x = tm // 8
    z = tm // 2 % 4
    y = tm % 2 * 2 + part // 2
    cc = x % 2 * 2 + z // 2
    return cc < 3, cc * 4 + y, x // 2, z % 2, part % 2


def copy_to(src, dst, send_sem, recv_sem, device, tm, part, start):
    same = (device[0] == tm) & (device[1] == part)

    @pl.when(same)
    def _():
        if start:
            pltpu.make_async_copy(src, dst, recv_sem).start()

    @pl.when(jnp.logical_not(same))
    def _():
        copy = pltpu.make_async_remote_copy(
            src_ref=src, dst_ref=dst, send_sem=send_sem, recv_sem=recv_sem, device_id=device, device_id_type=MESH
        )
        if start:
            copy.start()
        else:
            copy.wait_send()


def arrived(ref, sem):
    pltpu.make_async_copy(ref, ref, sem).wait()


def gather_kernel(q_ref, k_ref, v_ref, g_ref, kv_ref, qg_ref, kv_stage, qg_stage, kv_send, qg_send, kv_recv, qg_recv):
    tm, part = place()
    t = tm // 8
    h = tm // 4 % 2
    w = tm % 4

    @pl.loop(0, HEADS)
    def _(n):
        lanes = pl.ds(pl.multiple_of(n * HD, HD), HD)
        k = k_ref[:, lanes].astype(jnp.float32)
        inverse = lax.rsqrt(jnp.mean(k * k, axis=-1, keepdims=True) + EPSILON)
        kv_stage[n, :, 0:HD] = (k * inverse).astype(jnp.bfloat16)
        kv_stage[n, :, HD:] = v_ref[:, lanes]
        qg_stage[n, :, 0:HD] = q_ref[:, lanes]
        qg_stage[n, :, HD:] = g_ref[:, lanes]

    rows = pl.ds(pl.multiple_of(part * QUARTER, QUARTER), QUARTER)

    def each(start):
        @pl.loop(0, HEADS)
        def _(n):
            tile = t % 2 * 2 + w % 2
            copy_to(
                qg_stage.at[n],
                qg_ref.at[tile, rows],
                qg_send.at[n],
                qg_recv.at[tile, part],
                worker_of(n, t // 2, w // 2, h),
                tm,
                part,
                start,
            )
            for T in range(2):
                for W in range(2):

                    @pl.when((t >= T) & (t < T + 3) & (w >= W) & (w < W + 3))
                    def _():
                        slot = ((t - T) * 2 + h) * 3 + (w - W)
                        for core in range(2):
                            copy_to(
                                kv_stage.at[n],
                                kv_ref.at[slot, rows],
                                kv_send.at[n, T * 2 + W, core],
                                kv_recv.at[slot, part],
                                worker_of(n, T, W, core),
                                tm,
                                part,
                                start,
                            )

    each(True)
    active = work_here(tm, part)[0]

    @pl.when(active)
    def _():
        for quarter in range(4):
            span = pl.ds(quarter * QUARTER, QUARTER)

            @pl.loop(0, 4)
            def _(tile):
                arrived(qg_ref.at[tile, span], qg_recv.at[tile, quarter])

            @pl.loop(0, SLOTS)
            def _(slot):
                arrived(kv_ref.at[slot, span], kv_recv.at[slot, quarter])

    each(False)


def nt(a, b):
    return lax.dot_general(a, b, (((1,), (1,)), ((), ())), preferred_element_type=jnp.float32)


def tn(a, b):
    return lax.dot_general(a, b, (((0,), (0,)), ((), ())), preferred_element_type=jnp.float32)


def attend_kernel(place_ref, window_ref, qg_ref, kv_ref, og_ref, dkv_ref, acc, dq_acc, dkv_acc, weights, ones, q_unit, scaled):
    @pl.when(place_ref[0] == 1)
    def _():
        T, W, core = place_ref[1], place_ref[2], place_ref[3]
        ones[...] = jnp.ones_like(ones)
        dkv_acc[...] = jnp.zeros_like(dkv_acc)

        @pl.loop(0, 4)
        def _(tile):
            ti = tile // 2
            wi = tile % 2
            s = (2 * T + ti) * 8 + core * 4 + 2 * W + wi

            def live(slot):
                dt = slot // 6 - T - ti
                dh = slot // 3 % 2 - core
                dw = slot % 3 - W - wi
                near = (dt >= -1) & (dt <= 1) & (dw >= -1) & (dw <= 1)
                at = jnp.where(near, 9 * (dt + 1) + 3 * (dh + 1) + dw + 1, 0)
                return near & (window_ref[s, at] == 1)

            q = qg_ref[tile, :, 0:HD].astype(jnp.float32)
            inverse = lax.rsqrt(jnp.mean(q * q, axis=-1, keepdims=True) + EPSILON)
            q_unit[...] = (q * inverse).astype(jnp.bfloat16)
            acc[...] = jnp.zeros_like(acc)
            dq_acc[...] = jnp.zeros_like(dq_acc)

            @pl.loop(0, SLOTS)
            def _(slot):
                @pl.when(live(slot))
                def _():
                    scores = nt(q_unit[...], kv_ref[slot, :, 0:HD])
                    low = jnp.exp2(scores * (SCALE * LOG2E)).astype(jnp.bfloat16)
                    weights[slot] = low
                    packed = jnp.concatenate([kv_ref[slot, :, HD:], ones[...]], axis=1)
                    acc[...] += jnp.dot(low, packed, preferred_element_type=jnp.float32)

            over = 1.0 / acc[:, HD:]
            out = (acc[:, 0:HD] * over).astype(jnp.bfloat16)
            og_ref[tile, :, 0:HD] = out
            grad = qg_ref[tile, :, HD:].astype(jnp.float32)
            row_dot = jnp.sum(grad * out.astype(jnp.float32), axis=-1, keepdims=True)
            scaled[:, 0:HD] = (q_unit[...].astype(jnp.float32) * (over * SCALE)).astype(jnp.bfloat16)
            scaled[:, HD:] = (grad * over).astype(jnp.bfloat16)

            @pl.loop(0, SLOTS)
            def _(slot):
                @pl.when(live(slot))
                def _():
                    low = weights[slot]
                    prob_grad = nt(qg_ref[tile, :, HD:], kv_ref[slot, :, HD:])
                    score_grad = (low.astype(jnp.float32) * (prob_grad - row_dot)).astype(jnp.bfloat16)
                    dq_acc[...] += jnp.dot(score_grad, kv_ref[slot, :, 0:HD], preferred_element_type=jnp.float32)
                    dkv_acc[slot, :, 0:HD] += tn(score_grad, scaled[:, 0:HD])
                    dkv_acc[slot, :, HD:] += tn(low, scaled[:, HD:])

            grad_in = dq_acc[...] * (over * SCALE)
            unit = q * inverse
            dq = inverse * (grad_in - unit * jnp.mean(grad_in * unit, axis=-1, keepdims=True))
            og_ref[tile, :, HD:] = dq.astype(jnp.bfloat16)

        @pl.loop(0, SLOTS)
        def _(slot):
            dkv_ref[slot] = dkv_acc[slot].astype(jnp.bfloat16)


def scatter_kernel(og_ref, dkv_ref, k_ref, o_ref, dq_ref, dk_ref, dv_ref, og_in, dkv_in, og_send, dkv_send, og_recv, dkv_recv):
    tm, part = place()
    t = tm // 8
    w = tm % 4
    active, n, T, W, core = work_here(tm, part)
    source = (T * 2 + W) * 2 + core

    def each(start):
        for quarter in range(4):
            span = pl.ds(quarter * QUARTER, QUARTER)

            @pl.loop(0, 4)
            def _(tile):
                owner = (2 * T + tile // 2) * 8 + core * 4 + 2 * W + tile % 2
                copy_to(
                    og_ref.at[tile, span],
                    og_in.at[n],
                    og_send.at[tile, quarter],
                    og_recv.at[n],
                    (owner, quarter),
                    tm,
                    part,
                    start,
                )

            @pl.loop(0, SLOTS)
            def _(slot):
                owner = (T + slot // 6) * 8 + slot // 3 % 2 * 4 + W + slot % 3
                copy_to(
                    dkv_ref.at[slot, span],
                    dkv_in.at[source, n],
                    dkv_send.at[slot, quarter],
                    dkv_recv.at[source, n],
                    (owner, quarter),
                    tm,
                    part,
                    start,
                )

    @pl.when(active)
    def _():
        each(True)

    def needed(T, W):
        return (t >= T) & (t < T + 3) & (w >= W) & (w < W + 3)

    @pl.loop(0, HEADS)
    def _(n):
        lanes = pl.ds(pl.multiple_of(n * HD, HD), HD)
        arrived(og_in.at[n], og_recv.at[n])
        o_ref[:, lanes] = og_in[n, :, 0:HD]
        dq_ref[:, lanes] = og_in[n, :, HD:]
        total = jnp.zeros((QUARTER, 2 * HD), jnp.float32)
        for T in range(2):
            for W in range(2):

                def take(total, T=T, W=W):
                    for core in range(2):
                        at = (T * 2 + W) * 2 + core
                        arrived(dkv_in.at[at, n], dkv_recv.at[at, n])
                        total = total + dkv_in[at, n].astype(jnp.float32)
                    return total

                total = lax.cond(needed(T, W), take, lambda total: total, total)
        k = k_ref[:, lanes].astype(jnp.float32)
        inverse = lax.rsqrt(jnp.mean(k * k, axis=-1, keepdims=True) + EPSILON)
        unit = k * inverse
        grad_in = total[:, 0:HD]
        dk = inverse * (grad_in - unit * jnp.mean(grad_in * unit, axis=-1, keepdims=True))
        dk_ref[:, lanes] = dk.astype(jnp.bfloat16)
        dv_ref[:, lanes] = total[:, HD:].astype(jnp.bfloat16)

    @pl.when(active)
    def _():
        each(False)


def shards(queries, keys, values, out_grad, window):
    low = jnp.bfloat16
    vmem = pl.BlockSpec(memory_space=pltpu.VMEM)
    smem = pl.BlockSpec(memory_space=pltpu.SMEM)
    hbm = pl.BlockSpec(memory_space=pl.ANY)
    dma = pltpu.SemaphoreType.DMA
    kv, qg = pl.pallas_call(
        gather_kernel,
        out_shape=(jax.ShapeDtypeStruct((SLOTS, TILE, 2 * HD), low), jax.ShapeDtypeStruct((4, TILE, 2 * HD), low)),
        in_specs=[vmem] * 4,
        out_specs=(hbm, hbm),
        scratch_shapes=[
            pltpu.VMEM((HEADS, QUARTER, 2 * HD), low),
            pltpu.VMEM((HEADS, QUARTER, 2 * HD), low),
            dma((HEADS, 4, 2)),
            dma((HEADS,)),
            dma((SLOTS, 4)),
            dma((4, 4)),
        ],
        compiler_params=pltpu.CompilerParams(has_side_effects=True, vmem_limit_bytes=VMEM_LIMIT),
        name="gather",
    )(queries, keys, values, out_grad)

    tm, part = place()
    active, _, T, W, core = work_here(tm, part)
    placed = jnp.stack([active.astype(jnp.int32), T, W, core])
    og, dkv = pl.pallas_call(
        attend_kernel,
        out_shape=(jax.ShapeDtypeStruct((4, TILE, 2 * HD), low), jax.ShapeDtypeStruct((SLOTS, TILE, 2 * HD), low)),
        in_specs=[smem, smem, vmem, vmem],
        out_specs=(vmem, vmem),
        scratch_shapes=[
            pltpu.VMEM((TILE, 2 * HD), jnp.float32),
            pltpu.VMEM((TILE, HD), jnp.float32),
            pltpu.VMEM((SLOTS, TILE, 2 * HD), jnp.float32),
            pltpu.VMEM((SLOTS, TILE, TILE), low),
            pltpu.VMEM((TILE, HD), low),
            pltpu.VMEM((TILE, HD), low),
            pltpu.VMEM((TILE, 2 * HD), low),
        ],
        compiler_params=pltpu.CompilerParams(vmem_limit_bytes=VMEM_LIMIT),
        name="attend",
    )(placed, window, qg, kv)

    return pl.pallas_call(
        scatter_kernel,
        out_shape=tuple(jax.ShapeDtypeStruct((QUARTER, HEADS * HD), low) for _ in range(4)),
        in_specs=[hbm, hbm, vmem],
        out_specs=(vmem,) * 4,
        scratch_shapes=[
            pltpu.VMEM((HEADS, QUARTER, 2 * HD), low),
            pltpu.VMEM((8, HEADS, QUARTER, 2 * HD), low),
            dma((4, 4)),
            dma((SLOTS, 4)),
            dma((HEADS,)),
            dma((8, HEADS)),
        ],
        compiler_params=pltpu.CompilerParams(has_side_effects=True, vmem_limit_bytes=VMEM_LIMIT),
        name="scatter",
    )(og, dkv, keys)


def solution(mesh):
    rows = P(("tm", "head"), None)
    return jax.shard_map(
        shards, mesh=mesh, in_specs=(rows, rows, rows, rows, P()), out_specs=(rows, rows, rows, rows), check_vma=False
    )
```

```python
import jax
import jax.numpy as jnp
from jax import lax
from jax.experimental import pallas as pl
from jax.experimental.pallas import tpu as pltpu
from jax.sharding import PartitionSpec as P

TILE = 384
HEADS = 12
HD = 128
QUARTER = 96
SLOTS = 18
EPSILON = 1e-06
SCALE = HD**-0.5
LOG2E = 1.4426950408889634
MESH = pl.DeviceIdType.MESH
VMEM_LIMIT = 60 * 1024 * 1024
LOW = jnp.bfloat16

QUERY_AT = ((0, 1), (0, 0), (1, 0), (1, 1))
KINDS = ((0, 8, 0, 4), (8, 4, 0, 2), (12, 4, 1, 2), (16, 2, 1, 1))
CHIPS = (
    (0, 9, 11, 12, 22, 28, 30, 36, 38, 42, 49, 59),
    (3, 4, 13, 15, 17, 26, 35, 40, 41, 47, 48, 61),
    (6, 7, 19, 25, 27, 34, 44, 45, 51, 54, 57, 62),
    (2, 8, 16, 20, 21, 31, 33, 39, 53, 55, 58, 60),
)


def pick(table, index):
    found = jnp.int32(table[0])
    for at in range(1, len(table)):
        found = jnp.where(index == at, jnp.int32(table[at]), found)
    return found


def worker_of(n, block, core):
    chip = pick(CHIPS[block], n)
    x, y, z = chip // 16, chip // 4 % 4, chip % 4
    return x * 8 + z * 2 + y // 2, (y % 2) * 2 + core


def work_here(tm, part):
    x, y, z = tm // 8, tm % 2 * 2 + part // 2, tm // 2 % 4
    chip = x * 16 + y * 4 + z
    code = jnp.int32(-1)
    for block in range(4):
        for n in range(HEADS):
            code = jnp.where(chip == CHIPS[block][n], jnp.int32(block * HEADS + n), code)
    active = code >= 0
    code = jnp.where(active, code, 0)
    block = code // HEADS
    return active, code % HEADS, block // 2, block % 2, part % 2


def absolute(half, near):
    return 1 + half + near * (2 * half - 1)


def relative(half, index):
    return (index - 1 - half) * (2 * half - 1)


def slot_at(kind, i):
    if kind == 0:
        return i // 4, i % 2, i // 2 % 2
    if kind == 1:
        return -1, i % 2, i // 2
    if kind == 2:
        return i // 2, i % 2, -1
    return -1, i % 2, -1


def slot_number(near_t, h, near_w):
    return jnp.where(
        near_t >= 0,
        jnp.where(near_w >= 0, (near_t * 2 + near_w) * 2 + h, 12 + near_t * 2 + h),
        jnp.where(near_w >= 0, 8 + near_w * 2 + h, 16 + h),
    )


def query_number(near_t, near_w):
    return jnp.where(near_t == 0, 1 - near_w, 2 + near_w)


def copy_to(src, dst, send_sem, recv_sem, device, here, start):
    same = (device[0] == here[0]) & (device[1] == here[1])

    @pl.when(same)
    def _():
        if start:
            pltpu.make_async_copy(src, dst, recv_sem).start()

    @pl.when(jnp.logical_not(same))
    def _():
        copy = pltpu.make_async_remote_copy(
            src_ref=src, dst_ref=dst, send_sem=send_sem, recv_sem=recv_sem, device_id=device, device_id_type=MESH
        )
        if start:
            copy.start()
        else:
            copy.wait_send()


def arrived(ref, sem):
    pltpu.make_async_copy(ref, ref, sem).wait()


def nt(a, b):
    return lax.dot_general(a, b, (((1,), (1,)), ((), ())), preferred_element_type=jnp.float32)


def tn(a, b):
    return lax.dot_general(a, b, (((0,), (0,)), ((), ())), preferred_element_type=jnp.float32)


def quarter(j):
    return pl.ds(pl.multiple_of(j * QUARTER, QUARTER), QUARTER)


def lanes_of(n):
    return pl.ds(pl.multiple_of(n * HD, HD), HD)


def thrice(value):
    return jnp.concatenate([value] * 3, axis=1)


def fused_kernel(
    window_ref,
    q_ref,
    k_ref,
    v_ref,
    g_ref,
    o_ref,
    dq_ref,
    dk_ref,
    dv_ref,
    kv_stage,
    qg_stage,
    kv,
    qg,
    q_unit,
    weights0,
    weights1,
    weights2,
    weights3,
    acc,
    dq_acc,
    over,
    row_dot,
    scaled,
    o_stage,
    dq_stage,
    part_sum,
    sib_send,
    sib_recv,
    sum_stage,
    dkv_in,
    kv_send,
    qg_send,
    kv_recv,
    qg_recv,
    relay_send,
    sib_sent,
    sib_got,
    o_send,
    dq_send,
    sum_send,
    o_recv,
    dq_recv,
    dkv_recv,
):
    tm, part = lax.axis_index("tm"), lax.axis_index("head")
    here = (tm, part)
    t, h, w = tm // 8, tm // 4 % 2, tm % 4
    active, head, T, W, core = work_here(tm, part)
    block = T * 2 + W
    sibling = (tm, part + 1 - 2 * core)
    weights = (weights0, weights1, weights2, weights3)

    @pl.loop(0, HEADS)
    def _(n):
        lanes = lanes_of(n)
        k = k_ref[:, lanes].astype(jnp.float32)
        inverse = lax.rsqrt(jnp.mean(k * k, axis=-1, keepdims=True) + EPSILON)
        kv_stage[n, :, 0:HD] = (k * inverse).astype(LOW)
        kv_stage[n, :, HD:] = v_ref[:, lanes]
        qg_stage[n, :, 0:HD] = q_ref[:, lanes]
        qg_stage[n, :, HD:] = g_ref[:, lanes]

    def send_queries(start):
        for b in range(4):

            @pl.when((t // 2 == b // 2) & (w // 2 == b % 2))
            def _():
                at = query_number(relative(b // 2, t), relative(b % 2, w))

                @pl.loop(0, HEADS)
                def _(n):
                    copy_to(
                        qg_stage.at[n],
                        qg.at[at, quarter(part)],
                        qg_send.at[n],
                        qg_recv.at[at, part],
                        worker_of(n, b, h),
                        here,
                        start,
                    )

    def send_keys(own, start):
        for b in range(4):
            near_t, near_w = relative(b // 2, t), relative(b % 2, w)
            inside = (near_t >= 0) & (near_w >= 0)
            reached = (near_t <= 1) & (near_w <= 1) & (near_t >= -1) & (near_w >= -1)

            @pl.when(inside if own else reached & jnp.logical_not(inside))
            def _():
                slot = slot_number(near_t, h, near_w)

                @pl.loop(0, HEADS)
                def _(n):
                    copy_to(
                        kv_stage.at[n],
                        kv.at[slot, quarter(part)],
                        kv_send.at[n, b],
                        kv_recv.at[slot, part],
                        worker_of(n, b, core),
                        here,
                        start,
                    )

    send_queries(True)
    send_keys(True, True)
    send_keys(False, True)

    def relay(slot, start):
        for y in range(2):
            j = 2 * y + core
            if start:
                arrived(kv.at[slot, quarter(j)], kv_recv.at[slot, j])
            copy = pltpu.make_async_remote_copy(
                src_ref=kv.at[slot, quarter(j)],
                dst_ref=kv.at[slot, quarter(j)],
                send_sem=relay_send.at[slot, y],
                recv_sem=kv_recv.at[slot, j],
                device_id=sibling,
                device_id_type=MESH,
            )
            if start:
                copy.start()
            else:
                copy.wait_send()

    def relayed(slot):
        for y in range(2):
            j = 2 * y + 1 - core
            arrived(kv.at[slot, quarter(j)], kv_recv.at[slot, j])

    def score_step(kind, i):
        first, count, q0, qn = KINDS[kind]
        slot = first + i
        near_t, kh, near_w = slot_at(kind, i)

        @pl.when(slot + 1 < SLOTS)
        def _():
            relay(slot + 1, True)

        relayed(slot)
        scores = nt(q_unit[q0 * TILE : (q0 + qn) * TILE], kv[slot, :, 0:HD])
        lows = []
        for u in range(qn):
            qt, qw = QUERY_AT[q0 + u]
            dt = absolute(T, near_t) - absolute(T, qt)
            dw = absolute(W, near_w) - absolute(W, qw)
            tile = absolute(T, qt) * 8 + core * 4 + absolute(W, qw)
            live = window_ref[tile, 9 * (dt + 1) + 3 * (kh - core + 1) + dw + 1]
            bias = (live.astype(jnp.float32) - 1.0) * 1e30
            weight = jnp.exp2(scores[u * TILE : (u + 1) * TILE] * (SCALE * LOG2E) + bias)
            rows = slice((q0 + u) * TILE, (q0 + u + 1) * TILE)
            acc[rows, HD:] += weight[:, 0:HD] + weight[:, HD : 2 * HD] + weight[:, 2 * HD :]
            lows.append(weight.astype(LOW))
        low = jnp.concatenate(lows, axis=0) if qn > 1 else lows[0]
        weights[kind][i] = low
        acc[q0 * TILE : (q0 + qn) * TILE, 0:HD] += jnp.dot(low, kv[slot, :, HD:], preferred_element_type=jnp.float32)

    def send_sum(slot, coords, start):
        near_t, kh, near_w = coords
        owner = absolute(T, near_t) * 8 + kh * 4 + absolute(W, near_w)
        for y in range(2):
            copy_to(
                sum_stage.at[slot, y],
                dkv_in.at[block, head],
                sum_send.at[slot, y],
                dkv_recv.at[block, head],
                (owner, 2 * y + core),
                here,
                start,
            )

    def to_sibling(slot):
        return pltpu.make_async_remote_copy(
            src_ref=sib_send.at[slot],
            dst_ref=sib_recv.at[slot],
            send_sem=sib_sent.at[slot],
            recv_sem=sib_got.at[slot],
            device_id=sibling,
            device_id_type=MESH,
        )

    def finish_sum(slot, coords):
        to_sibling(slot).wait_recv()
        for y in range(2):
            mine = part_sum[slot % 2, quarter(2 * y + core)]
            sum_stage[slot, y] = (mine + sib_recv[slot, y].astype(jnp.float32)).astype(LOW)
        send_sum(slot, coords, True)

    def grad_step(kind, i):
        first, count, q0, qn = KINDS[kind]
        slot = first + i
        rows = slice(q0 * TILE, (q0 + qn) * TILE)
        low = weights[kind][i]
        prob_grad = nt(scaled[rows, 2 * HD :], kv[slot, :, HD:])
        score_grad = (low.astype(jnp.float32) * (prob_grad - thrice(row_dot[rows]))).astype(LOW)
        dq_acc[rows] += jnp.dot(score_grad, kv[slot, :, 0:HD], preferred_element_type=jnp.float32)
        part_sum[slot % 2, :, 0:HD] = tn(score_grad, scaled[rows, 0:HD])
        part_sum[slot % 2, :, HD:] = tn(low, scaled[rows, HD : 2 * HD])
        for y in range(2):
            sib_send[slot, y] = part_sum[slot % 2, quarter(2 * y + 1 - core)].astype(LOW)
        to_sibling(slot).start()

    def query_owner(u):
        qt, qw = QUERY_AT[u]
        return absolute(T, qt) * 8 + core * 4 + absolute(W, qw)

    def send_result(stage, dst, send_sem, recv_sem, start):
        for u in range(4):
            for j in range(4):
                copy_to(
                    stage.at[u, quarter(j)],
                    dst.at[:, lanes_of(head)],
                    send_sem.at[u, j],
                    recv_sem.at[head],
                    (query_owner(u), j),
                    here,
                    start,
                )

    @pl.when(active)
    def _():
        for u in range(4):
            for j in range(4):
                arrived(qg.at[u, quarter(j)], qg_recv.at[u, j])
            q = qg[u, :, 0:HD].astype(jnp.float32)
            inverse = lax.rsqrt(jnp.mean(q * q, axis=-1, keepdims=True) + EPSILON)
            rows = slice(u * TILE, (u + 1) * TILE)
            q_unit[rows] = (q * inverse).astype(LOW)
            scaled[rows, 2 * HD :] = qg[u, :, HD:]
        acc[...] = jnp.zeros_like(acc)
        dq_acc[...] = jnp.zeros_like(dq_acc)
        relay(0, True)
        for kind in range(4):

            @pl.loop(0, KINDS[kind][1])
            def _(i):
                score_step(kind, i)

        for u in range(4):
            rows = slice(u * TILE, (u + 1) * TILE)
            over[rows] = jnp.broadcast_to(1.0 / jnp.sum(acc[rows, HD:], axis=-1, keepdims=True), (TILE, HD))
            out = (acc[rows, 0:HD] * over[rows]).astype(LOW)
            o_stage[u] = out
            grad = qg[u, :, HD:].astype(jnp.float32)
            dot = jnp.sum(grad * out.astype(jnp.float32), axis=-1, keepdims=True)
            row_dot[rows] = jnp.broadcast_to(dot, (TILE, HD))
            scaled[rows, 0:HD] = (q_unit[rows].astype(jnp.float32) * (over[rows] * SCALE)).astype(LOW)
            scaled[rows, HD : 2 * HD] = (grad * over[rows]).astype(LOW)
        send_result(o_stage, o_ref, o_send, o_recv, True)

        for kind in (3, 2, 1, 0):

            @pl.loop(0, KINDS[kind][1])
            def _(i):
                grad_step(kind, i)

                @pl.when(i > 0)
                def _():
                    finish_sum(KINDS[kind][0] + i - 1, slot_at(kind, i - 1))

            last = KINDS[kind][1] - 1
            finish_sum(KINDS[kind][0] + last, slot_at(kind, last))

        for u in range(4):
            rows = slice(u * TILE, (u + 1) * TILE)
            q = qg[u, :, 0:HD].astype(jnp.float32)
            inverse = lax.rsqrt(jnp.mean(q * q, axis=-1, keepdims=True) + EPSILON)
            unit = q * inverse
            grad_in = dq_acc[rows] * (over[rows] * SCALE)
            dq = inverse * (grad_in - unit * jnp.mean(grad_in * unit, axis=-1, keepdims=True))
            dq_stage[u] = dq.astype(LOW)
        send_result(dq_stage, dq_ref, dq_send, dq_recv, True)

    def reached(b):
        near_t, near_w = relative(b // 2, t), relative(b % 2, w)
        return (near_t <= 1) & (near_w <= 1) & (near_t >= -1) & (near_w >= -1)

    @pl.loop(0, HEADS)
    def _(n):
        lanes = lanes_of(n)
        total = jnp.zeros((QUARTER, 2 * HD), jnp.float32)
        for b in range(4):

            def take(total, b=b):
                arrived(dkv_in.at[b, n], dkv_recv.at[b, n])
                return total + dkv_in[b, n].astype(jnp.float32)

            total = lax.cond(reached(b), take, lambda total: total, total)
        k = k_ref[:, lanes].astype(jnp.float32)
        inverse = lax.rsqrt(jnp.mean(k * k, axis=-1, keepdims=True) + EPSILON)
        unit = k * inverse
        grad_in = total[:, 0:HD]
        dk = inverse * (grad_in - unit * jnp.mean(grad_in * unit, axis=-1, keepdims=True))
        dk_ref[:, lanes] = dk.astype(LOW)
        dv_ref[:, lanes] = total[:, HD:].astype(LOW)

    @pl.loop(0, HEADS)
    def _(n):
        arrived(o_ref.at[:, lanes_of(n)], o_recv.at[n])
        arrived(dq_ref.at[:, lanes_of(n)], dq_recv.at[n])

    send_queries(False)
    send_keys(True, False)
    send_keys(False, False)

    @pl.when(active)
    def _():
        @pl.loop(0, SLOTS)
        def _(slot):
            relay(slot, False)
            to_sibling(slot).wait_send()

        for kind in range(4):

            @pl.loop(0, KINDS[kind][1])
            def _(i):
                send_sum(KINDS[kind][0] + i, slot_at(kind, i), False)

        send_result(o_stage, o_ref, o_send, o_recv, False)
        send_result(dq_stage, dq_ref, dq_send, dq_recv, False)


def shards(queries, keys, values, out_grad, window):
    vmem = pl.BlockSpec(memory_space=pltpu.VMEM)
    smem = pl.BlockSpec(memory_space=pltpu.SMEM)
    dma = pltpu.SemaphoreType.DMA
    f32 = jnp.float32
    return pl.pallas_call(
        fused_kernel,
        out_shape=tuple(jax.ShapeDtypeStruct((QUARTER, HEADS * HD), LOW) for _ in range(4)),
        in_specs=[smem] + [vmem] * 4,
        out_specs=(vmem,) * 4,
        scratch_shapes=[
            pltpu.VMEM((HEADS, QUARTER, 2 * HD), LOW),
            pltpu.VMEM((HEADS, QUARTER, 2 * HD), LOW),
            pltpu.VMEM((SLOTS, TILE, 2 * HD), LOW),
            pltpu.VMEM((4, TILE, 2 * HD), LOW),
            pltpu.VMEM((4 * TILE, HD), LOW),
            pltpu.VMEM((8, 4 * TILE, TILE), LOW),
            pltpu.VMEM((4, 2 * TILE, TILE), LOW),
            pltpu.VMEM((4, 2 * TILE, TILE), LOW),
            pltpu.VMEM((2, TILE, TILE), LOW),
            pltpu.VMEM((4 * TILE, 2 * HD), f32),
            pltpu.VMEM((4 * TILE, HD), f32),
            pltpu.VMEM((4 * TILE, HD), f32),
            pltpu.VMEM((4 * TILE, HD), f32),
            pltpu.VMEM((4 * TILE, 3 * HD), LOW),
            pltpu.VMEM((4, TILE, HD), LOW),
            pltpu.VMEM((4, TILE, HD), LOW),
            pltpu.VMEM((2, TILE, 2 * HD), f32),
            pltpu.VMEM((SLOTS, 2, QUARTER, 2 * HD), LOW),
            pltpu.VMEM((SLOTS, 2, QUARTER, 2 * HD), LOW),
            pltpu.VMEM((SLOTS, 2, QUARTER, 2 * HD), LOW),
            pltpu.VMEM((4, HEADS, QUARTER, 2 * HD), LOW),
            dma((HEADS, 4)),
            dma((HEADS,)),
            dma((SLOTS, 4)),
            dma((4, 4)),
            dma((SLOTS, 2)),
            dma((SLOTS,)),
            dma((SLOTS,)),
            dma((4, 4)),
            dma((4, 4)),
            dma((SLOTS, 2)),
            dma((HEADS,)),
            dma((HEADS,)),
            dma((4, HEADS)),
        ],
        compiler_params=pltpu.CompilerParams(has_side_effects=True, vmem_limit_bytes=VMEM_LIMIT),
        name="attend",
    )(window, queries, keys, values, out_grad)


def solution(mesh):
    rows = P(("tm", "head"), None)
    return jax.shard_map(
        shards, mesh=mesh, in_specs=(rows, rows, rows, rows, P()), out_specs=(rows, rows, rows, rows), check_vma=False
    )
```

```python
import jax
import jax.numpy as jnp
from jax import lax
from jax.experimental import pallas as pl
from jax.experimental.pallas import tpu as pltpu
from jax.sharding import PartitionSpec as P

TILE = 384
HEADS = 12
HD = 128
QUARTER = 96
SLOTS = 18
EPSILON = 1e-06
SCALE = HD**-0.5
LOG2E = 1.4426950408889634
MESH = pl.DeviceIdType.MESH
VMEM_LIMIT = 60 * 1024 * 1024
LOW = jnp.bfloat16

QUERY_AT = ((0, 1), (0, 0), (1, 0), (1, 1))
KINDS = ((0, 8, 0, 4), (8, 4, 0, 2), (12, 4, 1, 2), (16, 2, 1, 1))
CHIPS = (
    (16, 6, 24, 14, 18, 4, 26, 12, 0, 22, 8, 30),
    (17, 7, 25, 15, 19, 5, 23, 13, 1, 27, 9, 31),
    (32, 54, 40, 62, 34, 52, 42, 60, 48, 38, 56, 46),
    (33, 55, 41, 63, 35, 53, 39, 61, 49, 43, 57, 47),
)


def pick(table, index):
    found = jnp.int32(table[0])
    for at in range(1, len(table)):
        found = jnp.where(index == at, jnp.int32(table[at]), found)
    return found


def worker_of(n, block, core):
    chip = pick(sum(CHIPS, ()), block * HEADS + n)
    x, y, z = chip // 16, chip // 4 % 4, chip % 4
    return x * 8 + z * 2 + y // 2, (y % 2) * 2 + core


def work_here(tm, part):
    x, y, z = tm // 8, tm % 2 * 2 + part // 2, tm // 2 % 4
    chip = x * 16 + y * 4 + z
    code = jnp.int32(-1)
    for at, worker in enumerate(sum(CHIPS, ())):
        code = jnp.where(chip == worker, jnp.int32(at), code)
    active = code >= 0
    code = jnp.where(active, code, 0)
    return active, code % HEADS, code // HEADS, part % 2


def absolute(half, near):
    return 1 + half + near * (2 * half - 1)


def relative(half, index):
    return (index - 1 - half) * (2 * half - 1)


def slot_at(kind, i):
    if kind == 0:
        return i // 4, i % 2, i // 2 % 2
    if kind == 1:
        return -1, i % 2, i // 2
    if kind == 2:
        return i // 2, i % 2, -1
    return -1, i % 2, -1


def slot_number(near_t, h, near_w):
    return jnp.where(
        near_t >= 0,
        jnp.where(near_w >= 0, (near_t * 2 + near_w) * 2 + h, 12 + near_t * 2 + h),
        jnp.where(near_w >= 0, 8 + near_w * 2 + h, 16 + h),
    )


def query_number(near_t, near_w):
    return jnp.where(near_t == 0, 1 - near_w, 2 + near_w)


def copy_to(src, dst, send_sem, recv_sem, device, here, start):
    same = (device[0] == here[0]) & (device[1] == here[1])

    @pl.when(same)
    def _():
        if start:
            pltpu.make_async_copy(src, dst, recv_sem).start()

    @pl.when(jnp.logical_not(same))
    def _():
        copy = pltpu.make_async_remote_copy(
            src_ref=src, dst_ref=dst, send_sem=send_sem, recv_sem=recv_sem, device_id=device, device_id_type=MESH
        )
        if start:
            copy.start()
        else:
            copy.wait_send()


def arrived(ref, sem):
    pltpu.make_async_copy(ref, ref, sem).wait()


def nt(a, b):
    return lax.dot_general(a, b, (((1,), (1,)), ((), ())), preferred_element_type=jnp.float32)


def tn(a, b):
    return lax.dot_general(a, b, (((0,), (0,)), ((), ())), preferred_element_type=jnp.float32)


def quarter(j):
    return pl.ds(pl.multiple_of(j * QUARTER, QUARTER), QUARTER)


def lanes_of(n):
    return pl.ds(pl.multiple_of(n * HD, HD), HD)


def thrice(value):
    return jnp.concatenate([value] * 3, axis=1)


def attend_kernel(
    window_ref,
    q_hbm,
    k_hbm,
    v_hbm,
    g_hbm,
    o_ref,
    dq_ref,
    dkv_ref,
    q_in,
    k_in,
    v_in,
    g_in,
    kv_stage,
    qg_stage,
    kv,
    qg,
    q_unit,
    weights0,
    weights1,
    weights2,
    weights3,
    acc,
    dq_acc,
    over,
    row_dot,
    scaled,
    o_stage,
    dq_stage,
    part_sum,
    sib_send,
    sib_recv,
    sum_stage,
    near_recv,
    in_sem,
    kv_send,
    qg_send,
    kv_recv,
    qg_recv,
    relay_send,
    time_send,
    wide_send,
    sib_sent,
    sib_got,
    near_got,
    o_send,
    dq_send,
    sum_send,
    o_recv,
    dq_recv,
    dkv_recv,
):
    tm, part = lax.axis_index("tm"), lax.axis_index("head")
    here = (tm, part)
    t, h, w = tm // 8, tm // 4 % 2, tm % 4
    home = t // 2 * 2 + w // 2
    active, head, block, core = work_here(tm, part)
    T, W = block // 2, block % 2
    sibling = (tm, part + 1 - 2 * core)
    time_near = worker_of(head, (1 - T) * 2 + W, core)
    wide_near = worker_of(head, T * 2 + 1 - W, core)
    weights = (weights0, weights1, weights2, weights3)

    def copy_in(i):
        return pltpu.make_async_copy((k_hbm, v_hbm, q_hbm, g_hbm)[i], (k_in, v_in, q_in, g_in)[i], in_sem.at[i])

    for i in range(4):
        copy_in(i).start()

    def tile_of(near_t, kh, near_w):
        return absolute(T, near_t) * 8 + kh * 4 + absolute(W, near_w)

    barrier = pltpu.get_barrier_semaphore()

    def greet(device, count):
        other = jnp.logical_not((device[0] == tm) & (device[1] == part))

        @pl.when(other)
        def _():
            pl.semaphore_signal(barrier, inc=1, device_id=device, device_id_type=MESH)

        return count + other.astype(jnp.int32)

    def greet_workers(n, count):
        count = greet(worker_of(n, home, core), count)
        return lax.cond(h != core, lambda c: greet(worker_of(n, home, h), c), lambda c: c, count)

    greeted = lax.fori_loop(0, HEADS, greet_workers, jnp.int32(0))

    def greet_owners(i, count):
        owner = tile_of(*slot_at(0, i))
        for y in range(2):
            count = greet((owner, 2 * y + core), count)

        def others(count):
            for y in range(2):
                count = greet((owner, 2 * y + 1 - core), count)
            return count

        return lax.cond(i % 2 == core, others, lambda count: count, count)

    def greet_all(count):
        count = lax.fori_loop(0, 8, greet_owners, count)
        for device in (sibling, time_near, wide_near):
            count = greet(device, count)
        return count

    greeted = lax.cond(active, greet_all, lambda count: count, greeted)

    copy_in(0).wait()
    copy_in(1).wait()

    @pl.loop(0, HEADS)
    def _(n):
        lanes = lanes_of(n)
        k = k_in[:, lanes].astype(jnp.float32)
        inverse = lax.rsqrt(jnp.mean(k * k, axis=-1, keepdims=True) + EPSILON)
        kv_stage[n, :, 0:HD] = (k * inverse).astype(LOW)
        kv_stage[n, :, HD:] = v_in[:, lanes]

    copy_in(2).wait()
    copy_in(3).wait()

    @pl.loop(0, HEADS)
    def _(n):
        lanes = lanes_of(n)
        qg_stage[n, :, 0:HD] = q_in[:, lanes]
        qg_stage[n, :, HD:] = g_in[:, lanes]

    pl.semaphore_wait(barrier, greeted)
    near_t, near_w = relative(t // 2, t), relative(w // 2, w)

    def send_keys(start):
        slot = slot_number(near_t, h, near_w)

        @pl.loop(0, HEADS)
        def _(n):
            copy_to(
                kv_stage.at[n],
                kv.at[slot, quarter(part)],
                kv_send.at[n],
                kv_recv.at[slot, part],
                worker_of(n, home, core),
                here,
                start,
            )

    def send_queries(start):
        at = query_number(near_t, near_w)

        @pl.loop(0, HEADS)
        def _(n):
            copy_to(
                qg_stage.at[n],
                qg.at[at, quarter(part)],
                qg_send.at[n],
                qg_recv.at[at, part],
                worker_of(n, home, h),
                here,
                start,
            )

    send_keys(True)
    send_queries(True)

    def pass_on(kind, i, start):
        slot = KINDS[kind][0] + i
        near_t, kh, near_w = slot_at(kind, i)
        for y in range(2):
            j = 2 * y + core
            if start:
                arrived(kv.at[slot, quarter(j)], kv_recv.at[slot, j])

            def send(device, to, sem):
                copy = pltpu.make_async_remote_copy(
                    src_ref=kv.at[slot, quarter(j)],
                    dst_ref=kv.at[to, quarter(j)],
                    send_sem=sem.at[slot, y],
                    recv_sem=kv_recv.at[to, j],
                    device_id=device,
                    device_id_type=MESH,
                )
                if start:
                    copy.start()
                else:
                    copy.wait_send()

            if kind == 0:

                @pl.when(near_w == 0)
                def _():
                    send(wide_near, 12 + near_t * 2 + kh, wide_send)

            if kind in (0, 2):

                @pl.when(near_t == 0)
                def _():
                    send(time_near, 8 + near_w * 2 + kh if kind == 0 else 16 + kh, time_send)

            send(sibling, slot, relay_send)

    def relayed(slot):
        for y in range(2):
            j = 2 * y + 1 - core
            arrived(kv.at[slot, quarter(j)], kv_recv.at[slot, j])

    def score_step(kind, i):
        first, count, q0, qn = KINDS[kind]
        slot = first + i
        near_t, kh, near_w = slot_at(kind, i)
        relayed(slot)
        scores = nt(q_unit[q0 * TILE : (q0 + qn) * TILE], kv[slot, :, 0:HD])
        lows = []
        for u in range(qn):
            qt, qw = QUERY_AT[q0 + u]
            dt = absolute(T, near_t) - absolute(T, qt)
            dw = absolute(W, near_w) - absolute(W, qw)
            live = window_ref[tile_of(qt, core, qw), 9 * (dt + 1) + 3 * (kh - core + 1) + dw + 1]
            bias = (live.astype(jnp.float32) - 1.0) * 1e30
            weight = jnp.exp2(scores[u * TILE : (u + 1) * TILE] * (SCALE * LOG2E) + bias)
            rows = slice((q0 + u) * TILE, (q0 + u + 1) * TILE)
            acc[rows, HD:] += weight[:, 0:HD] + weight[:, HD : 2 * HD] + weight[:, 2 * HD :]
            lows.append(weight.astype(LOW))
        low = jnp.concatenate(lows, axis=0) if qn > 1 else lows[0]
        weights[kind][i] = low
        acc[q0 * TILE : (q0 + qn) * TILE, 0:HD] += jnp.dot(low, kv[slot, :, HD:], preferred_element_type=jnp.float32)

    def to_sibling(slot):
        return pltpu.make_async_remote_copy(
            src_ref=sib_send.at[slot],
            dst_ref=sib_recv.at[slot],
            send_sem=sib_sent.at[slot],
            recv_sem=sib_got.at[slot],
            device_id=sibling,
            device_id_type=MESH,
        )

    def send_sum(kind, i, start):
        slot = KINDS[kind][0] + i
        if kind == 0:
            owner = tile_of(*slot_at(kind, i))
            for y in range(2):
                copy_to(
                    sum_stage.at[slot, y],
                    dkv_ref.at[head],
                    sum_send.at[slot, y],
                    dkv_recv.at[head],
                    (owner, 2 * y + core),
                    here,
                    start,
                )
            return
        copy = pltpu.make_async_remote_copy(
            src_ref=sum_stage.at[slot],
            dst_ref=near_recv.at[slot - 8],
            send_sem=sum_send.at[slot, 0],
            recv_sem=near_got.at[slot - 8],
            device_id=wide_near if kind == 2 else time_near,
            device_id_type=MESH,
        )
        if start:
            copy.start()
        else:
            copy.wait_send()

    def finish_sum(kind, i):
        slot = KINDS[kind][0] + i
        near_t, kh, near_w = slot_at(kind, i)
        to_sibling(slot).wait_recv()
        for y in range(2):
            mine = quarter(2 * y + core)
            part_sum[slot % 2, mine] += sib_recv[slot, y].astype(jnp.float32)

        def add(at):
            arrived(near_recv.at[at], near_got.at[at])
            for y in range(2):
                part_sum[slot % 2, quarter(2 * y + core)] += near_recv[at, y].astype(jnp.float32)

        if kind == 0:
            pl.when(near_t == 0)(lambda: add(near_w * 2 + kh))
            pl.when(near_w == 0)(lambda: add(4 + near_t * 2 + kh))
        if kind == 2:
            pl.when(near_t == 0)(lambda: add(8 + kh))
        for y in range(2):
            sum_stage[slot, y] = part_sum[slot % 2, quarter(2 * y + core)].astype(LOW)
        send_sum(kind, i, True)

    def grad_step(kind, i):
        first, count, q0, qn = KINDS[kind]
        slot = first + i
        rows = slice(q0 * TILE, (q0 + qn) * TILE)
        low = weights[kind][i]
        prob_grad = nt(scaled[rows, 2 * HD :], kv[slot, :, HD:])
        score_grad = (low.astype(jnp.float32) * (prob_grad - thrice(row_dot[rows]))).astype(LOW)
        dq_acc[rows] += jnp.dot(score_grad, kv[slot, :, 0:HD], preferred_element_type=jnp.float32)
        part_sum[slot % 2, :, 0:HD] = tn(score_grad, scaled[rows, 0:HD])
        part_sum[slot % 2, :, HD:] = tn(low, scaled[rows, HD : 2 * HD])
        for y in range(2):
            sib_send[slot, y] = part_sum[slot % 2, quarter(2 * y + 1 - core)].astype(LOW)
        to_sibling(slot).start()

    def send_result(stage, dst, send_sem, recv_sem, start):
        for u in range(4):
            for j in range(4):
                copy_to(
                    stage.at[u, quarter(j)],
                    dst.at[:, lanes_of(head)],
                    send_sem.at[u, j],
                    recv_sem.at[head],
                    (tile_of(QUERY_AT[u][0], core, QUERY_AT[u][1]), j),
                    here,
                    start,
                )

    @pl.when(active)
    def _():
        acc[...] = jnp.zeros_like(acc)
        dq_acc[...] = jnp.zeros_like(dq_acc)

        @pl.loop(0, 8)
        def _(i):
            pass_on(0, i, True)

        for u in range(4):
            for j in range(4):
                arrived(qg.at[u, quarter(j)], qg_recv.at[u, j])
            q = qg[u, :, 0:HD].astype(jnp.float32)
            inverse = lax.rsqrt(jnp.mean(q * q, axis=-1, keepdims=True) + EPSILON)
            rows = slice(u * TILE, (u + 1) * TILE)
            q_unit[rows] = (q * inverse).astype(LOW)
            scaled[rows, 2 * HD :] = qg[u, :, HD:]

        @pl.loop(0, 8)
        def _(i):
            score_step(0, i)
            pl.when(i < 4)(lambda: pass_on(2, i, True))
            pl.when(i >= 4)(lambda: pass_on(1, i - 4, True))

        @pl.loop(0, 2)
        def _(i):
            pass_on(3, i, True)

        for kind in (2, 1, 3):

            @pl.loop(0, KINDS[kind][1])
            def _(i):
                score_step(kind, i)

        for u in range(4):
            rows = slice(u * TILE, (u + 1) * TILE)
            over[rows] = jnp.broadcast_to(1.0 / jnp.sum(acc[rows, HD:], axis=-1, keepdims=True), (TILE, HD))
            out = (acc[rows, 0:HD] * over[rows]).astype(LOW)
            o_stage[u] = out
            grad = qg[u, :, HD:].astype(jnp.float32)
            dot = jnp.sum(grad * out.astype(jnp.float32), axis=-1, keepdims=True)
            row_dot[rows] = jnp.broadcast_to(dot, (TILE, HD))
            scaled[rows, 0:HD] = (q_unit[rows].astype(jnp.float32) * (over[rows] * SCALE)).astype(LOW)
            scaled[rows, HD : 2 * HD] = (grad * over[rows]).astype(LOW)
        send_result(o_stage, o_ref, o_send, o_recv, True)

        for kind in (3, 1, 2, 0):
            count = KINDS[kind][1]

            @pl.loop(0, count)
            def _(step):
                i = count - 1 - step
                grad_step(kind, i)

                @pl.when(step > 0)
                def _():
                    finish_sum(kind, i + 1)

            finish_sum(kind, 0)

        for u in range(4):
            rows = slice(u * TILE, (u + 1) * TILE)
            q = qg[u, :, 0:HD].astype(jnp.float32)
            inverse = lax.rsqrt(jnp.mean(q * q, axis=-1, keepdims=True) + EPSILON)
            unit = q * inverse
            grad_in = dq_acc[rows] * (over[rows] * SCALE)
            dq = inverse * (grad_in - unit * jnp.mean(grad_in * unit, axis=-1, keepdims=True))
            dq_stage[u] = dq.astype(LOW)
        send_result(dq_stage, dq_ref, dq_send, dq_recv, True)

    @pl.loop(0, HEADS)
    def _(n):
        arrived(dkv_ref.at[n], dkv_recv.at[n])
        arrived(o_ref.at[:, lanes_of(n)], o_recv.at[n])
        arrived(dq_ref.at[:, lanes_of(n)], dq_recv.at[n])

    send_keys(False)
    send_queries(False)

    @pl.when(active)
    def _():
        for kind in range(4):

            @pl.loop(0, KINDS[kind][1])
            def _(i):
                pass_on(kind, i, False)
                to_sibling(KINDS[kind][0] + i).wait_send()
                send_sum(kind, i, False)

        send_result(o_stage, o_ref, o_send, o_recv, False)
        send_result(dq_stage, dq_ref, dq_send, dq_recv, False)


def finish_kernel(o_in, dq_in, dkv_in, k_in, o_ref, dq_ref, dk_ref, dv_ref, sems):
    copies = (
        pltpu.make_async_copy(o_in, o_ref, sems.at[0]),
        pltpu.make_async_copy(dq_in, dq_ref, sems.at[1]),
    )
    for copy in copies:
        copy.start()

    for n in range(HEADS):
        lanes = slice(n * HD, (n + 1) * HD)
        k = k_in[:, lanes].astype(jnp.float32)
        inverse = lax.rsqrt(jnp.mean(k * k, axis=-1, keepdims=True) + EPSILON)
        unit = k * inverse
        grad_in = dkv_in[n, :, 0:HD].astype(jnp.float32)
        dk = inverse * (grad_in - unit * jnp.mean(grad_in * unit, axis=-1, keepdims=True))
        dk_ref[:, lanes] = dk.astype(LOW)
        dv_ref[:, lanes] = dkv_in[n, :, HD:]
    for copy in copies:
        copy.wait()


def shards(queries, keys, values, out_grad, window):
    vmem = pl.BlockSpec(memory_space=pltpu.VMEM)
    smem = pl.BlockSpec(memory_space=pltpu.SMEM)
    hbm = pl.BlockSpec(memory_space=pl.ANY)
    dma = pltpu.SemaphoreType.DMA
    f32 = jnp.float32
    rows = jax.ShapeDtypeStruct((QUARTER, HEADS * HD), LOW)
    o, dq, dkv = pl.pallas_call(
        attend_kernel,
        out_shape=(rows, rows, jax.ShapeDtypeStruct((HEADS, QUARTER, 2 * HD), LOW)),
        in_specs=[smem] + [hbm] * 4,
        out_specs=(hbm,) * 3,
        scratch_shapes=[
            pltpu.VMEM((QUARTER, HEADS * HD), LOW),
            pltpu.VMEM((QUARTER, HEADS * HD), LOW),
            pltpu.VMEM((QUARTER, HEADS * HD), LOW),
            pltpu.VMEM((QUARTER, HEADS * HD), LOW),
            pltpu.VMEM((HEADS, QUARTER, 2 * HD), LOW),
            pltpu.VMEM((HEADS, QUARTER, 2 * HD), LOW),
            pltpu.VMEM((SLOTS, TILE, 2 * HD), LOW),
            pltpu.VMEM((4, TILE, 2 * HD), LOW),
            pltpu.VMEM((4 * TILE, HD), LOW),
            pltpu.VMEM((8, 4 * TILE, TILE), LOW),
            pltpu.VMEM((4, 2 * TILE, TILE), LOW),
            pltpu.VMEM((4, 2 * TILE, TILE), LOW),
            pltpu.VMEM((2, TILE, TILE), LOW),
            pltpu.VMEM((4 * TILE, 2 * HD), f32),
            pltpu.VMEM((4 * TILE, HD), f32),
            pltpu.VMEM((4 * TILE, HD), f32),
            pltpu.VMEM((4 * TILE, HD), f32),
            pltpu.VMEM((4 * TILE, 3 * HD), LOW),
            pltpu.VMEM((4, TILE, HD), LOW),
            pltpu.VMEM((4, TILE, HD), LOW),
            pltpu.VMEM((2, TILE, 2 * HD), f32),
            pltpu.VMEM((SLOTS, 2, QUARTER, 2 * HD), LOW),
            pltpu.VMEM((SLOTS, 2, QUARTER, 2 * HD), LOW),
            pltpu.VMEM((SLOTS, 2, QUARTER, 2 * HD), LOW),
            pltpu.VMEM((10, 2, QUARTER, 2 * HD), LOW),
            dma((4,)),
            dma((HEADS,)),
            dma((HEADS,)),
            dma((SLOTS, 4)),
            dma((4, 4)),
            dma((SLOTS, 2)),
            dma((SLOTS, 2)),
            dma((SLOTS, 2)),
            dma((SLOTS,)),
            dma((SLOTS,)),
            dma((10,)),
            dma((4, 4)),
            dma((4, 4)),
            dma((SLOTS, 2)),
            dma((HEADS,)),
            dma((HEADS,)),
            dma((HEADS,)),
        ],
        compiler_params=pltpu.CompilerParams(collective_id=0, has_side_effects=True, vmem_limit_bytes=VMEM_LIMIT),
        name="attend",
    )(window, queries, keys, values, out_grad)

    return pl.pallas_call(
        finish_kernel,
        out_shape=(rows,) * 4,
        in_specs=[hbm, hbm, vmem, vmem],
        out_specs=(hbm, hbm, vmem, vmem),
        scratch_shapes=[dma((2,))],
        compiler_params=pltpu.CompilerParams(vmem_limit_bytes=8 * 1024 * 1024),
        name="finish",
    )(o, dq, dkv, keys)


def solution(mesh):
    rows = P(("tm", "head"), None)
    return jax.shard_map(
        shards, mesh=mesh, in_specs=(rows, rows, rows, rows, P()), out_specs=(rows, rows, rows, rows), check_vma=False
    )
```

```python
import jax
import jax.numpy as jnp
from jax import lax
from jax.experimental import pallas as pl
from jax.experimental.pallas import tpu as pltpu
from jax.sharding import PartitionSpec as P

TILE = 384
HEADS = 12
HD = 128
QUARTER = 96
SLOTS = 18
LAG = 3
EPSILON = 1e-06
SCALE = HD**-0.5
LOG2E = 1.4426950408889634
MESH = pl.DeviceIdType.MESH
VMEM_LIMIT = 60 * 1024 * 1024
LOW = jnp.bfloat16

QUERY_AT = ((0, 1), (0, 0), (1, 0), (1, 1))
KINDS = ((0, 8, 0, 4), (8, 4, 0, 2), (12, 4, 1, 2), (16, 2, 1, 1))

def worker_of(n, T, W, core):
    y = n % 4
    spot = (n // 4 + y + 1) % 4
    x, z = absolute(T, spot // 2), 2 * (spot % 2) + W
    return x * 8 + z * 2 + y // 2, (y % 2) * 2 + core


def work_here(tm, part):
    x, y, z = tm // 8, tm % 2 * 2 + part // 2, tm // 2 % 4
    T, W = x // 2, z % 2
    row = (relative(T, x) * 2 + z // 2 + 7 - y) % 4
    return row < 3, jnp.where(row < 3, row * 4 + y, 0), T, W, part % 2


def absolute(half, near):
    return 1 + half + near * (2 * half - 1)


def relative(half, index):
    return (index - 1 - half) * (2 * half - 1)


def slot_at(kind, i):
    if kind == 0:
        return i // 4, i % 2, i // 2 % 2
    if kind == 1:
        return -1, i % 2, i // 2
    if kind == 2:
        return i // 2, i % 2, -1
    return -1, i % 2, -1


def slot_number(near_t, h, near_w):
    return jnp.where(
        near_t >= 0,
        jnp.where(near_w >= 0, (near_t * 2 + near_w) * 2 + h, 12 + near_t * 2 + h),
        jnp.where(near_w >= 0, 8 + near_w * 2 + h, 16 + h),
    )


def query_number(near_t, near_w):
    return jnp.where(near_t == 0, 1 - near_w, 2 + near_w)


def copy_to(src, dst, send_sem, recv_sem, device, here):
    same = (device[0] == here[0]) & (device[1] == here[1])

    @pl.when(same)
    def _():
        pltpu.make_async_copy(src, dst, recv_sem).start()

    @pl.when(jnp.logical_not(same))
    def _():
        pltpu.make_async_remote_copy(
            src_ref=src, dst_ref=dst, send_sem=send_sem, recv_sem=recv_sem, device_id=device, device_id_type=MESH
        ).start()


def arrived(ref, sem):
    pltpu.make_async_copy(ref, ref, sem).wait()


def nt(a, b):
    return lax.dot_general(a, b, (((1,), (1,)), ((), ())), preferred_element_type=jnp.float32)


def tn(a, b):
    return lax.dot_general(a, b, (((0,), (0,)), ((), ())), preferred_element_type=jnp.float32)


def quarter(j):
    return pl.ds(pl.multiple_of(j * QUARTER, QUARTER), QUARTER)


def lanes_of(n):
    return pl.ds(pl.multiple_of(n * HD, HD), HD)


def thrice(value):
    return jnp.concatenate([value] * 3, axis=1)


def attend_kernel(
    window_ref,
    q_hbm,
    k_hbm,
    v_hbm,
    g_hbm,
    o_ref,
    dq_ref,
    dkv_ref,
    q_in,
    k_in,
    v_in,
    g_in,
    kv_stage,
    qg_stage,
    kv,
    qg,
    q_unit,
    weights0,
    weights1,
    weights2,
    weights3,
    acc,
    dq_acc,
    over,
    row_dot,
    scaled,
    o_stage,
    dq_stage,
    part_sum,
    sib_send,
    sib_recv,
    sum_stage,
    near_recv,
    in_sem,
    kv_send,
    qg_send,
    kv_recv,
    qg_recv,
    relay_send,
    time_send,
    wide_send,
    sib_sent,
    sib_got,
    near_got,
    o_send,
    dq_send,
    sum_send,
    o_recv,
    dq_recv,
    dkv_recv,
):
    tm, part = lax.axis_index("tm"), lax.axis_index("head")
    here = (tm, part)
    t, h, w = tm // 8, tm // 4 % 2, tm % 4
    active, head, T, W, core = work_here(tm, part)
    home_t, home_w = t // 2, w // 2
    own_t, own_w = relative(home_t, t), relative(home_w, w)
    sibling = (tm, part + 1 - 2 * core)
    time_near = worker_of(head, 1 - T, W, core)
    wide_near = worker_of(head, T, 1 - W, core)
    weights = (weights0, weights1, weights2, weights3)

    def copy_in(i):
        return pltpu.make_async_copy((k_hbm, v_hbm, q_hbm, g_hbm)[i], (k_in, v_in, q_in, g_in)[i], in_sem.at[i])

    for i in range(4):
        copy_in(i).start()

    def tile_of(near_t, kh, near_w):
        return absolute(T, near_t) * 8 + kh * 4 + absolute(W, near_w)

    barrier = pltpu.get_barrier_semaphore()

    def greet(device, count):
        other = jnp.logical_not((device[0] == tm) & (device[1] == part))

        @pl.when(other)
        def _():
            pl.semaphore_signal(barrier, inc=1, device_id=device, device_id_type=MESH)

        return count + other.astype(jnp.int32)

    def greet_workers(n, count):
        count = greet(worker_of(n, home_t, home_w, core), count)
        return lax.cond(h != core, lambda c: greet(worker_of(n, home_t, home_w, h), c), lambda c: c, count)

    greeted = lax.fori_loop(0, HEADS, greet_workers, jnp.int32(0))

    def greet_owners(i, count):
        near_t, kh, near_w = slot_at(0, i)
        owner = tile_of(near_t, kh, near_w)
        for y in range(2):
            count = greet((owner, 2 * y + core), count)

        def others(count):
            for y in range(2):
                count = greet((owner, 2 * y + 1 - core), count)
            return count

        return lax.cond(kh == core, others, lambda count: count, count)

    def greet_all(count):
        count = lax.fori_loop(0, 8, greet_owners, count)
        for device in (sibling, time_near, wide_near):
            count = greet(device, count)
        return count

    greeted = lax.cond(active, greet_all, lambda count: count, greeted)

    copy_in(0).wait()
    copy_in(1).wait()

    @pl.loop(0, HEADS)
    def _(n):
        lanes = lanes_of(n)
        k = k_in[:, lanes].astype(jnp.float32)
        inverse = lax.rsqrt(jnp.mean(k * k, axis=-1, keepdims=True) + EPSILON)
        kv_stage[n, :, 0:HD] = (k * inverse).astype(LOW)
        kv_stage[n, :, HD:] = v_in[:, lanes]

    copy_in(2).wait()
    copy_in(3).wait()

    @pl.loop(0, HEADS)
    def _(n):
        lanes = lanes_of(n)
        qg_stage[n, :, 0:HD] = q_in[:, lanes]
        qg_stage[n, :, HD:] = g_in[:, lanes]

    pl.semaphore_wait(barrier, greeted)

    def send_keys():
        slot = (own_t * 2 + own_w) * 2 + h

        @pl.loop(0, HEADS)
        def _(n):
            copy_to(
                kv_stage.at[n],
                kv.at[slot, quarter(part)],
                kv_send,
                kv_recv.at[slot, part],
                worker_of(n, home_t, home_w, core),
                here,
            )

    def send_queries():
        at = query_number(own_t, own_w)

        @pl.loop(0, HEADS)
        def _(n):
            copy_to(
                qg_stage.at[n],
                qg.at[at, quarter(part)],
                qg_send,
                qg_recv,
                worker_of(n, home_t, home_w, h),
                here,
            )

    pl.when(own_t == 0)(send_keys)
    send_queries()
    pl.when(own_t != 0)(send_keys)

    def pass_on(kind, i):
        slot = KINDS[kind][0] + i
        near_t, kh, near_w = slot_at(kind, i)
        for y in range(2):
            j = 2 * y + core
            arrived(kv.at[slot, quarter(j)], kv_recv.at[slot, j])

            def send(device, to, sem):
                pltpu.make_async_remote_copy(
                    src_ref=kv.at[slot, quarter(j)],
                    dst_ref=kv.at[to, quarter(j)],
                    send_sem=sem,
                    recv_sem=kv_recv.at[to, j],
                    device_id=device,
                    device_id_type=MESH,
                ).start()

            if kind == 0:

                @pl.when(near_w == 0)
                def _():
                    send(wide_near, 12 + near_t * 2 + kh, wide_send)

            if kind in (0, 2):

                @pl.when(near_t == 0)
                def _():
                    send(time_near, 8 + near_w * 2 + kh if kind == 0 else 16 + kh, time_send)

            send(sibling, slot, relay_send)

    def relayed(slot):
        for y in range(2):
            j = 2 * y + 1 - core
            arrived(kv.at[slot, quarter(j)], kv_recv.at[slot, j])

    def score_step(kind, i):
        first, count, q0, qn = KINDS[kind]
        slot = first + i
        near_t, kh, near_w = slot_at(kind, i)
        relayed(slot)
        scores = nt(q_unit[q0 * TILE : (q0 + qn) * TILE], kv[slot, :, 0:HD])
        lows = []
        for u in range(qn):
            qt, qw = QUERY_AT[q0 + u]
            dt = absolute(T, near_t) - absolute(T, qt)
            dw = absolute(W, near_w) - absolute(W, qw)
            live = window_ref[tile_of(qt, core, qw), 9 * (dt + 1) + 3 * (kh - core + 1) + dw + 1]
            bias = (live.astype(jnp.float32) - 1.0) * 1e30
            weight = jnp.exp2(scores[u * TILE : (u + 1) * TILE] * (SCALE * LOG2E) + bias)
            rows = slice((q0 + u) * TILE, (q0 + u + 1) * TILE)
            acc[rows, HD:] += weight[:, 0:HD] + weight[:, HD : 2 * HD] + weight[:, 2 * HD :]
            lows.append(weight.astype(LOW))
        low = jnp.concatenate(lows, axis=0) if qn > 1 else lows[0]
        weights[kind][i] = low
        acc[q0 * TILE : (q0 + qn) * TILE, 0:HD] += jnp.dot(low, kv[slot, :, HD:], preferred_element_type=jnp.float32)

    def to_sibling(slot):
        return pltpu.make_async_remote_copy(
            src_ref=sib_send.at[slot],
            dst_ref=sib_recv.at[slot],
            send_sem=sib_sent,
            recv_sem=sib_got.at[slot],
            device_id=sibling,
            device_id_type=MESH,
        )

    def send_sum(slot):
        @pl.when(slot < 8)
        def _():
            owner = tile_of(*slot_at(0, slot))
            for y in range(2):
                copy_to(
                    sum_stage.at[slot, y],
                    dkv_ref.at[head],
                    sum_send,
                    dkv_recv,
                    (owner, 2 * y + core),
                    here,
                )

        def pass_back(device):
            pltpu.make_async_remote_copy(
                src_ref=sum_stage.at[slot],
                dst_ref=near_recv.at[slot - 8],
                send_sem=sum_send,
                recv_sem=near_got.at[slot - 8],
                device_id=device,
                device_id_type=MESH,
            ).start()

        wide = (slot >= 12) & (slot < 16)
        pl.when(wide)(lambda: pass_back(wide_near))
        pl.when((slot >= 8) & jnp.logical_not(wide))(lambda: pass_back(time_near))

    def taken(g):
        own = (17 - g) % 8
        return jnp.where(g < 2, 17 - g, jnp.where(g < 6, 13 - g, jnp.where(g < 10, 21 - g, own)))

    def wait_terms(slot):
        to_sibling(slot).wait_recv()
        for at in near_terms(slot):
            pl.when(at < 10)(lambda at=at: arrived(near_recv.at[at], near_got.at[at]))

    def near_terms(slot):
        near_t, kh, near_w = slot_at(0, slot)
        own = slot < 8
        time_at = jnp.where(own & (near_t == 0), near_w * 2 + kh, 10)
        wide_at = jnp.where(own & (near_w == 0), 4 + near_t * 2 + kh, 10)
        return time_at, jnp.where((slot == 12) | (slot == 13), slot - 4, wide_at)

    def add_terms(slot, held):
        terms = near_terms(slot)
        for y in range(2):
            total = part_sum[held, quarter(2 * y + core)] + sib_recv[slot, y].astype(jnp.float32)
            for at in terms:
                total += near_recv[at, y].astype(jnp.float32)
            sum_stage[slot, y] = total.astype(LOW)

    def finish_sum(g):
        slot = taken(g)
        wait_terms(slot)
        add_terms(slot, g % (LAG + 1))
        send_sum(slot)

    def grad_step(kind, g):
        first, count, q0, qn = KINDS[kind]
        slot = taken(g)
        i = slot - first
        held = g % (LAG + 1)
        done = g >= LAG
        before = jnp.where(done, taken(g - LAG), SLOTS)
        rows = slice(q0 * TILE, (q0 + qn) * TILE)
        pl.when(done)(lambda: wait_terms(before))
        add_terms(before, (g + 1) % (LAG + 1))
        low = weights[kind][i]
        prob_grad = nt(scaled[rows, 2 * HD :], kv[slot, :, HD:])
        score_grad = (low.astype(jnp.float32) * (prob_grad - thrice(row_dot[rows]))).astype(LOW)
        dq_acc[rows] += jnp.dot(score_grad, kv[slot, :, 0:HD], preferred_element_type=jnp.float32)
        part_sum[held, :, 0:HD] = tn(score_grad, scaled[rows, 0:HD])
        part_sum[held, :, HD:] = tn(low, scaled[rows, HD : 2 * HD])
        for y in range(2):
            sib_send[slot, y] = part_sum[held, quarter(2 * y + 1 - core)].astype(LOW)
        to_sibling(slot).start()
        pl.when(done)(lambda: send_sum(before))

    def send_result(stage, dst, send_sem, recv_sem):
        for u in range(4):
            for j in range(4):
                copy_to(
                    stage.at[u, quarter(j)],
                    dst.at[:, lanes_of(head)],
                    send_sem,
                    recv_sem,
                    (tile_of(QUERY_AT[u][0], core, QUERY_AT[u][1]), j),
                    here,
                )

    @pl.when(active)
    def _():
        acc[...] = jnp.zeros_like(acc)
        dq_acc[...] = jnp.zeros_like(dq_acc)
        near_recv[10] = jnp.zeros((2, QUARTER, 2 * HD), LOW)
        sib_recv[SLOTS] = jnp.zeros((2, QUARTER, 2 * HD), LOW)

        @pl.loop(0, 4)
        def _(i):
            pass_on(0, i)

        @pl.loop(0, 2)
        def _(i):
            pass_on(2, i)

        arrived(qg, qg_recv)
        for u in range(4):
            q = qg[u, :, 0:HD].astype(jnp.float32)
            inverse = lax.rsqrt(jnp.mean(q * q, axis=-1, keepdims=True) + EPSILON)
            rows = slice(u * TILE, (u + 1) * TILE)
            q_unit[rows] = (q * inverse).astype(LOW)
            scaled[rows, 2 * HD :] = qg[u, :, HD:]

        @pl.loop(0, 8)
        def _(i):
            score_step(0, i)
            pl.when(i < 4)(lambda: pass_on(0, i + 4))
            pl.when(i >= 4)(lambda: pass_on(1, i - 4))
            pl.when(i >= 6)(lambda: pass_on(2, i - 4))

        @pl.loop(0, 2)
        def _(i):
            pass_on(3, i)

        for kind in (2, 1, 3):

            @pl.loop(0, KINDS[kind][1])
            def _(i):
                score_step(kind, i)

        for u in range(4):
            rows = slice(u * TILE, (u + 1) * TILE)
            over[rows] = jnp.broadcast_to(1.0 / jnp.sum(acc[rows, HD:], axis=-1, keepdims=True), (TILE, HD))
            out = (acc[rows, 0:HD] * over[rows]).astype(LOW)
            o_stage[u] = out
            grad = qg[u, :, HD:].astype(jnp.float32)
            dot = jnp.sum(grad * out.astype(jnp.float32), axis=-1, keepdims=True)
            row_dot[rows] = jnp.broadcast_to(dot, (TILE, HD))
            scaled[rows, 0:HD] = (q_unit[rows].astype(jnp.float32) * (over[rows] * SCALE)).astype(LOW)
            scaled[rows, HD : 2 * HD] = (grad * over[rows]).astype(LOW)
        send_result(o_stage, o_ref, o_send, o_recv)

        for kind, start in ((3, 0), (1, 2), (2, 6), (0, 10)):

            @pl.loop(start, start + KINDS[kind][1])
            def _(g):
                grad_step(kind, g)

        finish_sum(SLOTS - 3)
        for u in range(4):
            rows = slice(u * TILE, (u + 1) * TILE)
            q = qg[u, :, 0:HD].astype(jnp.float32)
            inverse = lax.rsqrt(jnp.mean(q * q, axis=-1, keepdims=True) + EPSILON)
            unit = q * inverse
            grad_in = dq_acc[rows] * (over[rows] * SCALE)
            dq = inverse * (grad_in - unit * jnp.mean(grad_in * unit, axis=-1, keepdims=True))
            dq_stage[u] = dq.astype(LOW)
        finish_sum(SLOTS - 2)
        finish_sum(SLOTS - 1)
        send_result(dq_stage, dq_ref, dq_send, dq_recv)

    arrived(dkv_ref, dkv_recv)
    arrived(o_ref, o_recv)
    arrived(dq_ref, dq_recv)

    def left(ref, sem, kept, own):
        pl.when(kept)(lambda: arrived(ref.at[pl.ds(0, own)], sem))
        pl.when(jnp.logical_not(kept))(lambda: arrived(ref, sem))

    left(kv_stage, kv_send, active, HEADS - 1)
    left(qg_stage, qg_send, active & (h == core), HEADS - 1)

    @pl.when(active)
    def _():
        arrived(sib_send, relay_send)
        arrived(sib_send.at[pl.ds(0, 6)], time_send)
        arrived(sib_send.at[pl.ds(0, 4)], wide_send)
        arrived(sib_send, sib_sent)
        arrived(sib_send.at[pl.ds(0, SLOTS - 1)], sum_send)
        arrived(sib_send.at[0, 0], sum_send)
        for stage, sem in ((o_stage, o_send), (dq_stage, dq_send)):
            arrived(stage.at[pl.ds(0, 3)], sem)
            arrived(stage.at[3, pl.ds(0, 3 * QUARTER)], sem)
            pl.when(h != core)(lambda: arrived(stage.at[3, quarter(3)], sem))


def finish_kernel(o_in, dq_in, dkv_in, k_in, o_ref, dq_ref, dk_ref, dv_ref):
    o_ref[...] = o_in[...]
    dq_ref[...] = dq_in[...]
    for n in range(HEADS):
        lanes = slice(n * HD, (n + 1) * HD)
        k = k_in[:, lanes].astype(jnp.float32)
        inverse = lax.rsqrt(jnp.mean(k * k, axis=-1, keepdims=True) + EPSILON)
        unit = k * inverse
        grad_in = dkv_in[n, :, 0:HD].astype(jnp.float32)
        dk = inverse * (grad_in - unit * jnp.mean(grad_in * unit, axis=-1, keepdims=True))
        dk_ref[:, lanes] = dk.astype(LOW)
        dv_ref[:, lanes] = dkv_in[n, :, HD:]


def shards(queries, keys, values, out_grad, window):
    vmem = pl.BlockSpec(memory_space=pltpu.VMEM)
    smem = pl.BlockSpec(memory_space=pltpu.SMEM)
    hbm = pl.BlockSpec(memory_space=pl.ANY)
    dma = pltpu.SemaphoreType.DMA
    f32 = jnp.float32
    rows = jax.ShapeDtypeStruct((QUARTER, HEADS * HD), LOW)
    o, dq, dkv = pl.pallas_call(
        attend_kernel,
        out_shape=(rows, rows, jax.ShapeDtypeStruct((HEADS, QUARTER, 2 * HD), LOW)),
        in_specs=[smem] + [hbm] * 4,
        out_specs=(hbm,) * 3,
        scratch_shapes=[
            pltpu.VMEM((QUARTER, HEADS * HD), LOW),
            pltpu.VMEM((QUARTER, HEADS * HD), LOW),
            pltpu.VMEM((QUARTER, HEADS * HD), LOW),
            pltpu.VMEM((QUARTER, HEADS * HD), LOW),
            pltpu.VMEM((HEADS, QUARTER, 2 * HD), LOW),
            pltpu.VMEM((HEADS, QUARTER, 2 * HD), LOW),
            pltpu.VMEM((SLOTS, TILE, 2 * HD), LOW),
            pltpu.VMEM((4, TILE, 2 * HD), LOW),
            pltpu.VMEM((4 * TILE, HD), LOW),
            pltpu.VMEM((8, 4 * TILE, TILE), LOW),
            pltpu.VMEM((4, 2 * TILE, TILE), LOW),
            pltpu.VMEM((4, 2 * TILE, TILE), LOW),
            pltpu.VMEM((2, TILE, TILE), LOW),
            pltpu.VMEM((4 * TILE, 2 * HD), f32),
            pltpu.VMEM((4 * TILE, HD), f32),
            pltpu.VMEM((4 * TILE, HD), f32),
            pltpu.VMEM((4 * TILE, HD), f32),
            pltpu.VMEM((4 * TILE, 3 * HD), LOW),
            pltpu.VMEM((4, TILE, HD), LOW),
            pltpu.VMEM((4, TILE, HD), LOW),
            pltpu.VMEM((LAG + 1, TILE, 2 * HD), f32),
            pltpu.VMEM((SLOTS, 2, QUARTER, 2 * HD), LOW),
            pltpu.VMEM((SLOTS + 1, 2, QUARTER, 2 * HD), LOW),
            pltpu.VMEM((SLOTS + 1, 2, QUARTER, 2 * HD), LOW),
            pltpu.VMEM((11, 2, QUARTER, 2 * HD), LOW),
            dma((4,)),
            pltpu.SemaphoreType.DMA,
            pltpu.SemaphoreType.DMA,
            dma((SLOTS, 4)),
            pltpu.SemaphoreType.DMA,
            pltpu.SemaphoreType.DMA,
            pltpu.SemaphoreType.DMA,
            pltpu.SemaphoreType.DMA,
            pltpu.SemaphoreType.DMA,
            dma((SLOTS,)),
            dma((10,)),
            pltpu.SemaphoreType.DMA,
            pltpu.SemaphoreType.DMA,
            pltpu.SemaphoreType.DMA,
            pltpu.SemaphoreType.DMA,
            pltpu.SemaphoreType.DMA,
            pltpu.SemaphoreType.DMA,
        ],
        compiler_params=pltpu.CompilerParams(collective_id=0, has_side_effects=True, vmem_limit_bytes=VMEM_LIMIT),
        name="attend",
    )(window, queries, keys, values, out_grad)

    return pl.pallas_call(
        finish_kernel,
        out_shape=(rows,) * 4,
        in_specs=[vmem] * 4,
        out_specs=(vmem,) * 4,
        compiler_params=pltpu.CompilerParams(vmem_limit_bytes=VMEM_LIMIT),
        name="finish",
    )(o, dq, dkv, keys)


def solution(mesh):
    rows = P(("tm", "head"), None)
    return jax.shard_map(
        shards, mesh=mesh, in_specs=(rows, rows, rows, rows, P()), out_specs=(rows, rows, rows, rows), check_vma=False
    )
```

```python
import jax
import jax.numpy as jnp
from jax import lax
from jax.experimental import pallas as pl
from jax.experimental.pallas import tpu as pltpu
from jax.sharding import PartitionSpec as P

TILE = 384
HEADS = 12
HD = 128
QUARTER = 96
PAIR = 768
SLOTS = 9
LAG = 1
EPSILON = 1e-06
SCALE = HD**-0.5
LOG2E = 1.4426950408889634
MESH = pl.DeviceIdType.MESH
VMEM_LIMIT = 60 * 1024 * 1024
LOW = jnp.bfloat16

QUERY_AT = ((0, 1), (0, 0), (1, 0), (1, 1))
KINDS = ((0, 4, 0, 4), (4, 2, 0, 2), (6, 2, 1, 2), (8, 1, 1, 1))


def worker_of(n, T, W, core):
    y = n % 4
    spot = (n // 4 + y + 1) % 4
    x, z = absolute(T, spot // 2), 2 * (spot % 2) + W
    return x * 8 + z * 2 + y // 2, (y % 2) * 2 + core


def work_here(tm, part):
    x, y, z = tm // 8, tm % 2 * 2 + part // 2, tm // 2 % 4
    T, W = x // 2, z % 2
    row = (relative(T, x) * 2 + z // 2 + 7 - y) % 4
    return row < 3, jnp.where(row < 3, row * 4 + y, 0), T, W, part % 2


def absolute(half, near):
    return 1 + half + near * (2 * half - 1)


def relative(half, index):
    return (index - 1 - half) * (2 * half - 1)


def pair_at(kind, i):
    if kind == 0:
        return i // 2, i % 2
    if kind == 1:
        return -1, i
    if kind == 2:
        return i, -1
    return -1, -1


def query_number(near_t, near_w):
    return jnp.where(near_t == 0, 1 - near_w, 2 + near_w)


def copy_to(src, dst, send_sem, recv_sem, device, here):
    same = (device[0] == here[0]) & (device[1] == here[1])

    @pl.when(same)
    def _():
        pltpu.make_async_copy(src, dst, recv_sem).start()

    @pl.when(jnp.logical_not(same))
    def _():
        pltpu.make_async_remote_copy(
            src_ref=src, dst_ref=dst, send_sem=send_sem, recv_sem=recv_sem, device_id=device, device_id_type=MESH
        ).start()


def arrived(ref, sem):
    pltpu.make_async_copy(ref, ref, sem).wait()


def nt(a, b):
    return lax.dot_general(a, b, (((1,), (1,)), ((), ())), preferred_element_type=jnp.float32)


def quarter(j):
    return pl.ds(pl.multiple_of(j * QUARTER, QUARTER), QUARTER)


def half(core):
    return pl.ds(pl.multiple_of(core * TILE, TILE), TILE)


def lanes_of(n):
    return pl.ds(pl.multiple_of(n * HD, HD), HD)


def repeated(value):
    return jnp.concatenate([value] * (PAIR // HD), axis=1)


def attend_kernel(
    window_hbm,
    q_hbm,
    k_hbm,
    v_hbm,
    g_hbm,
    o_ref,
    dq_ref,
    dkv_ref,
    window_ref,
    q_in,
    k_in,
    v_in,
    g_in,
    kv_stage,
    qg_stage,
    kv,
    qg,
    q_unit,
    weights0,
    weights1,
    weights2,
    weights3,
    acc,
    dq_acc,
    over,
    row_dot,
    scaled,
    grad_rows,
    o_stage,
    dq_stage,
    part_sum,
    sib_send,
    sib_recv,
    sum_stage,
    near_recv,
    in_sem,
    kv_send,
    qg_send,
    kv_recv,
    qg_recv,
    relay_send,
    time_send,
    wide_send,
    sib_sent,
    sib_got,
    near_got,
    o_send,
    dq_send,
    sum_send,
    o_recv,
    dq_recv,
    dkv_recv,
):
    tm, part = lax.axis_index("tm"), lax.axis_index("head")
    here = (tm, part)
    t, h, w = tm // 8, tm // 4 % 2, tm % 4
    active, head, T, W, core = work_here(tm, part)
    home_t, home_w = t // 2, w // 2
    own_t, own_w = relative(home_t, t), relative(home_w, w)
    sibling = (tm, part + 1 - 2 * core)
    time_near = worker_of(head, 1 - T, W, core)
    wide_near = worker_of(head, T, 1 - W, core)
    weights = (weights0, weights1, weights2, weights3)

    def copy_in(i):
        source = (k_hbm, v_hbm, q_hbm, g_hbm, window_hbm)[i]
        return pltpu.make_async_copy(source, (k_in, v_in, q_in, g_in, window_ref)[i], in_sem.at[i])

    for i in range(5):
        copy_in(i).start()

    def tile_of(near_t, kh, near_w):
        return absolute(T, near_t) * 8 + kh * 4 + absolute(W, near_w)

    barrier = pltpu.get_barrier_semaphore()

    def greet(device, count):
        other = jnp.logical_not((device[0] == tm) & (device[1] == part))

        @pl.when(other)
        def _():
            pl.semaphore_signal(barrier, inc=1, device_id=device, device_id_type=MESH)

        return count + other.astype(jnp.int32)

    def greet_workers(n, count):
        count = greet(worker_of(n, home_t, home_w, core), count)
        return lax.cond(h != core, lambda c: greet(worker_of(n, home_t, home_w, h), c), lambda c: c, count)

    greeted = lax.fori_loop(0, HEADS, greet_workers, jnp.int32(0))

    def greet_owners(i, count):
        near_t, kh, near_w = i // 4, i % 2, i // 2 % 2
        owner = tile_of(near_t, kh, near_w)
        for y in range(2):
            count = greet((owner, 2 * y + core), count)

        def others(count):
            for y in range(2):
                count = greet((owner, 2 * y + 1 - core), count)
            return count

        return lax.cond(kh == core, others, lambda count: count, count)

    def greet_all(count):
        count = lax.fori_loop(0, 8, greet_owners, count)
        for device in (sibling, time_near, wide_near):
            count = greet(device, count)
        return count

    greeted = lax.cond(active, greet_all, lambda count: count, greeted)

    copy_in(0).wait()
    copy_in(1).wait()

    @pl.loop(0, HEADS)
    def _(n):
        lanes = lanes_of(n)
        k = k_in[:, lanes].astype(jnp.float32)
        inverse = lax.rsqrt(jnp.mean(k * k, axis=-1, keepdims=True) + EPSILON)
        kv_stage[n, :, 0:HD] = (k * inverse).astype(LOW)
        kv_stage[n, :, HD:] = v_in[:, lanes]

    pl.semaphore_wait(barrier, greeted)

    def send_keys():
        slot = own_t * 2 + own_w
        rows = pl.ds(pl.multiple_of(core * TILE + h * 2 * QUARTER + part // 2 * QUARTER, QUARTER), QUARTER)

        @pl.loop(0, HEADS)
        def _(n):
            copy_to(
                kv_stage.at[n],
                kv.at[slot, rows],
                kv_send,
                kv_recv.at[slot, core],
                worker_of(n, home_t, home_w, core),
                here,
            )

    def send_queries():
        at = query_number(own_t, own_w)

        @pl.loop(0, HEADS)
        def _(n):
            copy_to(
                qg_stage.at[n],
                qg.at[at, quarter(part)],
                qg_send,
                qg_recv,
                worker_of(n, home_t, home_w, h),
                here,
            )

    send_keys()
    copy_in(2).wait()
    copy_in(3).wait()

    @pl.loop(0, HEADS)
    def _(n):
        lanes = lanes_of(n)
        qg_stage[n, :, 0:HD] = q_in[:, lanes]
        qg_stage[n, :, HD:] = g_in[:, lanes]

    send_queries()
    copy_in(4).wait()

    def pass_on(kind, i):
        slot = KINDS[kind][0] + i
        near_t, near_w = pair_at(kind, i)
        arrived(kv.at[slot, half(core)], kv_recv.at[slot, core])

        def send(device, to, sem):
            pltpu.make_async_remote_copy(
                src_ref=kv.at[slot, half(core)],
                dst_ref=kv.at[to, half(core)],
                send_sem=sem,
                recv_sem=kv_recv.at[to, core],
                device_id=device,
                device_id_type=MESH,
            ).start()

        if kind == 0:
            pl.when(near_w == 0)(lambda: send(wide_near, 6 + near_t, wide_send))
        if kind in (0, 2):
            to = 4 + near_w if kind == 0 else 8
            pl.when(near_t == 0)(lambda: send(time_near, to, time_send))
        send(sibling, slot, relay_send)

    def relayed(slot):
        arrived(kv.at[slot, half(1 - core)], kv_recv.at[slot, 1 - core])

    def score_step(kind, i):
        first, count, q0, qn = KINDS[kind]
        slot = first + i
        near_t, near_w = pair_at(kind, i)
        relayed(slot)
        scores = nt(q_unit[q0 * TILE : (q0 + qn) * TILE], kv[slot, :, 0:HD])
        column = lax.broadcasted_iota(jnp.int32, (1, PAIR), 1)
        lower = (column < PAIR // 4) | ((column >= PAIR // 2) & (column < 3 * PAIR // 4))
        lows = []
        for u in range(qn):
            qt, qw = QUERY_AT[q0 + u]
            dt = absolute(T, near_t) - absolute(T, qt)
            dw = absolute(W, near_w) - absolute(W, qw)
            tile = tile_of(qt, core, qw)
            live = [window_ref[tile, 9 * (dt + 1) + 3 * (kh - core + 1) + dw + 1] for kh in range(2)]
            bias = [(one.astype(jnp.float32) - 1.0) * 1e30 for one in live]
            weight = jnp.exp2(scores[u * TILE : (u + 1) * TILE] * (SCALE * LOG2E) + jnp.where(lower, bias[0], bias[1]))
            rows = slice((q0 + u) * TILE, (q0 + u + 1) * TILE)
            total = weight[:, 0:HD]
            for at in range(HD, PAIR, HD):
                total += weight[:, at : at + HD]
            acc[rows, HD:] += total
            lows.append(weight.astype(LOW))
        low = jnp.concatenate(lows, axis=0) if qn > 1 else lows[0]
        weights[kind][i] = low
        acc[q0 * TILE : (q0 + qn) * TILE, 0:HD] += jnp.dot(low, kv[slot, :, HD:], preferred_element_type=jnp.float32)

    def to_sibling(slot):
        return pltpu.make_async_remote_copy(
            src_ref=sib_send.at[slot],
            dst_ref=sib_recv.at[slot],
            send_sem=sib_sent,
            recv_sem=sib_got.at[slot],
            device_id=sibling,
            device_id_type=MESH,
        )

    def send_sum(slot):
        @pl.when(slot < 4)
        def _():
            near_t, near_w = pair_at(0, slot)
            for kh in range(2):
                for y in range(2):
                    copy_to(
                        sum_stage.at[slot, quarter(kh * 2 + y)],
                        dkv_ref.at[head],
                        sum_send,
                        dkv_recv,
                        (tile_of(near_t, kh, near_w), 2 * y + core),
                        here,
                    )

        def pass_back(device):
            pltpu.make_async_remote_copy(
                src_ref=sum_stage.at[slot],
                dst_ref=near_recv.at[slot - 4],
                send_sem=sum_send,
                recv_sem=near_got.at[slot - 4],
                device_id=device,
                device_id_type=MESH,
            ).start()

        wide = (slot == 6) | (slot == 7)
        pl.when(wide)(lambda: pass_back(wide_near))
        pl.when((slot >= 4) & jnp.logical_not(wide))(lambda: pass_back(time_near))

    def taken(g):
        return jnp.where(g < 1, 8, jnp.where(g < 3, 6 - g, jnp.where(g < 5, 10 - g, 8 - g)))

    def finish_sum(g):
        slot = taken(g)
        near_t, near_w = pair_at(0, slot)
        own = slot < 4
        time_at = jnp.where(own & (near_t == 0), near_w, 5)
        wide_at = jnp.where(slot == 6, 4, jnp.where(own & (near_w == 0), 2 + near_t, 5))
        to_sibling(slot).wait_recv()
        for at in (time_at, wide_at):
            pl.when(at < 5)(lambda at=at: arrived(near_recv.at[at], near_got.at[at]))
        total = part_sum[g % (LAG + 1), half(core)] + sib_recv[slot].astype(jnp.float32)
        for at in (time_at, wide_at):
            total += near_recv[at].astype(jnp.float32)
        sum_stage[slot] = total.astype(LOW)
        send_sum(slot)

    def grad_step(kind, g):
        first, count, q0, qn = KINDS[kind]
        slot = taken(g)
        held = g % (LAG + 1)
        rows = slice(q0 * TILE, (q0 + qn) * TILE)
        low = weights[kind][slot - first]
        prob_grad = nt(grad_rows[rows], kv[slot, :, HD:])
        score_grad = (low.astype(jnp.float32) * (prob_grad - repeated(row_dot[rows]))).astype(LOW)
        dq_acc[rows] += jnp.dot(score_grad, kv[slot, :, 0:HD], preferred_element_type=jnp.float32)
        part_sum[held, :, 0:HD] = jnp.dot(scaled[0:HD, rows], score_grad, preferred_element_type=jnp.float32).T
        part_sum[held, :, HD:] = jnp.dot(scaled[HD:, rows], low, preferred_element_type=jnp.float32).T
        sib_send[slot] = part_sum[held, half(1 - core)].astype(LOW)
        to_sibling(slot).start()
        pl.when(g >= LAG)(lambda: finish_sum(g - LAG))

    def send_result(u, stage, dst, send_sem, recv_sem):
        near_t, near_w = u // 2, jnp.where((u == 1) | (u == 2), 0, 1)
        for j in range(4):
            copy_to(
                stage.at[u, quarter(j)],
                dst.at[:, lanes_of(head)],
                send_sem,
                recv_sem,
                (tile_of(near_t, core, near_w), j),
                here,
            )

    @pl.when(active)
    def _():
        acc[...] = jnp.zeros_like(acc)
        dq_acc[...] = jnp.zeros_like(dq_acc)
        near_recv[5] = jnp.zeros((TILE, 2 * HD), LOW)

        pass_on(0, 0)
        pass_on(0, 1)
        pass_on(2, 0)
        arrived(qg, qg_recv)
        for u in range(4):
            q = qg[u, :, 0:HD].astype(jnp.float32)
            inverse = lax.rsqrt(jnp.mean(q * q, axis=-1, keepdims=True) + EPSILON)
            rows = slice(u * TILE, (u + 1) * TILE)
            q_unit[rows] = (q * inverse).astype(LOW)
            grad_rows[rows] = qg[u, :, HD:]

        @pl.loop(0, 4)
        def _(i):
            score_step(0, i)
            pl.when(i < 2)(lambda: pass_on(0, i + 2))
            pl.when(i >= 2)(lambda: pass_on(1, i - 2))

        pass_on(2, 1)
        pass_on(3, 0)

        for kind in (2, 1, 3):

            @pl.loop(0, KINDS[kind][1])
            def _(i):
                score_step(kind, i)

        for u in range(4):
            rows = slice(u * TILE, (u + 1) * TILE)
            over[rows] = jnp.broadcast_to(1.0 / jnp.sum(acc[rows, HD:], axis=-1, keepdims=True), (TILE, HD))
            out = (acc[rows, 0:HD] * over[rows]).astype(LOW)
            o_stage[u] = out
            grad = qg[u, :, HD:].astype(jnp.float32)
            dot = jnp.sum(grad * out.astype(jnp.float32), axis=-1, keepdims=True)
            row_dot[rows] = jnp.broadcast_to(dot, (TILE, HD))
            scaled[0:HD, rows] = (q_unit[rows].astype(jnp.float32) * (over[rows] * SCALE)).T.astype(LOW)
            scaled[HD:, rows] = (grad * over[rows]).T.astype(LOW)

        for kind, start in ((3, 0), (1, 1), (2, 3), (0, 5)):

            @pl.loop(start, start + KINDS[kind][1])
            def _(g):
                grad_step(kind, g)
                if kind in (1, 2):
                    send_result(g - 1, o_stage, o_ref, o_send, o_recv)

        for u in range(4):
            rows = slice(u * TILE, (u + 1) * TILE)
            q = qg[u, :, 0:HD].astype(jnp.float32)
            inverse = lax.rsqrt(jnp.mean(q * q, axis=-1, keepdims=True) + EPSILON)
            unit = q * inverse
            grad_in = dq_acc[rows] * (over[rows] * SCALE)
            dq = inverse * (grad_in - unit * jnp.mean(grad_in * unit, axis=-1, keepdims=True))
            dq_stage[u] = dq.astype(LOW)
        for g in range(SLOTS - LAG, SLOTS):
            finish_sum(g)

        @pl.loop(0, 4)
        def _(u):
            send_result(u, dq_stage, dq_ref, dq_send, dq_recv)

    arrived(dkv_ref, dkv_recv)
    arrived(o_ref, o_recv)
    arrived(dq_ref, dq_recv)

    def left(ref, sem, kept, own):
        pl.when(kept)(lambda: arrived(ref.at[pl.ds(0, own)], sem))
        pl.when(jnp.logical_not(kept))(lambda: arrived(ref, sem))

    left(kv_stage, kv_send, active, HEADS - 1)
    left(qg_stage, qg_send, active & (h == core), HEADS - 1)

    @pl.when(active)
    def _():
        arrived(sib_send, relay_send)
        arrived(sib_send.at[pl.ds(0, 3)], time_send)
        arrived(sib_send.at[pl.ds(0, 2)], wide_send)
        arrived(sib_send, sib_sent)
        arrived(sib_send.at[pl.ds(0, SLOTS - 1)], sum_send)
        arrived(sib_send.at[0, pl.ds(0, 3 * QUARTER)], sum_send)
        for stage, sem in ((o_stage, o_send), (dq_stage, dq_send)):
            arrived(stage.at[pl.ds(0, 3)], sem)
            arrived(stage.at[3, pl.ds(0, 3 * QUARTER)], sem)
            pl.when(h != core)(lambda: arrived(stage.at[3, quarter(3)], sem))


def finish_kernel(o_in, dq_in, dkv_in, k_in, o_ref, dq_ref, dk_ref, dv_ref, o, dq, dkv, k_raw, dk, dv, in_sem, out_sem):
    parts = 3
    heads = HEADS // parts

    def lanes_in(p):
        return slice(p * heads * HD, (p + 1) * heads * HD)

    loads = [(o_in, o), (dq_in, dq)]
    for p in range(parts):
        loads.append((dkv_in.at[p * heads : (p + 1) * heads], dkv.at[p * heads : (p + 1) * heads]))
        loads.append((k_in.at[:, lanes_in(p)], k_raw.at[:, lanes_in(p)]))
    loads = [pltpu.make_async_copy(a, b, in_sem.at[i]) for i, (a, b) in enumerate(loads)]
    stores = [(o, o_ref), (dq, dq_ref)]
    for p in range(parts):
        stores.append((dk.at[:, lanes_in(p)], dk_ref.at[:, lanes_in(p)]))
        stores.append((dv.at[:, lanes_in(p)], dv_ref.at[:, lanes_in(p)]))
    stores = [pltpu.make_async_copy(a, b, out_sem.at[i]) for i, (a, b) in enumerate(stores)]
    for load in loads:
        load.start()
    for i in range(2):
        loads[i].wait()
        stores[i].start()
    for p in range(parts):
        loads[2 + 2 * p].wait()
        loads[3 + 2 * p].wait()
        for n in range(p * heads, (p + 1) * heads):
            lanes = slice(n * HD, (n + 1) * HD)
            k = k_raw[:, lanes].astype(jnp.float32)
            inverse = lax.rsqrt(jnp.mean(k * k, axis=-1, keepdims=True) + EPSILON)
            unit = k * inverse
            grad_in = dkv[n, :, 0:HD].astype(jnp.float32)
            grad = inverse * (grad_in - unit * jnp.mean(grad_in * unit, axis=-1, keepdims=True))
            dk[:, lanes] = grad.astype(LOW)
            dv[:, lanes] = dkv[n, :, HD:]
        stores[2 + 2 * p].start()
        stores[3 + 2 * p].start()
    for store in stores:
        store.wait()


def shards(queries, keys, values, out_grad, window):
    hbm = pl.BlockSpec(memory_space=pl.ANY)
    dma = pltpu.SemaphoreType.DMA
    f32 = jnp.float32
    rows = jax.ShapeDtypeStruct((QUARTER, HEADS * HD), LOW)
    o, dq, dkv = pl.pallas_call(
        attend_kernel,
        out_shape=(rows, rows, jax.ShapeDtypeStruct((HEADS, QUARTER, 2 * HD), LOW)),
        in_specs=[hbm] * 5,
        out_specs=(hbm,) * 3,
        scratch_shapes=[
            pltpu.SMEM(window.shape, window.dtype),
            pltpu.VMEM((QUARTER, HEADS * HD), LOW),
            pltpu.VMEM((QUARTER, HEADS * HD), LOW),
            pltpu.VMEM((QUARTER, HEADS * HD), LOW),
            pltpu.VMEM((QUARTER, HEADS * HD), LOW),
            pltpu.VMEM((HEADS, QUARTER, 2 * HD), LOW),
            pltpu.VMEM((HEADS, QUARTER, 2 * HD), LOW),
            pltpu.VMEM((SLOTS, PAIR, 2 * HD), LOW),
            pltpu.VMEM((4, TILE, 2 * HD), LOW),
            pltpu.VMEM((4 * TILE, HD), LOW),
            pltpu.VMEM((4, 4 * TILE, PAIR), LOW),
            pltpu.VMEM((2, 2 * TILE, PAIR), LOW),
            pltpu.VMEM((2, 2 * TILE, PAIR), LOW),
            pltpu.VMEM((1, TILE, PAIR), LOW),
            pltpu.VMEM((4 * TILE, 2 * HD), f32),
            pltpu.VMEM((4 * TILE, HD), f32),
            pltpu.VMEM((4 * TILE, HD), f32),
            pltpu.VMEM((4 * TILE, HD), f32),
            pltpu.VMEM((2 * HD, 4 * TILE), LOW),
            pltpu.VMEM((4 * TILE, HD), LOW),
            pltpu.VMEM((4, TILE, HD), LOW),
            pltpu.VMEM((4, TILE, HD), LOW),
            pltpu.VMEM((LAG + 1, PAIR, 2 * HD), f32),
            pltpu.VMEM((SLOTS, TILE, 2 * HD), LOW),
            pltpu.VMEM((SLOTS, TILE, 2 * HD), LOW),
            pltpu.VMEM((SLOTS, TILE, 2 * HD), LOW),
            pltpu.VMEM((6, TILE, 2 * HD), LOW),
            dma((5,)),
            pltpu.SemaphoreType.DMA,
            pltpu.SemaphoreType.DMA,
            dma((SLOTS, 2)),
            pltpu.SemaphoreType.DMA,
            pltpu.SemaphoreType.DMA,
            pltpu.SemaphoreType.DMA,
            pltpu.SemaphoreType.DMA,
            pltpu.SemaphoreType.DMA,
            dma((SLOTS,)),
            dma((5,)),
            pltpu.SemaphoreType.DMA,
            pltpu.SemaphoreType.DMA,
            pltpu.SemaphoreType.DMA,
            pltpu.SemaphoreType.DMA,
            pltpu.SemaphoreType.DMA,
            pltpu.SemaphoreType.DMA,
        ],
        compiler_params=pltpu.CompilerParams(collective_id=0, has_side_effects=True, vmem_limit_bytes=VMEM_LIMIT),
        name="attend",
    )(window, queries, keys, values, out_grad)

    return pl.pallas_call(
        finish_kernel,
        out_shape=(rows,) * 4,
        in_specs=[hbm] * 4,
        out_specs=(hbm,) * 4,
        scratch_shapes=[
            pltpu.VMEM((QUARTER, HEADS * HD), LOW),
            pltpu.VMEM((QUARTER, HEADS * HD), LOW),
            pltpu.VMEM((HEADS, QUARTER, 2 * HD), LOW),
            pltpu.VMEM((QUARTER, HEADS * HD), LOW),
            pltpu.VMEM((QUARTER, HEADS * HD), LOW),
            pltpu.VMEM((QUARTER, HEADS * HD), LOW),
            dma((8,)),
            dma((8,)),
        ],
        compiler_params=pltpu.CompilerParams(vmem_limit_bytes=VMEM_LIMIT),
        name="finish",
    )(o, dq, dkv, keys)


def solution(mesh):
    rows = P(("tm", "head"), None)
    return jax.shard_map(
        shards, mesh=mesh, in_specs=(rows, rows, rows, rows, P()), out_specs=(rows, rows, rows, rows), check_vma=False
    )
```

```python
import jax
import jax.numpy as jnp
from jax import lax
from jax.experimental import pallas as pl
from jax.experimental.pallas import tpu as pltpu
from jax.sharding import PartitionSpec as P

TILE = 384
HEADS = 12
HD = 128
QUARTER = 96
PAIR = 768
SLOTS = 9
EPSILON = 1e-06
SCALE = HD**-0.5
LOG2E = 1.4426950408889634
MESH = pl.DeviceIdType.MESH
VMEM_LIMIT = 60 * 1024 * 1024
LOW = jnp.bfloat16

QUERY_AT = ((0, 1), (0, 0), (1, 0), (1, 1))
KINDS = ((0, 4, 0, 4), (4, 2, 0, 2), (6, 2, 1, 2), (8, 1, 1, 1))
FAR = ((3, 0), (2, 1), (1, 1), (2, 0), (1, 0))


def worker_of(n, T, W, core):
    y = n % 4
    spot = (n // 4 + y + 1) % 4
    x, z = absolute(T, spot // 2), 2 * (spot % 2) + W
    return x * 8 + z * 2 + y // 2, (y % 2) * 2 + core


def work_here(tm, part):
    x, y, z = tm // 8, tm % 2 * 2 + part // 2, tm // 2 % 4
    T, W = x // 2, z % 2
    row = (relative(T, x) * 2 + z // 2 + 7 - y) % 4
    return row < 3, jnp.where(row < 3, row * 4 + y, 0), T, W, part % 2


def absolute(half, near):
    return 1 + half + near * (2 * half - 1)


def relative(half, index):
    return (index - 1 - half) * (2 * half - 1)


def pair_at(kind, i):
    if kind == 0:
        return i // 2, i % 2
    if kind == 1:
        return -1, i
    if kind == 2:
        return i, -1
    return -1, -1


def query_number(near_t, near_w):
    return jnp.where(near_t == 0, 1 - near_w, 2 + near_w)


def copy_to(src, dst, send_sem, recv_sem, device, here):
    same = (device[0] == here[0]) & (device[1] == here[1])

    @pl.when(same)
    def _():
        pltpu.make_async_copy(src, dst, recv_sem).start()

    @pl.when(jnp.logical_not(same))
    def _():
        pltpu.make_async_remote_copy(
            src_ref=src, dst_ref=dst, send_sem=send_sem, recv_sem=recv_sem, device_id=device, device_id_type=MESH
        ).start()


def arrived(ref, sem):
    pltpu.make_async_copy(ref, ref, sem).wait()


def nt(a, b):
    return lax.dot_general(a, b, (((1,), (1,)), ((), ())), preferred_element_type=jnp.float32)


def quarter(j):
    return pl.ds(pl.multiple_of(j * QUARTER, QUARTER), QUARTER)


def half(core):
    return pl.ds(pl.multiple_of(core * TILE, TILE), TILE)


def lanes_of(n):
    return pl.ds(pl.multiple_of(n * HD, HD), HD)


def repeated(value):
    return jnp.concatenate([value] * (PAIR // HD), axis=1)


def attend_kernel(
    window_hbm,
    q_hbm,
    k_hbm,
    v_hbm,
    g_hbm,
    o_ref,
    dq_ref,
    dkv_ref,
    window_ref,
    q_in,
    k_in,
    v_in,
    g_in,
    kv_stage,
    kv,
    q_raw,
    q_unit,
    weights0,
    weights1,
    weights2,
    weights3,
    acc,
    dq_acc,
    over,
    row_dot,
    scaled,
    grad_rows,
    o_stage,
    dq_stage,
    part_sum,
    sib_send,
    sib_recv,
    sum_stage,
    near_recv,
    in_sem,
    kv_send,
    q_send,
    g_send,
    kv_recv,
    q_recv,
    g_recv,
    relay_send,
    time_send,
    wide_send,
    sib_sent,
    sib_got,
    near_got,
    o_send,
    dq_send,
    sum_send,
    o_recv,
    dq_recv,
    dkv_recv,
):
    tm, part = lax.axis_index("tm"), lax.axis_index("head")
    here = (tm, part)
    t, h, w = tm // 8, tm // 4 % 2, tm % 4
    active, head, T, W, core = work_here(tm, part)
    home_t, home_w = t // 2, w // 2
    own_t, own_w = relative(home_t, t), relative(home_w, w)
    sibling = (tm, part + 1 - 2 * core)
    time_near = worker_of(head, 1 - T, W, core)
    wide_near = worker_of(head, T, 1 - W, core)
    weights = (weights0, weights1, weights2, weights3)

    def copy_in(i):
        source = (k_hbm, v_hbm, q_hbm, g_hbm, window_hbm)[i]
        return pltpu.make_async_copy(source, (k_in, v_in, q_in, g_in, window_ref)[i], in_sem.at[i])

    for i in range(5):
        copy_in(i).start()

    def tile_of(near_t, kh, near_w):
        return absolute(T, near_t) * 8 + kh * 4 + absolute(W, near_w)

    barrier = pltpu.get_barrier_semaphore()

    def greet(device, count):
        other = jnp.logical_not((device[0] == tm) & (device[1] == part))

        @pl.when(other)
        def _():
            pl.semaphore_signal(barrier, inc=1, device_id=device, device_id_type=MESH)

        return count + other.astype(jnp.int32)

    def greet_workers(n, count):
        count = greet(worker_of(n, home_t, home_w, core), count)
        return lax.cond(h != core, lambda c: greet(worker_of(n, home_t, home_w, h), c), lambda c: c, count)

    greeted = lax.fori_loop(0, HEADS, greet_workers, jnp.int32(0))

    def greet_owners(i, count):
        near_t, kh, near_w = i // 4, i % 2, i // 2 % 2
        owner = tile_of(near_t, kh, near_w)
        for y in range(2):
            count = greet((owner, 2 * y + core), count)

        def others(count):
            for y in range(2):
                count = greet((owner, 2 * y + 1 - core), count)
            return count

        return lax.cond(kh == core, others, lambda count: count, count)

    def greet_all(count):
        count = lax.fori_loop(0, 8, greet_owners, count)
        for device in (sibling, time_near, wide_near):
            count = greet(device, count)
        return count

    greeted = lax.cond(active, greet_all, lambda count: count, greeted)

    copy_in(0).wait()
    copy_in(1).wait()

    @pl.loop(0, HEADS)
    def _(n):
        lanes = lanes_of(n)
        k = k_in[:, lanes].astype(jnp.float32)
        inverse = lax.rsqrt(jnp.mean(k * k, axis=-1, keepdims=True) + EPSILON)
        kv_stage[n, :, 0:HD] = (k * inverse).astype(LOW)
        kv_stage[n, :, HD:] = v_in[:, lanes]

    pl.semaphore_wait(barrier, greeted)

    def send_keys():
        slot = own_t * 2 + own_w
        rows = pl.ds(pl.multiple_of(core * TILE + h * 2 * QUARTER + part // 2 * QUARTER, QUARTER), QUARTER)

        @pl.loop(0, HEADS)
        def _(n):
            copy_to(
                kv_stage.at[n],
                kv.at[slot, rows],
                kv_send,
                kv_recv.at[slot, core],
                worker_of(n, home_t, home_w, core),
                here,
            )

    def send_rows(held, to, send_sem, recv_sem):
        row = query_number(own_t, own_w) * TILE + part * QUARTER

        @pl.loop(0, HEADS)
        def _(n):
            copy_to(
                held.at[:, lanes_of(n)],
                to.at[pl.ds(pl.multiple_of(row, QUARTER), QUARTER)],
                send_sem,
                recv_sem,
                worker_of(n, home_t, home_w, h),
                here,
            )

    send_keys()
    copy_in(2).wait()
    send_rows(q_in, q_raw, q_send, q_recv)
    copy_in(3).wait()
    send_rows(g_in, grad_rows, g_send, g_recv)
    copy_in(4).wait()

    def pass_on(kind, i):
        slot = KINDS[kind][0] + i
        near_t, near_w = pair_at(kind, i)
        arrived(kv.at[slot, half(core)], kv_recv.at[slot, core])

        def send(device, to, sem):
            pltpu.make_async_remote_copy(
                src_ref=kv.at[slot, half(core)],
                dst_ref=kv.at[to, half(core)],
                send_sem=sem,
                recv_sem=kv_recv.at[to, core],
                device_id=device,
                device_id_type=MESH,
            ).start()

        if kind == 0:
            pl.when(near_w == 0)(lambda: send(wide_near, 6 + near_t, wide_send))
        if kind in (0, 2):
            to = 4 + near_w if kind == 0 else 8
            pl.when(near_t == 0)(lambda: send(time_near, to, time_send))
        send(sibling, slot, relay_send)

    def relayed(slot):
        arrived(kv.at[slot, half(1 - core)], kv_recv.at[slot, 1 - core])

    def score_step(kind, i):
        first, count, q0, qn = KINDS[kind]
        slot = first + i
        near_t, near_w = pair_at(kind, i)
        relayed(slot)
        scores = nt(q_unit[q0 * TILE : (q0 + qn) * TILE], kv[slot, :, 0:HD])
        column = lax.broadcasted_iota(jnp.int32, (1, PAIR), 1)
        lower = (column < PAIR // 4) | ((column >= PAIR // 2) & (column < 3 * PAIR // 4))
        lows = []
        for u in range(qn):
            qt, qw = QUERY_AT[q0 + u]
            dt = absolute(T, near_t) - absolute(T, qt)
            dw = absolute(W, near_w) - absolute(W, qw)
            tile = tile_of(qt, core, qw)
            live = [window_ref[tile, 9 * (dt + 1) + 3 * (kh - core + 1) + dw + 1] for kh in range(2)]
            bias = [(one.astype(jnp.float32) - 1.0) * 1e30 for one in live]
            weight = jnp.exp2(scores[u * TILE : (u + 1) * TILE] * (SCALE * LOG2E) + jnp.where(lower, bias[0], bias[1]))
            rows = slice((q0 + u) * TILE, (q0 + u + 1) * TILE)
            total = weight[:, 0:HD]
            for at in range(HD, PAIR, HD):
                total += weight[:, at : at + HD]
            acc[rows, HD:] += total
            lows.append(weight.astype(LOW))
        low = jnp.concatenate(lows, axis=0) if qn > 1 else lows[0]
        weights[kind][i] = low
        acc[q0 * TILE : (q0 + qn) * TILE, 0:HD] += jnp.dot(low, kv[slot, :, HD:], preferred_element_type=jnp.float32)

    def to_sibling(slot):
        return pltpu.make_async_remote_copy(
            src_ref=sib_send.at[slot],
            dst_ref=sib_recv.at[slot],
            send_sem=sib_sent,
            recv_sem=sib_got.at[slot],
            device_id=sibling,
            device_id_type=MESH,
        )

    def send_sum(slot):
        @pl.when(slot < 4)
        def _():
            near_t, near_w = pair_at(0, slot)
            for kh in range(2):
                for y in range(2):
                    copy_to(
                        sum_stage.at[slot, quarter(kh * 2 + y)],
                        dkv_ref.at[head],
                        sum_send,
                        dkv_recv,
                        (tile_of(near_t, kh, near_w), 2 * y + core),
                        here,
                    )

        def pass_back(device):
            pltpu.make_async_remote_copy(
                src_ref=sum_stage.at[slot],
                dst_ref=near_recv.at[slot - 4],
                send_sem=sum_send,
                recv_sem=near_got.at[slot - 4],
                device_id=device,
                device_id_type=MESH,
            ).start()

        wide = (slot == 6) | (slot == 7)
        pl.when(wide)(lambda: pass_back(wide_near))
        pl.when((slot >= 4) & jnp.logical_not(wide))(lambda: pass_back(time_near))

    def finish_sum(slot, held):
        slot = jnp.int32(slot)
        near_t, near_w = pair_at(0, slot)
        own = slot < 4
        time_at = jnp.where(own & (near_t == 0), near_w, 5)
        wide_at = jnp.where(slot == 6, 4, jnp.where(own & (near_w == 0), 2 + near_t, 5))
        to_sibling(slot).wait_recv()
        for at in (time_at, wide_at):
            pl.when(at < 5)(lambda at=at: arrived(near_recv.at[at], near_got.at[at]))
        total = part_sum[held, half(core)] + sib_recv[slot].astype(jnp.float32)
        for at in (time_at, wide_at):
            total += near_recv[at].astype(jnp.float32)
        sum_stage[slot] = total.astype(LOW)
        send_sum(slot)

    def grad_step(kind, i, held):
        first, count, q0, qn = KINDS[kind]
        slot = first + i
        rows = slice(q0 * TILE, (q0 + qn) * TILE)
        low = weights[kind][i]
        prob_grad = nt(grad_rows[rows], kv[slot, :, HD:])
        score_grad = (low.astype(jnp.float32) * (prob_grad - repeated(row_dot[rows]))).astype(LOW)
        dq_acc[rows] += jnp.dot(score_grad, kv[slot, :, 0:HD], preferred_element_type=jnp.float32)
        part_sum[held, :, 0:HD] = jnp.dot(scaled[0:HD, rows], score_grad, preferred_element_type=jnp.float32).T
        part_sum[held, :, HD:] = jnp.dot(scaled[HD:, rows], low, preferred_element_type=jnp.float32).T
        sib_send[slot] = part_sum[held, half(1 - core)].astype(LOW)
        to_sibling(slot).start()

    def send_result(u, stage, dst, send_sem, recv_sem):
        near_t, near_w = u // 2, jnp.where((u == 1) | (u == 2), 0, 1)
        for j in range(4):
            copy_to(
                stage.at[u, quarter(j)],
                dst.at[:, lanes_of(head)],
                send_sem,
                recv_sem,
                (tile_of(near_t, core, near_w), j),
                here,
            )

    @pl.when(active)
    def _():
        acc[...] = jnp.zeros_like(acc)
        dq_acc[...] = jnp.zeros_like(dq_acc)
        near_recv[5] = jnp.zeros((TILE, 2 * HD), LOW)

        pass_on(0, 0)
        pass_on(0, 1)
        pass_on(2, 0)
        arrived(q_raw, q_recv)
        for u in range(4):
            rows = slice(u * TILE, (u + 1) * TILE)
            q = q_raw[rows].astype(jnp.float32)
            inverse = lax.rsqrt(jnp.mean(q * q, axis=-1, keepdims=True) + EPSILON)
            q_unit[rows] = (q * inverse).astype(LOW)

        @pl.loop(0, 4)
        def _(i):
            score_step(0, i)
            pl.when(i < 2)(lambda: pass_on(0, i + 2))
            pl.when(i >= 2)(lambda: pass_on(1, i - 2))

        score_step(2, 0)
        pass_on(2, 1)

        @pl.loop(0, 2)
        def _(i):
            score_step(1, i)

        pass_on(3, 0)
        score_step(2, 1)
        score_step(3, 0)
        arrived(grad_rows, g_recv)

        for u in range(4):
            rows = slice(u * TILE, (u + 1) * TILE)
            over[rows] = jnp.broadcast_to(1.0 / jnp.sum(acc[rows, HD:], axis=-1, keepdims=True), (TILE, HD))
            out = (acc[rows, 0:HD] * over[rows]).astype(LOW)
            o_stage[u] = out
            grad = grad_rows[rows].astype(jnp.float32)
            dot = jnp.sum(grad * out.astype(jnp.float32), axis=-1, keepdims=True)
            row_dot[rows] = jnp.broadcast_to(dot, (TILE, HD))
            scaled[0:HD, rows] = (q_unit[rows].astype(jnp.float32) * (over[rows] * SCALE)).T.astype(LOW)
            scaled[HD:, rows] = (grad * over[rows]).T.astype(LOW)

        def finish_far(at):
            kind, i = FAR[at]
            finish_sum(KINDS[kind][0] + i, 4 + at % 2)

        for at, (kind, i) in enumerate(FAR):
            grad_step(kind, i, 4 + at % 2)
            if at > 0:
                finish_far(at - 1)
                send_result(at - 1, o_stage, o_ref, o_send, o_recv)

        @pl.loop(0, 4)
        def _(step):
            grad_step(0, 3 - step, 3 - step)
            pl.when(step == 0)(lambda: finish_far(4))
            pl.when(step == 1)(lambda: finish_sum(3, 3))

        for u in range(4):
            rows = slice(u * TILE, (u + 1) * TILE)
            q = q_raw[rows].astype(jnp.float32)
            inverse = lax.rsqrt(jnp.mean(q * q, axis=-1, keepdims=True) + EPSILON)
            unit = q * inverse
            grad_in = dq_acc[rows] * (over[rows] * SCALE)
            dq = inverse * (grad_in - unit * jnp.mean(grad_in * unit, axis=-1, keepdims=True))
            dq_stage[u] = dq.astype(LOW)
        @pl.loop(0, 4)
        def _(u):
            send_result(u, dq_stage, dq_ref, dq_send, dq_recv)

        for i in (2, 1, 0):
            finish_sum(i, i)

    arrived(dkv_ref, dkv_recv)
    arrived(o_ref, o_recv)
    arrived(dq_ref, dq_recv)

    def left(ref, sem, kept, own):
        pl.when(kept)(lambda: arrived(ref.at[pl.ds(0, own)], sem))
        pl.when(jnp.logical_not(kept))(lambda: arrived(ref, sem))

    left(kv_stage, kv_send, active, HEADS - 1)
    for held, sem in ((q_in, q_send), (g_in, g_send)):
        kept = active & (h == core)
        pl.when(kept)(lambda: arrived(held.at[:, 0 : (HEADS - 1) * HD], sem))
        pl.when(jnp.logical_not(kept))(lambda: arrived(held, sem))

    @pl.when(active)
    def _():
        arrived(sib_send, relay_send)
        arrived(sib_send.at[pl.ds(0, 3)], time_send)
        arrived(sib_send.at[pl.ds(0, 2)], wide_send)
        arrived(sib_send, sib_sent)
        arrived(sib_send.at[pl.ds(0, SLOTS - 1)], sum_send)
        arrived(sib_send.at[0, pl.ds(0, 3 * QUARTER)], sum_send)
        for stage, sem in ((o_stage, o_send), (dq_stage, dq_send)):
            arrived(stage.at[pl.ds(0, 3)], sem)
            arrived(stage.at[3, pl.ds(0, 3 * QUARTER)], sem)
            pl.when(h != core)(lambda: arrived(stage.at[3, quarter(3)], sem))


def finish_kernel(o_in, dq_in, dkv_in, k_in, o_ref, dq_ref, dk_ref, dv_ref, o, dq, dkv, k_raw, dk, dv, in_sem, out_sem):
    parts = 3
    heads = HEADS // parts

    def lanes_in(p):
        return slice(p * heads * HD, (p + 1) * heads * HD)

    loads = [(o_in, o), (dq_in, dq)]
    for p in range(parts):
        loads.append((dkv_in.at[p * heads : (p + 1) * heads], dkv.at[p * heads : (p + 1) * heads]))
        loads.append((k_in.at[:, lanes_in(p)], k_raw.at[:, lanes_in(p)]))
    loads = [pltpu.make_async_copy(a, b, in_sem.at[i]) for i, (a, b) in enumerate(loads)]
    stores = [(o, o_ref), (dq, dq_ref)]
    for p in range(parts):
        stores.append((dk.at[:, lanes_in(p)], dk_ref.at[:, lanes_in(p)]))
        stores.append((dv.at[:, lanes_in(p)], dv_ref.at[:, lanes_in(p)]))
    stores = [pltpu.make_async_copy(a, b, out_sem.at[i]) for i, (a, b) in enumerate(stores)]
    for load in loads:
        load.start()
    for i in range(2):
        loads[i].wait()
        stores[i].start()
    for p in range(parts):
        loads[2 + 2 * p].wait()
        loads[3 + 2 * p].wait()
        for n in range(p * heads, (p + 1) * heads):
            lanes = slice(n * HD, (n + 1) * HD)
            k = k_raw[:, lanes].astype(jnp.float32)
            inverse = lax.rsqrt(jnp.mean(k * k, axis=-1, keepdims=True) + EPSILON)
            unit = k * inverse
            grad_in = dkv[n, :, 0:HD].astype(jnp.float32)
            grad = inverse * (grad_in - unit * jnp.mean(grad_in * unit, axis=-1, keepdims=True))
            dk[:, lanes] = grad.astype(LOW)
            dv[:, lanes] = dkv[n, :, HD:]
        stores[2 + 2 * p].start()
        stores[3 + 2 * p].start()
    for store in stores:
        store.wait()


def shards(queries, keys, values, out_grad, window):
    hbm = pl.BlockSpec(memory_space=pl.ANY)
    dma = pltpu.SemaphoreType.DMA
    f32 = jnp.float32
    rows = jax.ShapeDtypeStruct((QUARTER, HEADS * HD), LOW)
    o, dq, dkv = pl.pallas_call(
        attend_kernel,
        out_shape=(rows, rows, jax.ShapeDtypeStruct((HEADS, QUARTER, 2 * HD), LOW)),
        in_specs=[hbm] * 5,
        out_specs=(hbm,) * 3,
        scratch_shapes=[
            pltpu.SMEM(window.shape, window.dtype),
            pltpu.VMEM((QUARTER, HEADS * HD), LOW),
            pltpu.VMEM((QUARTER, HEADS * HD), LOW),
            pltpu.VMEM((QUARTER, HEADS * HD), LOW),
            pltpu.VMEM((QUARTER, HEADS * HD), LOW),
            pltpu.VMEM((HEADS, QUARTER, 2 * HD), LOW),
            pltpu.VMEM((SLOTS, PAIR, 2 * HD), LOW),
            pltpu.VMEM((4 * TILE, HD), LOW),
            pltpu.VMEM((4 * TILE, HD), LOW),
            pltpu.VMEM((4, 4 * TILE, PAIR), LOW),
            pltpu.VMEM((2, 2 * TILE, PAIR), LOW),
            pltpu.VMEM((2, 2 * TILE, PAIR), LOW),
            pltpu.VMEM((1, TILE, PAIR), LOW),
            pltpu.VMEM((4 * TILE, 2 * HD), f32),
            pltpu.VMEM((4 * TILE, HD), f32),
            pltpu.VMEM((4 * TILE, HD), f32),
            pltpu.VMEM((4 * TILE, HD), f32),
            pltpu.VMEM((2 * HD, 4 * TILE), LOW),
            pltpu.VMEM((4 * TILE, HD), LOW),
            pltpu.VMEM((4, TILE, HD), LOW),
            pltpu.VMEM((4, TILE, HD), LOW),
            pltpu.VMEM((6, PAIR, 2 * HD), f32),
            pltpu.VMEM((SLOTS, TILE, 2 * HD), LOW),
            pltpu.VMEM((SLOTS, TILE, 2 * HD), LOW),
            pltpu.VMEM((SLOTS, TILE, 2 * HD), LOW),
            pltpu.VMEM((6, TILE, 2 * HD), LOW),
            dma((5,)),
            pltpu.SemaphoreType.DMA,
            pltpu.SemaphoreType.DMA,
            pltpu.SemaphoreType.DMA,
            dma((SLOTS, 2)),
            pltpu.SemaphoreType.DMA,
            pltpu.SemaphoreType.DMA,
            pltpu.SemaphoreType.DMA,
            pltpu.SemaphoreType.DMA,
            pltpu.SemaphoreType.DMA,
            pltpu.SemaphoreType.DMA,
            dma((SLOTS,)),
            dma((5,)),
            pltpu.SemaphoreType.DMA,
            pltpu.SemaphoreType.DMA,
            pltpu.SemaphoreType.DMA,
            pltpu.SemaphoreType.DMA,
            pltpu.SemaphoreType.DMA,
            pltpu.SemaphoreType.DMA,
        ],
        compiler_params=pltpu.CompilerParams(collective_id=0, has_side_effects=True, vmem_limit_bytes=VMEM_LIMIT),
        name="attend",
    )(window, queries, keys, values, out_grad)

    return pl.pallas_call(
        finish_kernel,
        out_shape=(rows,) * 4,
        in_specs=[hbm] * 4,
        out_specs=(hbm,) * 4,
        scratch_shapes=[
            pltpu.VMEM((QUARTER, HEADS * HD), LOW),
            pltpu.VMEM((QUARTER, HEADS * HD), LOW),
            pltpu.VMEM((HEADS, QUARTER, 2 * HD), LOW),
            pltpu.VMEM((QUARTER, HEADS * HD), LOW),
            pltpu.VMEM((QUARTER, HEADS * HD), LOW),
            pltpu.VMEM((QUARTER, HEADS * HD), LOW),
            dma((8,)),
            dma((8,)),
        ],
        compiler_params=pltpu.CompilerParams(vmem_limit_bytes=VMEM_LIMIT),
        name="finish",
    )(o, dq, dkv, keys)


def solution(mesh):
    rows = P(("tm", "head"), None)
    return jax.shard_map(
        shards, mesh=mesh, in_specs=(rows, rows, rows, rows, P()), out_specs=(rows, rows, rows, rows), check_vma=False
    )
```

```python
import jax
import jax.numpy as jnp
from jax import lax
from jax.experimental import pallas as pl
from jax.experimental.pallas import tpu as pltpu
from jax.sharding import PartitionSpec as P

TILE = 384
HEADS = 12
HD = 128
QUARTER = 96
PAIR = 768
SLOTS = 9
EPSILON = 1e-06
SCALE = HD**-0.5
LOG2E = 1.4426950408889634
MESH = pl.DeviceIdType.MESH
VMEM_LIMIT = 60 * 1024 * 1024
LOW = jnp.bfloat16

QUERY_AT = ((0, 1), (0, 0), (1, 0), (1, 1))
KINDS = ((0, 4, 0, 4), (4, 2, 0, 2), (6, 2, 1, 2), (8, 1, 1, 1))
FAR = ((3, 0), (2, 1), (1, 1), (2, 0), (1, 0))


def worker_of(n, T, W, core):
    y = n % 4
    spot = (n // 4 + y + 1) % 4
    x, z = absolute(T, spot // 2), 2 * (spot % 2) + W
    return x * 8 + z * 2 + y // 2, (y % 2) * 2 + core


def work_here(tm, part):
    x, y, z = tm // 8, tm % 2 * 2 + part // 2, tm // 2 % 4
    T, W = x // 2, z % 2
    row = (relative(T, x) * 2 + z // 2 + 7 - y) % 4
    return row < 3, jnp.where(row < 3, row * 4 + y, 0), T, W, part % 2


def absolute(half, near):
    return 1 + half + near * (2 * half - 1)


def relative(half, index):
    return (index - 1 - half) * (2 * half - 1)


def pair_at(kind, i):
    if kind == 0:
        return i // 2, i % 2
    if kind == 1:
        return -1, i
    if kind == 2:
        return i, -1
    return -1, -1


def query_number(near_t, near_w):
    return jnp.where(near_t == 0, 1 - near_w, 2 + near_w)


def copy_to(src, dst, send_sem, recv_sem, device, here):
    same = (device[0] == here[0]) & (device[1] == here[1])

    @pl.when(same)
    def _():
        pltpu.make_async_copy(src, dst, recv_sem).start()

    @pl.when(jnp.logical_not(same))
    def _():
        pltpu.make_async_remote_copy(
            src_ref=src, dst_ref=dst, send_sem=send_sem, recv_sem=recv_sem, device_id=device, device_id_type=MESH
        ).start()


def arrived(ref, sem):
    pltpu.make_async_copy(ref, ref, sem).wait()


def nt(a, b):
    return lax.dot_general(a, b, (((1,), (1,)), ((), ())), preferred_element_type=jnp.float32)


def quarter(j):
    return pl.ds(pl.multiple_of(j * QUARTER, QUARTER), QUARTER)


def half(core):
    return pl.ds(pl.multiple_of(core * TILE, TILE), TILE)


def lanes_of(n):
    return pl.ds(pl.multiple_of(n * HD, HD), HD)


def repeated(value):
    return jnp.concatenate([value] * (PAIR // HD), axis=1)


def attend_kernel(
    window_hbm,
    q_hbm,
    k_hbm,
    v_hbm,
    g_hbm,
    o_ref,
    dq_ref,
    dkv_ref,
    window_ref,
    q_in,
    k_in,
    v_in,
    g_in,
    kv_stage,
    kv,
    q_raw,
    q_unit,
    weights0,
    weights1,
    weights2,
    weights3,
    acc,
    dq_acc,
    over,
    row_dot,
    scaled,
    grad_rows,
    o_stage,
    dq_stage,
    part_sum,
    sib_send,
    sib_recv,
    sum_stage,
    near_recv,
    in_sem,
    kv_send,
    q_send,
    g_send,
    kv_recv,
    q_recv,
    g_recv,
    relay_send,
    time_send,
    wide_send,
    sib_sent,
    sib_got,
    near_got,
    o_send,
    dq_send,
    sum_send,
    o_recv,
    dq_recv,
    dkv_recv,
):
    tm, part = lax.axis_index("tm"), lax.axis_index("head")
    here = (tm, part)
    t, h, w = tm // 8, tm // 4 % 2, tm % 4
    active, head, T, W, core = work_here(tm, part)
    home_t, home_w = t // 2, w // 2
    own_t, own_w = relative(home_t, t), relative(home_w, w)
    sibling = (tm, part + 1 - 2 * core)
    time_near = worker_of(head, 1 - T, W, core)
    wide_near = worker_of(head, T, 1 - W, core)
    weights = (weights0, weights1, weights2, weights3)

    def copy_in(i):
        source = (k_hbm, v_hbm, q_hbm, g_hbm, window_hbm)[i]
        return pltpu.make_async_copy(source, (k_in, v_in, q_in, g_in, window_ref)[i], in_sem.at[i])

    for i in range(5):
        copy_in(i).start()

    def tile_of(near_t, kh, near_w):
        return absolute(T, near_t) * 8 + kh * 4 + absolute(W, near_w)

    barrier = pltpu.get_barrier_semaphore()

    def greet(device, count):
        other = jnp.logical_not((device[0] == tm) & (device[1] == part))

        @pl.when(other)
        def _():
            pl.semaphore_signal(barrier, inc=1, device_id=device, device_id_type=MESH)

        return count + other.astype(jnp.int32)

    def greet_workers(n, count):
        count = greet(worker_of(n, home_t, home_w, core), count)
        return lax.cond(h != core, lambda c: greet(worker_of(n, home_t, home_w, h), c), lambda c: c, count)

    greeted = lax.fori_loop(0, HEADS, greet_workers, jnp.int32(0), unroll=True)

    def greet_owners(i, count):
        near_t, kh, near_w = i // 4, i % 2, i // 2 % 2
        owner = tile_of(near_t, kh, near_w)
        for y in range(2):
            count = greet((owner, 2 * y + core), count)

        def others(count):
            for y in range(2):
                count = greet((owner, 2 * y + 1 - core), count)
            return count

        return lax.cond(kh == core, others, lambda count: count, count)

    def greet_all(count):
        count = lax.fori_loop(0, 8, greet_owners, count, unroll=True)
        for device in (sibling, time_near, wide_near):
            count = greet(device, count)
        return count

    greeted = lax.cond(active, greet_all, lambda count: count, greeted)

    copy_in(0).wait()
    copy_in(1).wait()

    @pl.loop(0, HEADS)
    def _(n):
        lanes = lanes_of(n)
        k = k_in[:, lanes].astype(jnp.float32)
        inverse = lax.rsqrt(jnp.mean(k * k, axis=-1, keepdims=True) + EPSILON)
        kv_stage[n, :, 0:HD] = (k * inverse).astype(LOW)
        kv_stage[n, :, HD:] = v_in[:, lanes]

    pl.semaphore_wait(barrier, greeted)

    def send_keys():
        slot = own_t * 2 + own_w
        rows = pl.ds(pl.multiple_of(core * TILE + h * 2 * QUARTER + part // 2 * QUARTER, QUARTER), QUARTER)

        @pl.loop(0, HEADS, unroll=True)
        def _(n):
            copy_to(
                kv_stage.at[n],
                kv.at[slot, rows],
                kv_send,
                kv_recv.at[slot, core],
                worker_of(n, home_t, home_w, core),
                here,
            )

    def send_rows(held, to, send_sem, recv_sem):
        row = query_number(own_t, own_w) * TILE + part * QUARTER

        @pl.loop(0, HEADS, unroll=True)
        def _(n):
            copy_to(
                held.at[:, lanes_of(n)],
                to.at[pl.ds(pl.multiple_of(row, QUARTER), QUARTER)],
                send_sem,
                recv_sem,
                worker_of(n, home_t, home_w, h),
                here,
            )

    copy_in(2).wait()
    send_rows(q_in, q_raw, q_send, q_recv)
    send_keys()
    copy_in(3).wait()
    copy_in(4).wait()

    def send_grads():
        send_rows(g_in, grad_rows, g_send, g_recv)

    @pl.when(jnp.logical_not(active))
    def _():
        arrived(kv_stage, kv_send)
        send_grads()


    def pass_on(kind, i):
        slot = KINDS[kind][0] + i
        near_t, near_w = pair_at(kind, i)
        arrived(kv.at[slot, half(core)], kv_recv.at[slot, core])

        def send(device, to, sem):
            pltpu.make_async_remote_copy(
                src_ref=kv.at[slot, half(core)],
                dst_ref=kv.at[to, half(core)],
                send_sem=sem,
                recv_sem=kv_recv.at[to, core],
                device_id=device,
                device_id_type=MESH,
            ).start()

        if kind == 0:
            pl.when(near_w == 0)(lambda: send(wide_near, 6 + near_t, wide_send))
        if kind in (0, 2):
            to = 4 + near_w if kind == 0 else 8
            pl.when(near_t == 0)(lambda: send(time_near, to, time_send))
        send(sibling, slot, relay_send)

    def relayed(slot):
        arrived(kv.at[slot, half(1 - core)], kv_recv.at[slot, 1 - core])

    def score_step(kind, i):
        first, count, q0, qn = KINDS[kind]
        slot = first + i
        near_t, near_w = pair_at(kind, i)
        relayed(slot)
        scores = nt(q_unit[q0 * TILE : (q0 + qn) * TILE], kv[slot, :, 0:HD])
        column = lax.broadcasted_iota(jnp.int32, (1, PAIR), 1)
        lower = (column < PAIR // 4) | ((column >= PAIR // 2) & (column < 3 * PAIR // 4))
        lows = []
        for u in range(qn):
            qt, qw = QUERY_AT[q0 + u]
            dt = absolute(T, near_t) - absolute(T, qt)
            dw = absolute(W, near_w) - absolute(W, qw)
            tile = tile_of(qt, core, qw)
            live = [window_ref[tile, 9 * (dt + 1) + 3 * (kh - core + 1) + dw + 1] for kh in range(2)]
            bias = [(one.astype(jnp.float32) - 1.0) * 1e30 for one in live]
            weight = jnp.exp2(scores[u * TILE : (u + 1) * TILE] * (SCALE * LOG2E) + jnp.where(lower, bias[0], bias[1]))
            rows = slice((q0 + u) * TILE, (q0 + u + 1) * TILE)
            total = weight[:, 0:HD]
            for at in range(HD, PAIR, HD):
                total += weight[:, at : at + HD]
            acc[rows, HD:] += total
            lows.append(weight.astype(LOW))
        low = jnp.concatenate(lows, axis=0) if qn > 1 else lows[0]
        weights[kind][i] = low
        acc[q0 * TILE : (q0 + qn) * TILE, 0:HD] += jnp.dot(low, kv[slot, :, HD:], preferred_element_type=jnp.float32)

    def to_sibling(slot):
        return pltpu.make_async_remote_copy(
            src_ref=sib_send.at[slot],
            dst_ref=sib_recv.at[slot],
            send_sem=sib_sent,
            recv_sem=sib_got.at[slot],
            device_id=sibling,
            device_id_type=MESH,
        )

    def send_sum(slot):
        @pl.when(slot < 4)
        def _():
            near_t, near_w = pair_at(0, slot)
            for kh in range(2):
                for y in range(2):
                    copy_to(
                        sum_stage.at[slot, quarter(kh * 2 + y)],
                        dkv_ref.at[head],
                        sum_send,
                        dkv_recv,
                        (tile_of(near_t, kh, near_w), 2 * y + core),
                        here,
                    )

        def pass_back(device):
            pltpu.make_async_remote_copy(
                src_ref=sum_stage.at[slot],
                dst_ref=near_recv.at[slot - 4],
                send_sem=sum_send,
                recv_sem=near_got.at[slot - 4],
                device_id=device,
                device_id_type=MESH,
            ).start()

        wide = (slot == 6) | (slot == 7)
        pl.when(wide)(lambda: pass_back(wide_near))
        pl.when((slot >= 4) & jnp.logical_not(wide))(lambda: pass_back(time_near))

    def finish_sum(slot, held):
        slot = jnp.int32(slot)
        near_t, near_w = pair_at(0, slot)
        own = slot < 4
        time_at = jnp.where(own & (near_t == 0), near_w, 5)
        wide_at = jnp.where(slot == 6, 4, jnp.where(own & (near_w == 0), 2 + near_t, 5))
        to_sibling(slot).wait_recv()
        for at in (time_at, wide_at):
            pl.when(at < 5)(lambda at=at: arrived(near_recv.at[at], near_got.at[at]))
        total = part_sum[held, half(core)] + sib_recv[slot].astype(jnp.float32)
        for at in (time_at, wide_at):
            total += near_recv[at].astype(jnp.float32)
        sum_stage[slot] = total.astype(LOW)
        send_sum(slot)

    def grad_step(kind, i, held):
        first, count, q0, qn = KINDS[kind]
        slot = first + i
        rows = slice(q0 * TILE, (q0 + qn) * TILE)
        low = weights[kind][i]
        prob_grad = nt(grad_rows[rows], kv[slot, :, HD:])
        score_grad = (low.astype(jnp.float32) * (prob_grad - repeated(row_dot[rows]))).astype(LOW)
        dq_acc[rows] += jnp.dot(score_grad, kv[slot, :, 0:HD], preferred_element_type=jnp.float32)
        part_sum[held, :, 0:HD] = jnp.dot(scaled[0:HD, rows], score_grad, preferred_element_type=jnp.float32).T
        part_sum[held, :, HD:] = jnp.dot(scaled[HD:, rows], low, preferred_element_type=jnp.float32).T
        sib_send[slot] = part_sum[held, half(1 - core)].astype(LOW)
        to_sibling(slot).start()

    def send_result(u, stage, dst, send_sem, recv_sem):
        near_t, near_w = u // 2, jnp.where((u == 1) | (u == 2), 0, 1)
        for j in range(4):
            copy_to(
                stage.at[u, quarter(j)],
                dst.at[:, lanes_of(head)],
                send_sem,
                recv_sem,
                (tile_of(near_t, core, near_w), j),
                here,
            )

    @pl.when(active)
    def _():
        acc[...] = jnp.zeros_like(acc)
        dq_acc[...] = jnp.zeros_like(dq_acc)
        near_recv[5] = jnp.zeros((TILE, 2 * HD), LOW)

        pass_on(0, 0)
        pass_on(0, 1)
        pass_on(2, 0)
        send_grads()
        arrived(q_raw, q_recv)
        for u in range(4):
            rows = slice(u * TILE, (u + 1) * TILE)
            q = q_raw[rows].astype(jnp.float32)
            inverse = lax.rsqrt(jnp.mean(q * q, axis=-1, keepdims=True) + EPSILON)
            q_unit[rows] = (q * inverse).astype(LOW)

        @pl.loop(0, 4)
        def _(i):
            score_step(0, i)
            pl.when(i < 2)(lambda: pass_on(0, i + 2))
            pl.when(i >= 2)(lambda: pass_on(1, i - 2))

        score_step(2, 0)
        pass_on(2, 1)

        @pl.loop(0, 2)
        def _(i):
            score_step(1, i)

        pass_on(3, 0)
        score_step(2, 1)
        score_step(3, 0)
        arrived(grad_rows, g_recv)

        for u in range(4):
            rows = slice(u * TILE, (u + 1) * TILE)
            over[rows] = jnp.broadcast_to(1.0 / jnp.sum(acc[rows, HD:], axis=-1, keepdims=True), (TILE, HD))
            out = (acc[rows, 0:HD] * over[rows]).astype(LOW)
            o_stage[u] = out
            grad = grad_rows[rows].astype(jnp.float32)
            dot = jnp.sum(grad * out.astype(jnp.float32), axis=-1, keepdims=True)
            row_dot[rows] = jnp.broadcast_to(dot, (TILE, HD))
            scaled[0:HD, rows] = (q_unit[rows].astype(jnp.float32) * (over[rows] * SCALE)).T.astype(LOW)
            scaled[HD:, rows] = (grad * over[rows]).T.astype(LOW)

        def finish_far(at):
            kind, i = FAR[at]
            finish_sum(KINDS[kind][0] + i, 4 + at % 2)

        for at, (kind, i) in enumerate(FAR):
            grad_step(kind, i, 4 + at % 2)
            if at > 0:
                finish_far(at - 1)
                send_result(at - 1, o_stage, o_ref, o_send, o_recv)

        @pl.loop(0, 4)
        def _(step):
            grad_step(0, 3 - step, 3 - step)
            pl.when(step == 0)(lambda: finish_far(4))
            pl.when(step == 1)(lambda: finish_sum(3, 3))

        for u in range(4):
            rows = slice(u * TILE, (u + 1) * TILE)
            q = q_raw[rows].astype(jnp.float32)
            inverse = lax.rsqrt(jnp.mean(q * q, axis=-1, keepdims=True) + EPSILON)
            unit = q * inverse
            grad_in = dq_acc[rows] * (over[rows] * SCALE)
            dq = inverse * (grad_in - unit * jnp.mean(grad_in * unit, axis=-1, keepdims=True))
            dq_stage[u] = dq.astype(LOW)
            send_result(u, dq_stage, dq_ref, dq_send, dq_recv)

        for i in (2, 1, 0):
            finish_sum(i, i)

    arrived(dkv_ref, dkv_recv)
    arrived(o_ref, o_recv)
    arrived(dq_ref, dq_recv)

    pl.when(active)(lambda: arrived(kv_stage.at[pl.ds(0, HEADS - 1)], kv_send))
    for held, sem in ((q_in, q_send), (g_in, g_send)):
        kept = active & (h == core)
        pl.when(kept)(lambda: arrived(held.at[:, 0 : (HEADS - 1) * HD], sem))
        pl.when(jnp.logical_not(kept))(lambda: arrived(held, sem))

    @pl.when(active)
    def _():
        arrived(sib_send, relay_send)
        arrived(sib_send.at[pl.ds(0, 3)], time_send)
        arrived(sib_send.at[pl.ds(0, 2)], wide_send)
        arrived(sib_send, sib_sent)
        arrived(sib_send.at[pl.ds(0, SLOTS - 1)], sum_send)
        arrived(sib_send.at[0, pl.ds(0, 3 * QUARTER)], sum_send)
        for stage, sem in ((o_stage, o_send), (dq_stage, dq_send)):
            arrived(stage.at[pl.ds(0, 3)], sem)
            arrived(stage.at[3, pl.ds(0, 3 * QUARTER)], sem)
            pl.when(h != core)(lambda: arrived(stage.at[3, quarter(3)], sem))


def finish_kernel(o_in, dq_in, dkv_in, k_in, o_ref, dq_ref, dk_ref, dv_ref, o, dq, dkv, k_raw, dk, dv, in_sem, out_sem):
    parts = 3
    heads = HEADS // parts

    def lanes_in(p):
        return slice(p * heads * HD, (p + 1) * heads * HD)

    loads = [(o_in, o), (dq_in, dq)]
    for p in range(parts):
        loads.append((dkv_in.at[p * heads : (p + 1) * heads], dkv.at[p * heads : (p + 1) * heads]))
        loads.append((k_in.at[:, lanes_in(p)], k_raw.at[:, lanes_in(p)]))
    loads = [pltpu.make_async_copy(a, b, in_sem.at[i]) for i, (a, b) in enumerate(loads)]
    stores = [(o, o_ref), (dq, dq_ref)]
    for p in range(parts):
        stores.append((dk.at[:, lanes_in(p)], dk_ref.at[:, lanes_in(p)]))
        stores.append((dv.at[:, lanes_in(p)], dv_ref.at[:, lanes_in(p)]))
    stores = [pltpu.make_async_copy(a, b, out_sem.at[i]) for i, (a, b) in enumerate(stores)]
    for load in loads:
        load.start()
    for i in range(2):
        loads[i].wait()
        stores[i].start()
    for p in range(parts):
        loads[2 + 2 * p].wait()
        loads[3 + 2 * p].wait()
        for n in range(p * heads, (p + 1) * heads):
            lanes = slice(n * HD, (n + 1) * HD)
            k = k_raw[:, lanes].astype(jnp.float32)
            inverse = lax.rsqrt(jnp.mean(k * k, axis=-1, keepdims=True) + EPSILON)
            unit = k * inverse
            grad_in = dkv[n, :, 0:HD].astype(jnp.float32)
            grad = inverse * (grad_in - unit * jnp.mean(grad_in * unit, axis=-1, keepdims=True))
            dk[:, lanes] = grad.astype(LOW)
            dv[:, lanes] = dkv[n, :, HD:]
        stores[2 + 2 * p].start()
        stores[3 + 2 * p].start()
    for store in stores:
        store.wait()


def shards(queries, keys, values, out_grad, window):
    hbm = pl.BlockSpec(memory_space=pl.ANY)
    dma = pltpu.SemaphoreType.DMA
    f32 = jnp.float32
    rows = jax.ShapeDtypeStruct((QUARTER, HEADS * HD), LOW)
    o, dq, dkv = pl.pallas_call(
        attend_kernel,
        out_shape=(rows, rows, jax.ShapeDtypeStruct((HEADS, QUARTER, 2 * HD), LOW)),
        in_specs=[hbm] * 5,
        out_specs=(hbm,) * 3,
        scratch_shapes=[
            pltpu.SMEM(window.shape, window.dtype),
            pltpu.VMEM((QUARTER, HEADS * HD), LOW),
            pltpu.VMEM((QUARTER, HEADS * HD), LOW),
            pltpu.VMEM((QUARTER, HEADS * HD), LOW),
            pltpu.VMEM((QUARTER, HEADS * HD), LOW),
            pltpu.VMEM((HEADS, QUARTER, 2 * HD), LOW),
            pltpu.VMEM((SLOTS, PAIR, 2 * HD), LOW),
            pltpu.VMEM((4 * TILE, HD), LOW),
            pltpu.VMEM((4 * TILE, HD), LOW),
            pltpu.VMEM((4, 4 * TILE, PAIR), LOW),
            pltpu.VMEM((2, 2 * TILE, PAIR), LOW),
            pltpu.VMEM((2, 2 * TILE, PAIR), LOW),
            pltpu.VMEM((1, TILE, PAIR), LOW),
            pltpu.VMEM((4 * TILE, 2 * HD), f32),
            pltpu.VMEM((4 * TILE, HD), f32),
            pltpu.VMEM((4 * TILE, HD), f32),
            pltpu.VMEM((4 * TILE, HD), f32),
            pltpu.VMEM((2 * HD, 4 * TILE), LOW),
            pltpu.VMEM((4 * TILE, HD), LOW),
            pltpu.VMEM((4, TILE, HD), LOW),
            pltpu.VMEM((4, TILE, HD), LOW),
            pltpu.VMEM((6, PAIR, 2 * HD), f32),
            pltpu.VMEM((SLOTS, TILE, 2 * HD), LOW),
            pltpu.VMEM((SLOTS, TILE, 2 * HD), LOW),
            pltpu.VMEM((SLOTS, TILE, 2 * HD), LOW),
            pltpu.VMEM((6, TILE, 2 * HD), LOW),
            dma((5,)),
            pltpu.SemaphoreType.DMA,
            pltpu.SemaphoreType.DMA,
            pltpu.SemaphoreType.DMA,
            dma((SLOTS, 2)),
            pltpu.SemaphoreType.DMA,
            pltpu.SemaphoreType.DMA,
            pltpu.SemaphoreType.DMA,
            pltpu.SemaphoreType.DMA,
            pltpu.SemaphoreType.DMA,
            pltpu.SemaphoreType.DMA,
            dma((SLOTS,)),
            dma((5,)),
            pltpu.SemaphoreType.DMA,
            pltpu.SemaphoreType.DMA,
            pltpu.SemaphoreType.DMA,
            pltpu.SemaphoreType.DMA,
            pltpu.SemaphoreType.DMA,
            pltpu.SemaphoreType.DMA,
        ],
        compiler_params=pltpu.CompilerParams(collective_id=0, has_side_effects=True, vmem_limit_bytes=VMEM_LIMIT),
        name="attend",
    )(window, queries, keys, values, out_grad)

    return pl.pallas_call(
        finish_kernel,
        out_shape=(rows,) * 4,
        in_specs=[hbm] * 4,
        out_specs=(hbm,) * 4,
        scratch_shapes=[
            pltpu.VMEM((QUARTER, HEADS * HD), LOW),
            pltpu.VMEM((QUARTER, HEADS * HD), LOW),
            pltpu.VMEM((HEADS, QUARTER, 2 * HD), LOW),
            pltpu.VMEM((QUARTER, HEADS * HD), LOW),
            pltpu.VMEM((QUARTER, HEADS * HD), LOW),
            pltpu.VMEM((QUARTER, HEADS * HD), LOW),
            dma((8,)),
            dma((8,)),
        ],
        compiler_params=pltpu.CompilerParams(vmem_limit_bytes=VMEM_LIMIT),
        name="finish",
    )(o, dq, dkv, keys)


def solution(mesh):
    rows = P(("tm", "head"), None)
    return jax.shard_map(
        shards, mesh=mesh, in_specs=(rows, rows, rows, rows, P()), out_specs=(rows, rows, rows, rows), check_vma=False
    )
```

```python
import jax
import jax.numpy as jnp
from jax import lax
from jax.experimental import pallas as pl
from jax.experimental.pallas import tpu as pltpu
from jax.sharding import PartitionSpec as P

TILE = 384
HEADS = 12
HD = 128
QUARTER = 96
PAIR = 768
SLOTS = 9
EPSILON = 1e-06
SCALE = HD**-0.5
LOG2E = 1.4426950408889634
MESH = pl.DeviceIdType.MESH
VMEM_LIMIT = 60 * 1024 * 1024
LOW = jnp.bfloat16

QUERY_AT = ((0, 1), (0, 0), (1, 0), (1, 1))
KINDS = ((0, 4, 0, 4), (4, 2, 0, 2), (6, 2, 1, 2), (8, 1, 1, 1))
FAR = ((3, 0), (2, 1), (1, 1), (1, 0), (2, 0))


def worker_of(n, T, W, core):
    y = n % 4
    spot = (n // 4 + y + 1) % 4
    x, z = absolute(T, spot // 2), 2 * (spot % 2) + W
    return x * 8 + z * 2 + y // 2, (y % 2) * 2 + core


def work_here(tm, part):
    x, y, z = tm // 8, tm % 2 * 2 + part // 2, tm // 2 % 4
    T, W = x // 2, z % 2
    row = (relative(T, x) * 2 + z // 2 + 7 - y) % 4
    return row < 3, jnp.where(row < 3, row * 4 + y, 0), T, W, part % 2


def absolute(half, near):
    return 1 + half + near * (2 * half - 1)


def relative(half, index):
    return (index - 1 - half) * (2 * half - 1)


def pair_at(kind, i):
    if kind == 0:
        return i // 2, i % 2
    if kind == 1:
        return -1, i
    if kind == 2:
        return i, -1
    return -1, -1


def query_number(near_t, near_w):
    return jnp.where(near_t == 0, 1 - near_w, 2 + near_w)


def copy_to(src, dst, send_sem, recv_sem, device, here):
    same = (device[0] == here[0]) & (device[1] == here[1])

    @pl.when(same)
    def _():
        pltpu.make_async_copy(src, dst, recv_sem).start()

    @pl.when(jnp.logical_not(same))
    def _():
        pltpu.make_async_remote_copy(
            src_ref=src, dst_ref=dst, send_sem=send_sem, recv_sem=recv_sem, device_id=device, device_id_type=MESH
        ).start()


def arrived(ref, sem):
    pltpu.make_async_copy(ref, ref, sem).wait()


def nt(a, b):
    return lax.dot_general(a, b, (((1,), (1,)), ((), ())), preferred_element_type=jnp.float32)


def quarter(j):
    return pl.ds(pl.multiple_of(j * QUARTER, QUARTER), QUARTER)


def half(core):
    return pl.ds(pl.multiple_of(core * TILE, TILE), TILE)


def lanes_of(n):
    return pl.ds(pl.multiple_of(n * HD, HD), HD)


def repeated(value):
    return jnp.concatenate([value] * (PAIR // HD), axis=1)


def attend_kernel(
    window_hbm,
    q_hbm,
    k_hbm,
    v_hbm,
    g_hbm,
    o_ref,
    dq_ref,
    dkv_ref,
    window_ref,
    q_in,
    k_in,
    v_in,
    g_in,
    kv_stage,
    kv,
    q_raw,
    q_unit,
    weights0,
    weights1,
    weights2,
    weights3,
    acc,
    dq_acc,
    over,
    row_dot,
    scaled,
    grad_rows,
    o_stage,
    dq_stage,
    part_sum,
    sib_send,
    sib_recv,
    sum_stage,
    near_recv,
    in_sem,
    kv_send,
    q_send,
    g_send,
    kv_recv,
    q_recv,
    g_recv,
    relay_send,
    time_send,
    wide_send,
    sib_sent,
    sib_got,
    near_got,
    o_send,
    dq_send,
    sum_send,
    o_recv,
    dq_recv,
    dkv_recv,
):
    tm, part = lax.axis_index("tm"), lax.axis_index("head")
    here = (tm, part)
    t, h, w = tm // 8, tm // 4 % 2, tm % 4
    active, head, T, W, core = work_here(tm, part)
    home_t, home_w = t // 2, w // 2
    own_t, own_w = relative(home_t, t), relative(home_w, w)
    sibling = (tm, part + 1 - 2 * core)
    time_near = worker_of(head, 1 - T, W, core)
    wide_near = worker_of(head, T, 1 - W, core)
    weights = (weights0, weights1, weights2, weights3)

    def copy_in(i):
        source = (k_hbm, v_hbm, q_hbm, g_hbm, window_hbm)[i]
        return pltpu.make_async_copy(source, (k_in, v_in, q_in, g_in, window_ref)[i], in_sem.at[i])

    for i in range(5):
        copy_in(i).start()

    def tile_of(near_t, kh, near_w):
        return absolute(T, near_t) * 8 + kh * 4 + absolute(W, near_w)

    barrier = pltpu.get_barrier_semaphore()

    def greet(device, count):
        other = jnp.logical_not((device[0] == tm) & (device[1] == part))

        @pl.when(other)
        def _():
            pl.semaphore_signal(barrier, inc=1, device_id=device, device_id_type=MESH)

        return count + other.astype(jnp.int32)

    def greet_workers(n, count):
        count = greet(worker_of(n, home_t, home_w, core), count)
        return lax.cond(h != core, lambda c: greet(worker_of(n, home_t, home_w, h), c), lambda c: c, count)

    greeted = lax.fori_loop(0, HEADS, greet_workers, jnp.int32(0), unroll=True)

    def greet_owners(i, count):
        near_t, kh, near_w = i // 4, i % 2, i // 2 % 2
        owner = tile_of(near_t, kh, near_w)
        for y in range(2):
            count = greet((owner, 2 * y + core), count)

        def others(count):
            for y in range(2):
                count = greet((owner, 2 * y + 1 - core), count)
            return count

        return lax.cond(kh == core, others, lambda count: count, count)

    def greet_all(count):
        count = lax.fori_loop(0, 8, greet_owners, count, unroll=True)
        for device in (sibling, time_near, wide_near):
            count = greet(device, count)
        return count

    greeted = lax.cond(active, greet_all, lambda count: count, greeted)

    copy_in(0).wait()
    copy_in(1).wait()

    @pl.loop(0, HEADS)
    def _(n):
        lanes = lanes_of(n)
        k = k_in[:, lanes].astype(jnp.float32)
        inverse = lax.rsqrt(jnp.mean(k * k, axis=-1, keepdims=True) + EPSILON)
        kv_stage[n, :, 0:HD] = (k * inverse).astype(LOW)
        kv_stage[n, :, HD:] = v_in[:, lanes]

    pl.semaphore_wait(barrier, greeted)

    def send_keys():
        slot = own_t * 2 + own_w
        rows = pl.ds(pl.multiple_of(core * TILE + h * 2 * QUARTER + part // 2 * QUARTER, QUARTER), QUARTER)

        @pl.loop(0, HEADS, unroll=True)
        def _(n):
            copy_to(
                kv_stage.at[n],
                kv.at[slot, rows],
                kv_send,
                kv_recv.at[slot, core],
                worker_of(n, home_t, home_w, core),
                here,
            )

    def send_rows(held, to, send_sem, recv_sem):
        row = query_number(own_t, own_w) * TILE + part * QUARTER

        @pl.loop(0, HEADS, unroll=True)
        def _(n):
            copy_to(
                held.at[:, lanes_of(n)],
                to.at[pl.ds(pl.multiple_of(row, QUARTER), QUARTER)],
                send_sem,
                recv_sem,
                worker_of(n, home_t, home_w, h),
                here,
            )

    copy_in(2).wait()
    send_rows(q_in, q_raw, q_send, q_recv)
    send_keys()
    copy_in(3).wait()
    copy_in(4).wait()

    def send_grads():
        send_rows(g_in, grad_rows, g_send, g_recv)

    @pl.when(jnp.logical_not(active))
    def _():
        arrived(kv_stage, kv_send)
        send_grads()


    def pass_on(kind, i):
        slot = KINDS[kind][0] + i
        near_t, near_w = pair_at(kind, i)
        arrived(kv.at[slot, half(core)], kv_recv.at[slot, core])

        def send(device, to, sem):
            pltpu.make_async_remote_copy(
                src_ref=kv.at[slot, half(core)],
                dst_ref=kv.at[to, half(core)],
                send_sem=sem,
                recv_sem=kv_recv.at[to, core],
                device_id=device,
                device_id_type=MESH,
            ).start()

        if kind == 0:
            pl.when(near_w == 0)(lambda: send(wide_near, 6 + near_t, wide_send))
        if kind in (0, 2):
            to = 4 + near_w if kind == 0 else 8
            pl.when(near_t == 0)(lambda: send(time_near, to, time_send))
        send(sibling, slot, relay_send)

    def relayed(slot):
        arrived(kv.at[slot, half(1 - core)], kv_recv.at[slot, 1 - core])

    def score_step(kind, i):
        first, count, q0, qn = KINDS[kind]
        slot = first + i
        near_t, near_w = pair_at(kind, i)
        relayed(slot)
        scores = nt(q_unit[q0 * TILE : (q0 + qn) * TILE], kv[slot, :, 0:HD])
        column = lax.broadcasted_iota(jnp.int32, (1, PAIR), 1)
        lower = (column < PAIR // 4) | ((column >= PAIR // 2) & (column < 3 * PAIR // 4))
        lows = []
        for u in range(qn):
            qt, qw = QUERY_AT[q0 + u]
            dt = absolute(T, near_t) - absolute(T, qt)
            dw = absolute(W, near_w) - absolute(W, qw)
            tile = tile_of(qt, core, qw)
            live = [window_ref[tile, 9 * (dt + 1) + 3 * (kh - core + 1) + dw + 1] for kh in range(2)]
            bias = [(one.astype(jnp.float32) - 1.0) * 1e30 for one in live]
            weight = jnp.exp2(scores[u * TILE : (u + 1) * TILE] * (SCALE * LOG2E) + jnp.where(lower, bias[0], bias[1]))
            rows = slice((q0 + u) * TILE, (q0 + u + 1) * TILE)
            total = weight[:, 0:HD]
            for at in range(HD, PAIR, HD):
                total += weight[:, at : at + HD]
            acc[rows, HD:] += total
            lows.append(weight.astype(LOW))
        low = jnp.concatenate(lows, axis=0) if qn > 1 else lows[0]
        weights[kind][i] = low
        acc[q0 * TILE : (q0 + qn) * TILE, 0:HD] += jnp.dot(low, kv[slot, :, HD:], preferred_element_type=jnp.float32)

    def to_sibling(slot):
        return pltpu.make_async_remote_copy(
            src_ref=sib_send.at[slot],
            dst_ref=sib_recv.at[slot],
            send_sem=sib_sent,
            recv_sem=sib_got.at[slot],
            device_id=sibling,
            device_id_type=MESH,
        )

    def send_sum(slot):
        @pl.when(slot < 4)
        def _():
            near_t, near_w = pair_at(0, slot)
            for kh in range(2):
                for y in range(2):
                    copy_to(
                        sum_stage.at[slot, quarter(kh * 2 + y)],
                        dkv_ref.at[head],
                        sum_send,
                        dkv_recv,
                        (tile_of(near_t, kh, near_w), 2 * y + core),
                        here,
                    )

        def pass_back(device):
            pltpu.make_async_remote_copy(
                src_ref=sum_stage.at[slot],
                dst_ref=near_recv.at[slot - 4],
                send_sem=sum_send,
                recv_sem=near_got.at[slot - 4],
                device_id=device,
                device_id_type=MESH,
            ).start()

        wide = (slot == 6) | (slot == 7)
        pl.when(wide)(lambda: pass_back(wide_near))
        pl.when((slot >= 4) & jnp.logical_not(wide))(lambda: pass_back(time_near))

    def finish_sum(slot, held):
        slot = jnp.int32(slot)
        near_t, near_w = pair_at(0, slot)
        own = slot < 4
        time_at = jnp.where(own & (near_t == 0), near_w, 5)
        wide_at = jnp.where(slot == 6, 4, jnp.where(own & (near_w == 0), 2 + near_t, 5))
        to_sibling(slot).wait_recv()
        for at in (time_at, wide_at):
            pl.when(at < 5)(lambda at=at: arrived(near_recv.at[at], near_got.at[at]))
        total = part_sum[held, half(core)] + sib_recv[slot].astype(jnp.float32)
        for at in (time_at, wide_at):
            total += near_recv[at].astype(jnp.float32)
        sum_stage[slot] = total.astype(LOW)
        send_sum(slot)

    def grad_step(kind, i, held):
        first, count, q0, qn = KINDS[kind]
        slot = first + i
        rows = slice(q0 * TILE, (q0 + qn) * TILE)
        low = weights[kind][i]
        prob_grad = nt(grad_rows[rows], kv[slot, :, HD:])
        score_grad = (low.astype(jnp.float32) * (prob_grad - repeated(row_dot[rows]))).astype(LOW)
        dq_acc[rows] += jnp.dot(score_grad, kv[slot, :, 0:HD], preferred_element_type=jnp.float32)
        part_sum[held, :, 0:HD] = jnp.dot(scaled[0:HD, rows], score_grad, preferred_element_type=jnp.float32).T
        part_sum[held, :, HD:] = jnp.dot(scaled[HD:, rows], low, preferred_element_type=jnp.float32).T
        sib_send[slot] = part_sum[held, half(1 - core)].astype(LOW)
        to_sibling(slot).start()

    def send_result(u, stage, dst, send_sem, recv_sem):
        near_t, near_w = u // 2, jnp.where((u == 1) | (u == 2), 0, 1)
        for j in range(4):
            copy_to(
                stage.at[u, quarter(j)],
                dst.at[:, lanes_of(head)],
                send_sem,
                recv_sem,
                (tile_of(near_t, core, near_w), j),
                here,
            )

    @pl.when(active)
    def _():
        acc[...] = jnp.zeros_like(acc)
        dq_acc[...] = jnp.zeros_like(dq_acc)
        near_recv[5] = jnp.zeros((TILE, 2 * HD), LOW)

        pass_on(0, 0)
        pass_on(0, 1)
        pass_on(2, 0)
        send_grads()
        arrived(q_raw, q_recv)
        for u in range(4):
            rows = slice(u * TILE, (u + 1) * TILE)
            q = q_raw[rows].astype(jnp.float32)
            inverse = lax.rsqrt(jnp.mean(q * q, axis=-1, keepdims=True) + EPSILON)
            q_unit[rows] = (q * inverse).astype(LOW)

        @pl.loop(0, 4)
        def _(i):
            score_step(0, i)
            pl.when(i < 2)(lambda: pass_on(0, i + 2))
            pl.when(i >= 2)(lambda: pass_on(1, i - 2))

        score_step(2, 0)
        pass_on(2, 1)

        @pl.loop(0, 2)
        def _(i):
            score_step(1, i)

        pass_on(3, 0)
        score_step(2, 1)
        score_step(3, 0)
        arrived(grad_rows, g_recv)

        for u in range(4):
            rows = slice(u * TILE, (u + 1) * TILE)
            over[rows] = jnp.broadcast_to(1.0 / jnp.sum(acc[rows, HD:], axis=-1, keepdims=True), (TILE, HD))
            out = (acc[rows, 0:HD] * over[rows]).astype(LOW)
            o_stage[u] = out
            grad = grad_rows[rows].astype(jnp.float32)
            dot = jnp.sum(grad * out.astype(jnp.float32), axis=-1, keepdims=True)
            row_dot[rows] = jnp.broadcast_to(dot, (TILE, HD))
            scaled[0:HD, rows] = (q_unit[rows].astype(jnp.float32) * (over[rows] * SCALE)).T.astype(LOW)
            scaled[HD:, rows] = (grad * over[rows]).T.astype(LOW)

        def finish_far(at):
            kind, i = FAR[at]
            finish_sum(KINDS[kind][0] + i, 4 + at % 2)

        for at, (kind, i) in enumerate(FAR):
            grad_step(kind, i, 4 + at % 2)
            if at > 0:
                finish_far(at - 1)
                send_result(at - 1, o_stage, o_ref, o_send, o_recv)

        @pl.loop(0, 4)
        def _(step):
            grad_step(0, 3 - step, 3 - step)
            pl.when(step == 0)(lambda: finish_far(4))
            pl.when(step == 1)(lambda: finish_sum(3, 3))

        for u in range(4):
            rows = slice(u * TILE, (u + 1) * TILE)
            q = q_raw[rows].astype(jnp.float32)
            inverse = lax.rsqrt(jnp.mean(q * q, axis=-1, keepdims=True) + EPSILON)
            unit = q * inverse
            grad_in = dq_acc[rows] * (over[rows] * SCALE)
            dq = inverse * (grad_in - unit * jnp.mean(grad_in * unit, axis=-1, keepdims=True))
            dq_stage[u] = dq.astype(LOW)
            send_result(u, dq_stage, dq_ref, dq_send, dq_recv)

        for i in (2, 1, 0):
            finish_sum(i, i)

    arrived(dkv_ref, dkv_recv)
    arrived(o_ref, o_recv)
    arrived(dq_ref, dq_recv)

    pl.when(active)(lambda: arrived(kv_stage.at[pl.ds(0, HEADS - 1)], kv_send))
    for held, sem in ((q_in, q_send), (g_in, g_send)):
        kept = active & (h == core)
        pl.when(kept)(lambda: arrived(held.at[:, 0 : (HEADS - 1) * HD], sem))
        pl.when(jnp.logical_not(kept))(lambda: arrived(held, sem))

    @pl.when(active)
    def _():
        arrived(sib_send, relay_send)
        arrived(sib_send.at[pl.ds(0, 3)], time_send)
        arrived(sib_send.at[pl.ds(0, 2)], wide_send)
        arrived(sib_send, sib_sent)
        arrived(sib_send.at[pl.ds(0, SLOTS - 1)], sum_send)
        arrived(sib_send.at[0, pl.ds(0, 3 * QUARTER)], sum_send)
        for stage, sem in ((o_stage, o_send), (dq_stage, dq_send)):
            arrived(stage.at[pl.ds(0, 3)], sem)
            arrived(stage.at[3, pl.ds(0, 3 * QUARTER)], sem)
            pl.when(h != core)(lambda: arrived(stage.at[3, quarter(3)], sem))


def finish_kernel(o_in, dq_in, dkv_in, k_in, o_ref, dq_ref, dk_ref, dv_ref, o, dq, dkv, k_raw, dk, dv, in_sem, out_sem):
    parts = 3
    heads = HEADS // parts

    def lanes_in(p):
        return slice(p * heads * HD, (p + 1) * heads * HD)

    loads = [(o_in, o), (dq_in, dq)]
    for p in range(parts):
        loads.append((dkv_in.at[p * heads : (p + 1) * heads], dkv.at[p * heads : (p + 1) * heads]))
        loads.append((k_in.at[:, lanes_in(p)], k_raw.at[:, lanes_in(p)]))
    loads = [pltpu.make_async_copy(a, b, in_sem.at[i]) for i, (a, b) in enumerate(loads)]
    stores = [(o, o_ref), (dq, dq_ref)]
    for p in range(parts):
        stores.append((dk.at[:, lanes_in(p)], dk_ref.at[:, lanes_in(p)]))
        stores.append((dv.at[:, lanes_in(p)], dv_ref.at[:, lanes_in(p)]))
    stores = [pltpu.make_async_copy(a, b, out_sem.at[i]) for i, (a, b) in enumerate(stores)]
    for load in loads:
        load.start()
    for i in range(2):
        loads[i].wait()
        stores[i].start()
    for p in range(parts):
        loads[2 + 2 * p].wait()
        loads[3 + 2 * p].wait()
        for n in range(p * heads, (p + 1) * heads):
            lanes = slice(n * HD, (n + 1) * HD)
            k = k_raw[:, lanes].astype(jnp.float32)
            inverse = lax.rsqrt(jnp.mean(k * k, axis=-1, keepdims=True) + EPSILON)
            unit = k * inverse
            grad_in = dkv[n, :, 0:HD].astype(jnp.float32)
            grad = inverse * (grad_in - unit * jnp.mean(grad_in * unit, axis=-1, keepdims=True))
            dk[:, lanes] = grad.astype(LOW)
            dv[:, lanes] = dkv[n, :, HD:]
        stores[2 + 2 * p].start()
        stores[3 + 2 * p].start()
    for store in stores:
        store.wait()


def shards(queries, keys, values, out_grad, window):
    hbm = pl.BlockSpec(memory_space=pl.ANY)
    dma = pltpu.SemaphoreType.DMA
    f32 = jnp.float32
    rows = jax.ShapeDtypeStruct((QUARTER, HEADS * HD), LOW)
    o, dq, dkv = pl.pallas_call(
        attend_kernel,
        out_shape=(rows, rows, jax.ShapeDtypeStruct((HEADS, QUARTER, 2 * HD), LOW)),
        in_specs=[hbm] * 5,
        out_specs=(hbm,) * 3,
        scratch_shapes=[
            pltpu.SMEM(window.shape, window.dtype),
            pltpu.VMEM((QUARTER, HEADS * HD), LOW),
            pltpu.VMEM((QUARTER, HEADS * HD), LOW),
            pltpu.VMEM((QUARTER, HEADS * HD), LOW),
            pltpu.VMEM((QUARTER, HEADS * HD), LOW),
            pltpu.VMEM((HEADS, QUARTER, 2 * HD), LOW),
            pltpu.VMEM((SLOTS, PAIR, 2 * HD), LOW),
            pltpu.VMEM((4 * TILE, HD), LOW),
            pltpu.VMEM((4 * TILE, HD), LOW),
            pltpu.VMEM((4, 4 * TILE, PAIR), LOW),
            pltpu.VMEM((2, 2 * TILE, PAIR), LOW),
            pltpu.VMEM((2, 2 * TILE, PAIR), LOW),
            pltpu.VMEM((1, TILE, PAIR), LOW),
            pltpu.VMEM((4 * TILE, 2 * HD), f32),
            pltpu.VMEM((4 * TILE, HD), f32),
            pltpu.VMEM((4 * TILE, HD), f32),
            pltpu.VMEM((4 * TILE, HD), f32),
            pltpu.VMEM((2 * HD, 4 * TILE), LOW),
            pltpu.VMEM((4 * TILE, HD), LOW),
            pltpu.VMEM((4, TILE, HD), LOW),
            pltpu.VMEM((4, TILE, HD), LOW),
            pltpu.VMEM((6, PAIR, 2 * HD), f32),
            pltpu.VMEM((SLOTS, TILE, 2 * HD), LOW),
            pltpu.VMEM((SLOTS, TILE, 2 * HD), LOW),
            pltpu.VMEM((SLOTS, TILE, 2 * HD), LOW),
            pltpu.VMEM((6, TILE, 2 * HD), LOW),
            dma((5,)),
            pltpu.SemaphoreType.DMA,
            pltpu.SemaphoreType.DMA,
            pltpu.SemaphoreType.DMA,
            dma((SLOTS, 2)),
            pltpu.SemaphoreType.DMA,
            pltpu.SemaphoreType.DMA,
            pltpu.SemaphoreType.DMA,
            pltpu.SemaphoreType.DMA,
            pltpu.SemaphoreType.DMA,
            pltpu.SemaphoreType.DMA,
            dma((SLOTS,)),
            dma((5,)),
            pltpu.SemaphoreType.DMA,
            pltpu.SemaphoreType.DMA,
            pltpu.SemaphoreType.DMA,
            pltpu.SemaphoreType.DMA,
            pltpu.SemaphoreType.DMA,
            pltpu.SemaphoreType.DMA,
        ],
        compiler_params=pltpu.CompilerParams(collective_id=0, has_side_effects=True, vmem_limit_bytes=VMEM_LIMIT),
        name="attend",
    )(window, queries, keys, values, out_grad)

    return pl.pallas_call(
        finish_kernel,
        out_shape=(rows,) * 4,
        in_specs=[hbm] * 4,
        out_specs=(hbm,) * 4,
        scratch_shapes=[
            pltpu.VMEM((QUARTER, HEADS * HD), LOW),
            pltpu.VMEM((QUARTER, HEADS * HD), LOW),
            pltpu.VMEM((HEADS, QUARTER, 2 * HD), LOW),
            pltpu.VMEM((QUARTER, HEADS * HD), LOW),
            pltpu.VMEM((QUARTER, HEADS * HD), LOW),
            pltpu.VMEM((QUARTER, HEADS * HD), LOW),
            dma((8,)),
            dma((8,)),
        ],
        compiler_params=pltpu.CompilerParams(vmem_limit_bytes=VMEM_LIMIT),
        name="finish",
    )(o, dq, dkv, keys)


def solution(mesh):
    rows = P(("tm", "head"), None)
    return jax.shard_map(
        shards, mesh=mesh, in_specs=(rows, rows, rows, rows, P()), out_specs=(rows, rows, rows, rows), check_vma=False
    )
```

```python
import jax
import jax.numpy as jnp
from jax import lax
from jax.experimental import pallas as pl
from jax.experimental.pallas import tpu as pltpu
from jax.sharding import PartitionSpec as P

TILE = 384
HEADS = 12
HD = 128
QUARTER = 96
PAIR = 768
SLOTS = 9
EPSILON = 1e-06
SCALE = HD**-0.5
LOG2E = 1.4426950408889634
MESH = pl.DeviceIdType.MESH
VMEM_LIMIT = 60 * 1024 * 1024
LOW = jnp.bfloat16

QUERY_AT = ((0, 1), (0, 0), (1, 0), (1, 1))
KINDS = ((0, 4, 0, 4), (4, 2, 0, 2), (6, 2, 1, 2), (8, 1, 1, 1))
FAR = ((3, 0), (2, 1), (1, 1), (1, 0), (2, 0))


def worker_of(n, T, W, core):
    y = n % 4
    spot = (n // 4 + y + 1) % 4
    x, z = absolute(T, spot // 2), 2 * (spot % 2) + W
    return x * 8 + z * 2 + y // 2, (y % 2) * 2 + core


def work_here(tm, part):
    x, y, z = tm // 8, tm % 2 * 2 + part // 2, tm // 2 % 4
    T, W = x // 2, z % 2
    row = (relative(T, x) * 2 + z // 2 + 7 - y) % 4
    return row < 3, jnp.where(row < 3, row * 4 + y, 0), T, W, part % 2


def absolute(half, near):
    return 1 + half + near * (2 * half - 1)


def relative(half, index):
    return (index - 1 - half) * (2 * half - 1)


def pair_at(kind, i):
    if kind == 0:
        return i // 2, i % 2
    if kind == 1:
        return -1, i
    if kind == 2:
        return i, -1
    return -1, -1


def query_number(near_t, near_w):
    return jnp.where(near_t == 0, 1 - near_w, 2 + near_w)


def copy_to(src, dst, send_sem, recv_sem, device, here):
    same = (device[0] == here[0]) & (device[1] == here[1])

    @pl.when(same)
    def _():
        pltpu.make_async_copy(src, dst, recv_sem).start()

    @pl.when(jnp.logical_not(same))
    def _():
        pltpu.make_async_remote_copy(
            src_ref=src, dst_ref=dst, send_sem=send_sem, recv_sem=recv_sem, device_id=device, device_id_type=MESH
        ).start()


def arrived(ref, sem):
    pltpu.make_async_copy(ref, ref, sem).wait()


def nt(a, b):
    return lax.dot_general(a, b, (((1,), (1,)), ((), ())), preferred_element_type=jnp.float32)


def quarter(j):
    return pl.ds(pl.multiple_of(j * QUARTER, QUARTER), QUARTER)


def half(core):
    return pl.ds(pl.multiple_of(core * TILE, TILE), TILE)


def lanes_of(n):
    return pl.ds(pl.multiple_of(n * HD, HD), HD)


def repeated(value):
    return jnp.concatenate([value] * (PAIR // HD), axis=1)


def attend_kernel(
    window_hbm,
    q_hbm,
    k_hbm,
    v_hbm,
    g_hbm,
    o_ref,
    dq_ref,
    dkv_ref,
    window_ref,
    q_in,
    k_in,
    v_in,
    g_in,
    kv_stage,
    kv,
    q_raw,
    q_unit,
    weights0,
    weights1,
    weights2,
    weights3,
    acc,
    dq_acc,
    over,
    row_dot,
    scaled,
    grad_rows,
    o_stage,
    dq_stage,
    part_sum,
    sib_send,
    sib_recv,
    sum_stage,
    near_recv,
    in_sem,
    kv_send,
    q_send,
    g_send,
    kv_recv,
    q_recv,
    g_recv,
    relay_send,
    time_send,
    wide_send,
    sib_sent,
    sib_got,
    near_got,
    o_send,
    dq_send,
    sum_send,
    o_recv,
    dq_recv,
    dkv_recv,
):
    tm, part = lax.axis_index("tm"), lax.axis_index("head")
    here = (tm, part)
    t, h, w = tm // 8, tm // 4 % 2, tm % 4
    active, head, T, W, core = work_here(tm, part)
    home_t, home_w = t // 2, w // 2
    own_t, own_w = relative(home_t, t), relative(home_w, w)
    sibling = (tm, part + 1 - 2 * core)
    time_near = worker_of(head, 1 - T, W, core)
    wide_near = worker_of(head, T, 1 - W, core)
    weights = (weights0, weights1, weights2, weights3)

    def copy_in(i):
        source = (k_hbm, v_hbm, q_hbm, g_hbm, window_hbm)[i]
        return pltpu.make_async_copy(source, (k_in, v_in, q_in, g_in, window_ref)[i], in_sem.at[i])

    for i in range(5):
        copy_in(i).start()

    def tile_of(near_t, kh, near_w):
        return absolute(T, near_t) * 8 + kh * 4 + absolute(W, near_w)

    barrier = pltpu.get_barrier_semaphore()

    def greet(device, count):
        other = jnp.logical_not((device[0] == tm) & (device[1] == part))

        @pl.when(other)
        def _():
            pl.semaphore_signal(barrier, inc=1, device_id=device, device_id_type=MESH)

        return count + other.astype(jnp.int32)

    def greet_workers(n, count):
        count = greet(worker_of(n, home_t, home_w, core), count)
        return lax.cond(h != core, lambda c: greet(worker_of(n, home_t, home_w, h), c), lambda c: c, count)

    greeted = lax.fori_loop(0, HEADS, greet_workers, jnp.int32(0), unroll=True)

    def greet_owners(i, count):
        near_t, kh, near_w = i // 4, i % 2, i // 2 % 2
        owner = tile_of(near_t, kh, near_w)
        for y in range(2):
            count = greet((owner, 2 * y + core), count)

        def others(count):
            for y in range(2):
                count = greet((owner, 2 * y + 1 - core), count)
            return count

        return lax.cond(kh == core, others, lambda count: count, count)

    def greet_all(count):
        count = lax.fori_loop(0, 8, greet_owners, count, unroll=True)
        for device in (sibling, time_near, wide_near):
            count = greet(device, count)
        return count

    greeted = lax.cond(active, greet_all, lambda count: count, greeted)

    copy_in(0).wait()
    copy_in(1).wait()

    @pl.loop(0, HEADS)
    def _(n):
        lanes = lanes_of(n)
        k = k_in[:, lanes].astype(jnp.float32)
        inverse = lax.rsqrt(jnp.mean(k * k, axis=-1, keepdims=True) + EPSILON)
        kv_stage[n, :, 0:HD] = (k * inverse).astype(LOW)
        kv_stage[n, :, HD:] = v_in[:, lanes]

    pl.semaphore_wait(barrier, greeted)

    def send_keys():
        slot = own_t * 2 + own_w
        rows = pl.ds(pl.multiple_of(core * TILE + h * 2 * QUARTER + part // 2 * QUARTER, QUARTER), QUARTER)

        @pl.loop(0, HEADS, unroll=True)
        def _(n):
            copy_to(
                kv_stage.at[n],
                kv.at[slot, rows],
                kv_send,
                kv_recv.at[slot, core],
                worker_of(n, home_t, home_w, core),
                here,
            )

    def send_rows(held, to, send_sem, recv_sem):
        row = query_number(own_t, own_w) * TILE + part * QUARTER

        @pl.loop(0, HEADS, unroll=True)
        def _(n):
            copy_to(
                held.at[:, lanes_of(n)],
                to.at[pl.ds(pl.multiple_of(row, QUARTER), QUARTER)],
                send_sem,
                recv_sem,
                worker_of(n, home_t, home_w, h),
                here,
            )

    copy_in(2).wait()
    send_rows(q_in, q_raw, q_send, q_recv)
    send_keys()
    copy_in(3).wait()
    copy_in(4).wait()

    def send_grads():
        send_rows(g_in, grad_rows, g_send, g_recv)

    @pl.when(jnp.logical_not(active))
    def _():
        arrived(kv_stage, kv_send)
        send_grads()


    def pass_on(kind, i):
        slot = KINDS[kind][0] + i
        near_t, near_w = pair_at(kind, i)
        arrived(kv.at[slot, half(core)], kv_recv.at[slot, core])

        def send(device, to, sem):
            pltpu.make_async_remote_copy(
                src_ref=kv.at[slot, half(core)],
                dst_ref=kv.at[to, half(core)],
                send_sem=sem,
                recv_sem=kv_recv.at[to, core],
                device_id=device,
                device_id_type=MESH,
            ).start()

        if kind == 0:
            pl.when(near_w == 0)(lambda: send(wide_near, 6 + near_t, wide_send))
        if kind in (0, 2):
            to = 4 + near_w if kind == 0 else 8
            pl.when(near_t == 0)(lambda: send(time_near, to, time_send))
        send(sibling, slot, relay_send)

    def relayed(slot):
        arrived(kv.at[slot, half(1 - core)], kv_recv.at[slot, 1 - core])

    def score_step(kind, i):
        first, count, q0, qn = KINDS[kind]
        slot = first + i
        near_t, near_w = pair_at(kind, i)
        relayed(slot)
        scores = nt(q_unit[q0 * TILE : (q0 + qn) * TILE], kv[slot, :, 0:HD])
        column = lax.broadcasted_iota(jnp.int32, (1, PAIR), 1)
        lower = (column < PAIR // 4) | ((column >= PAIR // 2) & (column < 3 * PAIR // 4))
        lows = []
        for u in range(qn):
            qt, qw = QUERY_AT[q0 + u]
            dt = absolute(T, near_t) - absolute(T, qt)
            dw = absolute(W, near_w) - absolute(W, qw)
            tile = tile_of(qt, core, qw)
            live = [window_ref[tile, 9 * (dt + 1) + 3 * (kh - core + 1) + dw + 1] for kh in range(2)]
            bias = [(one.astype(jnp.float32) - 1.0) * 1e30 for one in live]
            weight = jnp.exp2(scores[u * TILE : (u + 1) * TILE] * (SCALE * LOG2E) + jnp.where(lower, bias[0], bias[1]))
            rows = slice((q0 + u) * TILE, (q0 + u + 1) * TILE)
            total = weight[:, 0:HD]
            for at in range(HD, PAIR, HD):
                total += weight[:, at : at + HD]
            acc[rows, HD:] += total
            lows.append(weight.astype(LOW))
        low = jnp.concatenate(lows, axis=0) if qn > 1 else lows[0]
        weights[kind][i] = low
        acc[q0 * TILE : (q0 + qn) * TILE, 0:HD] += jnp.dot(low, kv[slot, :, HD:], preferred_element_type=jnp.float32)

    def to_sibling(slot):
        return pltpu.make_async_remote_copy(
            src_ref=sib_send.at[slot],
            dst_ref=sib_recv.at[slot],
            send_sem=sib_sent,
            recv_sem=sib_got.at[slot],
            device_id=sibling,
            device_id_type=MESH,
        )

    def send_sum(slot):
        @pl.when(slot < 4)
        def _():
            near_t, near_w = pair_at(0, slot)
            for kh in range(2):
                for y in range(2):
                    copy_to(
                        sum_stage.at[slot, quarter(kh * 2 + y)],
                        dkv_ref.at[head],
                        sum_send,
                        dkv_recv,
                        (tile_of(near_t, kh, near_w), 2 * y + core),
                        here,
                    )

        def pass_back(device):
            pltpu.make_async_remote_copy(
                src_ref=sum_stage.at[slot],
                dst_ref=near_recv.at[slot - 4],
                send_sem=sum_send,
                recv_sem=near_got.at[slot - 4],
                device_id=device,
                device_id_type=MESH,
            ).start()

        wide = (slot == 6) | (slot == 7)
        pl.when(wide)(lambda: pass_back(wide_near))
        pl.when((slot >= 4) & jnp.logical_not(wide))(lambda: pass_back(time_near))

    def finish_sum(slot, held):
        slot = jnp.int32(slot)
        near_t, near_w = pair_at(0, slot)
        own = slot < 4
        time_at = jnp.where(own & (near_t == 0), near_w, 5)
        wide_at = jnp.where(slot == 6, 4, jnp.where(own & (near_w == 0), 2 + near_t, 5))
        to_sibling(slot).wait_recv()
        for at in (time_at, wide_at):
            pl.when(at < 5)(lambda at=at: arrived(near_recv.at[at], near_got.at[at]))
        total = part_sum[held, half(core)] + sib_recv[slot].astype(jnp.float32)
        for at in (time_at, wide_at):
            total += near_recv[at].astype(jnp.float32)
        sum_stage[slot] = total.astype(LOW)
        send_sum(slot)

    def grad_step(kind, i, held):
        first, count, q0, qn = KINDS[kind]
        slot = first + i
        rows = slice(q0 * TILE, (q0 + qn) * TILE)
        low = weights[kind][i]
        prob_grad = nt(grad_rows[rows], kv[slot, :, HD:])
        score_grad = (low.astype(jnp.float32) * (prob_grad - repeated(row_dot[rows]))).astype(LOW)
        dq_acc[rows] += jnp.dot(score_grad, kv[slot, :, 0:HD], preferred_element_type=jnp.float32)
        part_sum[held, :, 0:HD] = jnp.dot(scaled[0:HD, rows], score_grad, preferred_element_type=jnp.float32).T
        part_sum[held, :, HD:] = jnp.dot(scaled[HD:, rows], low, preferred_element_type=jnp.float32).T
        sib_send[slot] = part_sum[held, half(1 - core)].astype(LOW)
        to_sibling(slot).start()

    def send_result(u, stage, dst, send_sem, recv_sem):
        near_t, near_w = u // 2, jnp.where((u == 1) | (u == 2), 0, 1)
        for j in range(4):
            copy_to(
                stage.at[u, quarter(j)],
                dst.at[:, lanes_of(head)],
                send_sem,
                recv_sem,
                (tile_of(near_t, core, near_w), j),
                here,
            )

    @pl.when(active)
    def _():
        acc[...] = jnp.zeros_like(acc)
        dq_acc[...] = jnp.zeros_like(dq_acc)
        near_recv[5] = jnp.zeros((TILE, 2 * HD), LOW)

        pass_on(0, 0)
        pass_on(0, 1)
        pass_on(2, 0)
        send_grads()
        arrived(q_raw, q_recv)
        for u in range(4):
            rows = slice(u * TILE, (u + 1) * TILE)
            q = q_raw[rows].astype(jnp.float32)
            inverse = lax.rsqrt(jnp.mean(q * q, axis=-1, keepdims=True) + EPSILON)
            q_unit[rows] = (q * inverse).astype(LOW)

        @pl.loop(0, 4)
        def _(i):
            score_step(0, i)
            pl.when(i < 2)(lambda: pass_on(0, i + 2))
            pl.when(i >= 2)(lambda: pass_on(1, i - 2))

        score_step(2, 0)
        pass_on(2, 1)

        @pl.loop(0, 2)
        def _(i):
            score_step(1, i)

        pass_on(3, 0)
        score_step(2, 1)
        score_step(3, 0)
        arrived(grad_rows, g_recv)

        for u in range(4):
            rows = slice(u * TILE, (u + 1) * TILE)
            over[rows] = jnp.broadcast_to(1.0 / jnp.sum(acc[rows, HD:], axis=-1, keepdims=True), (TILE, HD))
            out = (acc[rows, 0:HD] * over[rows]).astype(LOW)
            o_stage[u] = out
            grad = grad_rows[rows].astype(jnp.float32)
            dot = jnp.sum(grad * out.astype(jnp.float32), axis=-1, keepdims=True)
            row_dot[rows] = jnp.broadcast_to(dot, (TILE, HD))
            scaled[0:HD, rows] = (q_unit[rows].astype(jnp.float32) * (over[rows] * SCALE)).T.astype(LOW)
            scaled[HD:, rows] = (grad * over[rows]).T.astype(LOW)

        def finish_far(at):
            kind, i = FAR[at]
            finish_sum(KINDS[kind][0] + i, 4 + at % 2)

        grad_step(0, 3, 3)
        for at, (kind, i) in enumerate(FAR):
            grad_step(kind, i, 4 + at % 2)
            if at == 0:
                finish_sum(3, 3)
            if at > 0:
                finish_far(at - 1)
                send_result(at - 1, o_stage, o_ref, o_send, o_recv)

        @pl.loop(0, 3)
        def _(step):
            grad_step(0, 2 - step, 2 - step)
            pl.when(step == 0)(lambda: finish_far(4))

        for u in range(4):
            rows = slice(u * TILE, (u + 1) * TILE)
            q = q_raw[rows].astype(jnp.float32)
            inverse = lax.rsqrt(jnp.mean(q * q, axis=-1, keepdims=True) + EPSILON)
            unit = q * inverse
            grad_in = dq_acc[rows] * (over[rows] * SCALE)
            dq = inverse * (grad_in - unit * jnp.mean(grad_in * unit, axis=-1, keepdims=True))
            dq_stage[u] = dq.astype(LOW)
            send_result(u, dq_stage, dq_ref, dq_send, dq_recv)

        for i in (2, 1, 0):
            finish_sum(i, i)

    arrived(dkv_ref, dkv_recv)
    arrived(o_ref, o_recv)
    arrived(dq_ref, dq_recv)

    pl.when(active)(lambda: arrived(kv_stage.at[pl.ds(0, HEADS - 1)], kv_send))
    for held, sem in ((q_in, q_send), (g_in, g_send)):
        kept = active & (h == core)
        pl.when(kept)(lambda: arrived(held.at[:, 0 : (HEADS - 1) * HD], sem))
        pl.when(jnp.logical_not(kept))(lambda: arrived(held, sem))

    @pl.when(active)
    def _():
        arrived(sib_send, relay_send)
        arrived(sib_send.at[pl.ds(0, 3)], time_send)
        arrived(sib_send.at[pl.ds(0, 2)], wide_send)
        arrived(sib_send, sib_sent)
        arrived(sib_send.at[pl.ds(0, SLOTS - 1)], sum_send)
        arrived(sib_send.at[0, pl.ds(0, 3 * QUARTER)], sum_send)
        for stage, sem in ((o_stage, o_send), (dq_stage, dq_send)):
            arrived(stage.at[pl.ds(0, 3)], sem)
            arrived(stage.at[3, pl.ds(0, 3 * QUARTER)], sem)
            pl.when(h != core)(lambda: arrived(stage.at[3, quarter(3)], sem))


def finish_kernel(o_in, dq_in, dkv_in, k_in, o_ref, dq_ref, dk_ref, dv_ref, o, dq, dkv, k_raw, dk, dv, in_sem, out_sem):
    parts = 3
    heads = HEADS // parts

    def lanes_in(p):
        return slice(p * heads * HD, (p + 1) * heads * HD)

    loads = [(o_in, o), (dq_in, dq)]
    for p in range(parts):
        loads.append((dkv_in.at[p * heads : (p + 1) * heads], dkv.at[p * heads : (p + 1) * heads]))
        loads.append((k_in.at[:, lanes_in(p)], k_raw.at[:, lanes_in(p)]))
    loads = [pltpu.make_async_copy(a, b, in_sem.at[i]) for i, (a, b) in enumerate(loads)]
    stores = [(o, o_ref), (dq, dq_ref)]
    for p in range(parts):
        stores.append((dk.at[:, lanes_in(p)], dk_ref.at[:, lanes_in(p)]))
        stores.append((dv.at[:, lanes_in(p)], dv_ref.at[:, lanes_in(p)]))
    stores = [pltpu.make_async_copy(a, b, out_sem.at[i]) for i, (a, b) in enumerate(stores)]
    for load in loads:
        load.start()
    for i in range(2):
        loads[i].wait()
        stores[i].start()
    for p in range(parts):
        loads[2 + 2 * p].wait()
        loads[3 + 2 * p].wait()
        for n in range(p * heads, (p + 1) * heads):
            lanes = slice(n * HD, (n + 1) * HD)
            k = k_raw[:, lanes].astype(jnp.float32)
            inverse = lax.rsqrt(jnp.mean(k * k, axis=-1, keepdims=True) + EPSILON)
            unit = k * inverse
            grad_in = dkv[n, :, 0:HD].astype(jnp.float32)
            grad = inverse * (grad_in - unit * jnp.mean(grad_in * unit, axis=-1, keepdims=True))
            dk[:, lanes] = grad.astype(LOW)
            dv[:, lanes] = dkv[n, :, HD:]
        stores[2 + 2 * p].start()
        stores[3 + 2 * p].start()
    for store in stores:
        store.wait()


def shards(queries, keys, values, out_grad, window):
    hbm = pl.BlockSpec(memory_space=pl.ANY)
    dma = pltpu.SemaphoreType.DMA
    f32 = jnp.float32
    rows = jax.ShapeDtypeStruct((QUARTER, HEADS * HD), LOW)
    o, dq, dkv = pl.pallas_call(
        attend_kernel,
        out_shape=(rows, rows, jax.ShapeDtypeStruct((HEADS, QUARTER, 2 * HD), LOW)),
        in_specs=[hbm] * 5,
        out_specs=(hbm,) * 3,
        scratch_shapes=[
            pltpu.SMEM(window.shape, window.dtype),
            pltpu.VMEM((QUARTER, HEADS * HD), LOW),
            pltpu.VMEM((QUARTER, HEADS * HD), LOW),
            pltpu.VMEM((QUARTER, HEADS * HD), LOW),
            pltpu.VMEM((QUARTER, HEADS * HD), LOW),
            pltpu.VMEM((HEADS, QUARTER, 2 * HD), LOW),
            pltpu.VMEM((SLOTS, PAIR, 2 * HD), LOW),
            pltpu.VMEM((4 * TILE, HD), LOW),
            pltpu.VMEM((4 * TILE, HD), LOW),
            pltpu.VMEM((4, 4 * TILE, PAIR), LOW),
            pltpu.VMEM((2, 2 * TILE, PAIR), LOW),
            pltpu.VMEM((2, 2 * TILE, PAIR), LOW),
            pltpu.VMEM((1, TILE, PAIR), LOW),
            pltpu.VMEM((4 * TILE, 2 * HD), f32),
            pltpu.VMEM((4 * TILE, HD), f32),
            pltpu.VMEM((4 * TILE, HD), f32),
            pltpu.VMEM((4 * TILE, HD), f32),
            pltpu.VMEM((2 * HD, 4 * TILE), LOW),
            pltpu.VMEM((4 * TILE, HD), LOW),
            pltpu.VMEM((4, TILE, HD), LOW),
            pltpu.VMEM((4, TILE, HD), LOW),
            pltpu.VMEM((6, PAIR, 2 * HD), f32),
            pltpu.VMEM((SLOTS, TILE, 2 * HD), LOW),
            pltpu.VMEM((SLOTS, TILE, 2 * HD), LOW),
            pltpu.VMEM((SLOTS, TILE, 2 * HD), LOW),
            pltpu.VMEM((6, TILE, 2 * HD), LOW),
            dma((5,)),
            pltpu.SemaphoreType.DMA,
            pltpu.SemaphoreType.DMA,
            pltpu.SemaphoreType.DMA,
            dma((SLOTS, 2)),
            pltpu.SemaphoreType.DMA,
            pltpu.SemaphoreType.DMA,
            pltpu.SemaphoreType.DMA,
            pltpu.SemaphoreType.DMA,
            pltpu.SemaphoreType.DMA,
            pltpu.SemaphoreType.DMA,
            dma((SLOTS,)),
            dma((5,)),
            pltpu.SemaphoreType.DMA,
            pltpu.SemaphoreType.DMA,
            pltpu.SemaphoreType.DMA,
            pltpu.SemaphoreType.DMA,
            pltpu.SemaphoreType.DMA,
            pltpu.SemaphoreType.DMA,
        ],
        compiler_params=pltpu.CompilerParams(collective_id=0, has_side_effects=True, vmem_limit_bytes=VMEM_LIMIT),
        name="attend",
    )(window, queries, keys, values, out_grad)

    return pl.pallas_call(
        finish_kernel,
        out_shape=(rows,) * 4,
        in_specs=[hbm] * 4,
        out_specs=(hbm,) * 4,
        scratch_shapes=[
            pltpu.VMEM((QUARTER, HEADS * HD), LOW),
            pltpu.VMEM((QUARTER, HEADS * HD), LOW),
            pltpu.VMEM((HEADS, QUARTER, 2 * HD), LOW),
            pltpu.VMEM((QUARTER, HEADS * HD), LOW),
            pltpu.VMEM((QUARTER, HEADS * HD), LOW),
            pltpu.VMEM((QUARTER, HEADS * HD), LOW),
            dma((8,)),
            dma((8,)),
        ],
        compiler_params=pltpu.CompilerParams(vmem_limit_bytes=VMEM_LIMIT),
        name="finish",
    )(o, dq, dkv, keys)


def solution(mesh):
    rows = P(("tm", "head"), None)
    return jax.shard_map(
        shards, mesh=mesh, in_specs=(rows, rows, rows, rows, P()), out_specs=(rows, rows, rows, rows), check_vma=False
    )
```
